32 devices in a mesh: clips: 8 (over y, x, core), tm: 4 (over z).
Axes of the slice: x: 2, y: 2, z: 4, core: 2. Of those that a mesh axis runs over, the one named last changes fastest.
Arguments:
- patches: bfloat16 [64, 512, 768], P('clips', 'tm'), may hold values from -6 to 6
- mask_index: int32 [64, 450], P('clips'), may hold values from 0 to 511, as said below
- mask_count: int32 [64], P('clips'), may hold values from 100 to 450, as said below
- w_qkv: bfloat16 [768, 2304], replicated, may hold values from -0.21875 to 0.21875
- q_bias: bfloat16 [768], replicated, may hold values from -3 to 3
- v_bias: bfloat16 [768], replicated, may hold values from -3 to 3
- w_out: bfloat16 [768, 768], replicated, may hold values from -0.875 to 0.875
- out_bias: bfloat16 [768], replicated, may hold values from -3 to 3
- w_up: bfloat16 [768, 3072], replicated, may hold values from -0.21875 to 0.21875
- up_bias: bfloat16 [3072], replicated, may hold values from -3 to 3
- w_down: bfloat16 [3072, 768], replicated, may hold values from -0.109375 to 0.109375
- down_bias: bfloat16 [768], replicated, may hold values from -3 to 3
- norm1_scale: bfloat16 [768], replicated, may hold values from 0.5 to 1.5
- norm1_shift: bfloat16 [768], replicated, may hold values from -3 to 3
- norm2_scale: bfloat16 [768], replicated, may hold values from 0.5 to 1.5
- norm2_shift: bfloat16 [768], replicated, may hold values from -3 to 3
- mask_embed: bfloat16 [768], replicated, may hold values from -6 to 6
- pos_embed: bfloat16 [512, 768], replicated, may hold values from -3 to 3
- cotangent: bfloat16 [64, 512, 768], P('clips', 'tm'), may hold values from -6 to 6
Outputs:
- block_out: bfloat16 [64, 512, 768], P('clips', 'tm')
- input_grad: bfloat16 [64, 512, 768], P('clips', 'tm')
- grad_w_qkv: float32 [768, 2304], replicated
- grad_q_bias: float32 [768], replicated
- grad_v_bias: float32 [768], replicated
- grad_w_out: float32 [768, 768], replicated
- grad_out_bias: float32 [768], replicated
- grad_w_up: float32 [768, 3072], replicated
- grad_up_bias: float32 [3072], replicated
- grad_w_down: float32 [3072, 768], replicated
- grad_down_bias: float32 [768], replicated
- grad_norm1_scale: float32 [768], replicated
- grad_norm1_shift: float32 [768], replicated
- grad_norm2_scale: float32 [768], replicated
- grad_norm2_shift: float32 [768], replicated
- grad_mask_embed: float32 [768], replicated
- grad_pos_embed: float32 [512, 768], replicated
The draws below stay inside these ranges and needn't reach their ends.
Inputs may be any that keep to these rules, and one draw needn't show every extreme that they name: `mask_index`: the entries of one clip's list are distinct positions of that clip; the entries after its first mask_count ones are other positions and are not masked. `mask_count`: every draw has a clip with exactly 450 and a clip with exactly 100 masked positions.
All inputs are finite; a program needn't handle non-finite values.
Results may differ from the reference program's by a relative error of at most 0.012.
Values may be sent and summed in bfloat16 or wider, within the bound.
No kernel may reach another device: no remote copies, remote signals or barrier semaphores. Data moves between devices by JAX's collectives and lax.ppermute only.
A program may use at most 256 MiB of HBM per device.

```python
import math
import jax
import jax.numpy as jnp
from jax import lax

D = 768
HEADS = 12
HD = 64
FF = 3072
LENGTH = 512
MAXM = 450
MINM = 100
CLIPS = 64


def draw_mask_index(key, part):
    clip_keys = jax.random.split(key, CLIPS)
    orders = jax.vmap(lambda subkey: jax.random.permutation(subkey, LENGTH))(clip_keys)
    return orders[:, :MAXM].astype(jnp.int32)


def draw_mask_count(key, part):
    counts = jax.random.randint(jax.random.fold_in(key, 1), (CLIPS,), MINM, MAXM + 1)
    high_clip = jax.random.randint(jax.random.fold_in(key, 2), (), 0, CLIPS)
    low_clip = (high_clip + 1 + jax.random.randint(jax.random.fold_in(key, 3), (), 0, CLIPS - 1)) % CLIPS
    counts = counts.at[high_clip].set(MAXM).at[low_clip].set(MINM)
    return counts.astype(jnp.int32)


def raised(result, stream_key, source, target, parts, factor):
    owner, partner = [(jnp.arange(result.shape[axis_at]) // (result.shape[axis_at] // parts)).reshape([-1 if axis == axis_at else 1 for axis in range(result.ndim)]) for axis_at in (source, target)]
    chosen = jax.random.permutation(stream_key, parts)[partner]
    strong = (owner == chosen) | (owner == (partner + parts // 2) % parts)
    return jnp.where(strong, factor * result, result)


def block_levels(stream_key, shape, cuts, least, top_value):
    loudness = 1.0
    for axis_at, blocks in cuts:
        heights = jax.random.uniform(jax.random.fold_in(jax.random.fold_in(stream_key, 6), axis_at), (blocks,), jnp.float32, least / len(cuts), top_value / len(cuts))
        loudness = loudness * jnp.repeat(jnp.exp(heights), shape[axis_at] // blocks).reshape((-1,) + (1,) * (len(shape) - 1 - axis_at))
    return loudness


def bell_draw(own_key, extent, scale, most, cuts=(), held_as=jnp.bfloat16):
    factor_of = block_levels(own_key, extent, cuts, -0.22, 0.18) if cuts else 1.0
    drawn = jax.random.normal(own_key, extent, jnp.float32) * scale * factor_of
    return jnp.minimum(jnp.maximum(drawn, -most), most).astype(held_as)


def noise_with(key, extent, scale, bound, shards, heavy, kind=jnp.bfloat16):
    entries = scale * jax.random.normal(key, extent, jnp.float32)
    if shards:
        entries = entries * block_levels(key, extent, shards, -0.22, 0.18)
    return jnp.clip(raised(entries, jax.random.fold_in(key, 3), *heavy), -bound, bound).astype(kind)


def setup_inputs(seed: int = 0) -> dict:
    splits = jax.random.split(jax.random.key(seed), 20)
    patches = bell_draw(splits[0], (CLIPS, LENGTH, D), 1.0, 6.0, ((0, 8), (1, 4)))
    mask_index = draw_mask_index(jax.random.fold_in(splits[19], 71), 0)
    mask_count = draw_mask_count(jax.random.fold_in(splits[19], 71), 0)
    w_qkv = bell_draw(splits[3], (D, 3 * D), D ** -0.5, 0.21875)
    q_bias = bell_draw(splits[4], (D,), 0.5, 3.0)
    v_bias = bell_draw(splits[5], (D,), 0.5, 3.0)
    w_out = bell_draw(splits[6], (D, D), (D // 16) ** -0.5, 0.875)
    out_bias = bell_draw(splits[7], (D,), 0.5, 3.0)
    w_up = bell_draw(splits[8], (D, FF), D ** -0.5, 0.21875)
    up_bias = bell_draw(splits[9], (FF,), 0.5, 3.0)
    w_down = bell_draw(splits[10], (FF, D), FF ** -0.5, 0.109375)
    down_bias = bell_draw(splits[11], (D,), 0.5, 3.0)
    norm1_scale = jnp.clip(1.0 + 0.1 * jax.random.normal(splits[12], (D,), jnp.float32), 0.5, 1.5).astype(jnp.bfloat16)
    norm1_shift = bell_draw(splits[13], (D,), 0.5, 3.0)
    norm2_scale = jnp.clip(1.0 + 0.1 * jax.random.normal(splits[14], (D,), jnp.float32), 0.5, 1.5).astype(jnp.bfloat16)
    norm2_shift = bell_draw(splits[15], (D,), 0.5, 3.0)
    mask_embed = bell_draw(splits[16], (D,), 1.0, 6.0)
    pos_embed = bell_draw(splits[17], (LENGTH, D), 1.0, 3.0)
    cotangent = noise_with(splits[18], (CLIPS, LENGTH, D), 1.0, 6.0, ((0, 8), (1, 4)), (0, 2, 8, 2.0))
    return {"patches": patches, "mask_index": mask_index, "mask_count": mask_count, "w_qkv": w_qkv, "q_bias": q_bias, "v_bias": v_bias, "w_out": w_out, "out_bias": out_bias, "w_up": w_up, "up_bias": up_bias, "w_down": w_down, "down_bias": down_bias, "norm1_scale": norm1_scale, "norm1_shift": norm1_shift, "norm2_scale": norm2_scale, "norm2_shift": norm2_shift, "mask_embed": mask_embed, "pos_embed": pos_embed, "cotangent": cotangent}


NORM_EPS = 1e-06
HIGHEST = lax.Precision.HIGHEST

@jax.custom_vjp
def low(v):
    return lax.optimization_barrier(v.astype(jnp.bfloat16)).astype(jnp.float32)

@jax.custom_vjp
def low_back(v):
    return v

def low_keep(v):
    return (low(v), None)

def low_pass(kept, grad):
    return (grad,)

def back_keep(v):
    return (v, None)

def back_low(kept, grad):
    return (low(grad),)
low.defvjp(low_keep, low_pass)
low_back.defvjp(back_keep, back_low)

def layer_norm(values, gains, shifts):
    centred = values - lax.optimization_barrier(jnp.mean(values, -1, keepdims=True))
    spread = lax.optimization_barrier(jnp.mean(centred * centred, -1, keepdims=True))
    return centred * lax.rsqrt(spread + NORM_EPS) * gains + shifts

def attend(block_items):
    queries, key_rows, value_rows = block_items
    scores = low_back(jnp.einsum('qhe,khe->hqk', queries, key_rows, precision=HIGHEST) * HD ** (-0.5))
    attn_probs = jax.nn.softmax(scores, axis=-1)
    return jnp.einsum('hqk,khe->qhe', low(attn_probs), value_rows, precision=HIGHEST)

def forward(inputs, masked, params):
    w_qkv, q_bias, v_bias, w_out, out_bias, w_up, up_bias, w_down, down_bias, norm1_scale, norm1_shift, norm2_scale, norm2_shift, mask_embed, pos_embed = params
    bundle = inputs.shape[0]
    filled = jnp.where(masked[..., None], mask_embed[None, None, :], inputs) + pos_embed[None, :, :]
    normed_one = low(layer_norm(filled, norm1_scale, norm1_shift))
    joint_proj = jnp.einsum('bld,de->ble', normed_one, w_qkv, precision=HIGHEST)
    queries = low(low_back(joint_proj[..., :D] + q_bias))
    key_rows = low(low_back(joint_proj[..., D:2 * D]))
    value_rows = low(low_back(joint_proj[..., 2 * D:] + v_bias))
    heads_shape = (bundle, LENGTH, HEADS, HD)
    attended = lax.map(jax.checkpoint(attend), (queries.reshape(heads_shape), key_rows.reshape(heads_shape), value_rows.reshape(heads_shape)))
    attended = low(low_back(attended.reshape(bundle, LENGTH, D)))
    hidden = filled + low_back(jnp.einsum('bld,de->ble', attended, w_out, precision=HIGHEST) + out_bias)
    normed_two = low(layer_norm(hidden, norm2_scale, norm2_shift))
    up_proj = low_back(jnp.einsum('bld,df->blf', normed_two, w_up, precision=HIGHEST) + up_bias)
    activated = low(jax.nn.gelu(up_proj, approximate=False))
    return hidden + jnp.einsum('blf,fd->bld', activated, w_down, precision=HIGHEST) + down_bias

def reference(patches, mask_index, mask_count, w_qkv, q_bias, v_bias, w_out, out_bias, w_up, up_bias, w_down, down_bias, norm1_scale, norm1_shift, norm2_scale, norm2_shift, mask_embed, pos_embed, cotangent):
    params = tuple((weight.astype(jnp.float32) for weight in (w_qkv, q_bias, v_bias, w_out, out_bias, w_up, up_bias, w_down, down_bias, norm1_scale, norm1_shift, norm2_scale, norm2_shift, mask_embed, pos_embed)))
    slots = jnp.arange(MAXM, dtype=jnp.int32)
    places = jnp.arange(LENGTH, dtype=jnp.int32)
    live = slots[None, :] < mask_count[:, None]
    masked = jnp.any((mask_index[:, :, None] == places[None, None, :]) & live[:, :, None], axis=1)
    bundle = math.gcd(CLIPS, max(1, 4096 // LENGTH))
    groups = CLIPS // bundle
    inputs = patches.astype(jnp.float32).reshape(groups, bundle, LENGTH, D)
    mask_rows = masked.reshape(groups, bundle, LENGTH)
    grad_rows = cotangent.astype(jnp.float32).reshape(groups, bundle, LENGTH, D)

    def step(carry, block_items):
        values, mask_block, grad_block = block_items
        outputs, pullback = jax.vjp(lambda xs, weights: forward(xs, mask_block, weights), values, params)
        input_grad, weight_grads = pullback(grad_block)
        carry = jax.tree.map(lambda acc, new: acc + new, carry, weight_grads)
        return (carry, (outputs.astype(jnp.bfloat16), input_grad.astype(jnp.bfloat16)))
    zeros = jax.tree.map(jnp.zeros_like, params)
    totals, (outputs, input_grads) = lax.scan(step, zeros, (inputs, mask_rows, grad_rows))
    block_out = outputs.reshape(CLIPS, LENGTH, D)
    input_grad = input_grads.reshape(CLIPS, LENGTH, D)
    return (block_out, input_grad, totals[0], totals[1], totals[2], totals[3], totals[4], totals[5], totals[6], totals[7], totals[8], totals[9], totals[10], totals[11], totals[12], totals[13], totals[14])
```

```python
import jax
import jax.numpy as jnp
from jax import lax
from jax.sharding import PartitionSpec as P

HEADS = 12
NORM_EPS = 1e-06
ROOT_HALF = 0.7071067811865476
ROOT_TWO_PI = 2.5066282746310002
F32 = jnp.float32
BF16 = jnp.bfloat16


def bits_of(size):
    return size.bit_length() - 1


def hop(value, axis, bit):
    size = lax.axis_size(axis)
    return lax.ppermute(value, axis, [(i, i ^ bit) for i in range(size)])


def unshuffle(blocks, axis_name):
    me = lax.axis_index(axis_name)
    blocks = list(blocks)
    for b in range(bits_of(len(blocks))):
        odd = ((me >> b) & 1) == 1
        blocks = [jnp.where(odd, blocks[i ^ (1 << b)], blocks[i]) for i in range(len(blocks))]
    return blocks


def take_clip(values, group):
    tm = lax.axis_size("tm")
    me = lax.axis_index("tm")
    out = []
    for d in range(tm):
        block = lax.dynamic_index_in_dim(values, group * tm + (me ^ d), 0, keepdims=False)
        out.append(hop(block, "tm", d) if d else block)
    return out


def give_back(parts):
    tm = lax.axis_size("tm")
    out = []
    for part in parts:
        blocks = jnp.split(part, tm, 0)
        blocks = [hop(block, "tm", d) if d else block for d, block in enumerate(blocks)]
        out.extend(unshuffle(blocks, "tm"))
    return jnp.stack(out)


def stages():
    clip_bits = [("clips", 1 << b) for b in range(bits_of(lax.axis_size("clips")))]
    time_bits = [("tm", 1 << b) for b in range(bits_of(lax.axis_size("tm")))]
    return clip_bits + time_bits


def scatter_sum(flat, order):
    for axis, bit in order:
        halves = flat.reshape((2, flat.shape[0] // 2) + flat.shape[1:])
        mine = (lax.axis_index(axis) // bit) % 2
        away = lax.dynamic_index_in_dim(halves, 1 - mine, 0, keepdims=False)
        kept = lax.dynamic_index_in_dim(halves, mine, 0, keepdims=False)
        flat = (kept.astype(F32) + hop(away, axis, bit).astype(F32)).astype(BF16)
    return flat


def gather_back(share, order):
    for axis, bit in reversed(order):
        other = hop(share, axis, bit)
        high = ((lax.axis_index(axis) // bit) % 2) == 1
        share = jnp.concatenate(
            [jnp.where(high, other, share), jnp.where(high, share, other)], 0
        )
    return share


def sum_all(flat):
    order = stages()
    first, rest = order[:1], order[1:]
    swapped = list(rest)
    if len(swapped) > 1:
        swapped[0], swapped[1] = swapped[1], swapped[0]
    half = scatter_sum(flat, first)
    cut = half.shape[0] // 2
    left = gather_back(scatter_sum(half[:cut], rest), rest)
    right = gather_back(scatter_sum(half[cut:], swapped), swapped)
    return gather_back(jnp.concatenate([left, right], 0), first)


def norm_forward(values, gains, shifts):
    centred = values - jnp.mean(values, -1, keepdims=True)
    spread = jnp.mean(centred * centred, -1, keepdims=True)
    inverse = lax.rsqrt(spread + NORM_EPS)
    unit = centred * inverse
    return (unit * gains + shifts, unit, inverse)


def norm_backward(grad_norm, unit, inverse, gains):
    scaled = grad_norm * gains
    return inverse * (
        scaled
        - jnp.mean(scaled, -1, keepdims=True)
        - unit * jnp.mean(scaled * unit, -1, keepdims=True)
    )


def dot(a, b):
    return jnp.dot(a, b, preferred_element_type=F32)


def dot_nt(a, b):
    return lax.dot_general(a, b, (((1,), (1,)), ((), ())), preferred_element_type=F32)


def dot_tn(a, b):
    return lax.dot_general(a, b, (((0,), (0,)), ((), ())), preferred_element_type=F32)


def heads_of(values):
    return values.reshape(values.shape[0], HEADS, values.shape[1] // HEADS)


def attend(queries, keys, values):
    scale = (queries.shape[1] // HEADS) ** (-0.5)
    scores = jnp.einsum("qhe,khe->hqk", heads_of(queries), heads_of(keys), preferred_element_type=F32) * scale
    peak = jnp.max(scores, -1, keepdims=True)
    raised = jnp.exp(scores - peak)
    total = jnp.sum(raised, -1, keepdims=True)
    probs = (raised / total).astype(BF16)
    mixed = jnp.einsum("hqk,khe->qhe", probs, heads_of(values), preferred_element_type=F32)
    return mixed.reshape(queries.shape).astype(BF16), peak + jnp.log(total)


def attend_back(queries, keys, values, grad_mix, log_sum):
    scale = (queries.shape[1] // HEADS) ** (-0.5)
    q, k, v, g = map(heads_of, (queries, keys, values, grad_mix))
    scores = jnp.einsum("qhe,khe->hqk", q, k, preferred_element_type=F32) * scale
    probs = jnp.exp(scores - log_sum)
    grad_probs = jnp.einsum("qhe,khe->hqk", g, v, preferred_element_type=F32)
    delta = jnp.sum(probs * grad_probs, -1, keepdims=True)
    grad_scores = (probs * (grad_probs - delta)).astype(BF16)
    grad_q = jnp.einsum("hqk,khe->qhe", grad_scores, k, preferred_element_type=F32) * scale
    grad_k = jnp.einsum("hqk,qhe->khe", grad_scores, q, preferred_element_type=F32) * scale
    grad_v = jnp.einsum("hqk,qhe->khe", probs.astype(BF16), g, preferred_element_type=F32)
    return tuple(x.reshape(queries.shape).astype(BF16) for x in (grad_q, grad_k, grad_v))


def on_device(
    patches, mask_index, mask_count, w_qkv, q_bias, v_bias, w_out, out_bias, w_up, up_bias,
    w_down, down_bias, norm1_scale, norm1_shift, norm2_scale, norm2_shift, mask_embed, pos_embed,
    cotangent,
):
    clip_count, seg, width = patches.shape
    ff = w_up.shape[1]
    tm = lax.axis_size("tm")
    me = lax.axis_index("tm")
    length = seg * tm
    groups = clip_count // tm
    q_bias, v_bias, out_bias, up_bias, down_bias = (
        x.astype(F32) for x in (q_bias, v_bias, out_bias, up_bias, down_bias)
    )
    gain1, shift1, gain2, shift2, embed = (
        x.astype(F32) for x in (norm1_scale, norm1_shift, norm2_scale, norm2_shift, mask_embed)
    )

    starts = (me ^ jnp.arange(tm, dtype=jnp.int32)) * seg
    places = (starts[:, None] + jnp.arange(seg, dtype=jnp.int32)[None, :]).reshape(length)
    pos = jnp.concatenate(
        [lax.dynamic_slice_in_dim(pos_embed, (me ^ d) * seg, seg, 0) for d in range(tm)], 0
    ).astype(F32)
    slots = jnp.arange(mask_index.shape[1], dtype=jnp.int32)

    parts = [take_clip(patches, g) for g in range(groups)]
    cots = [take_clip(cotangent, g) for g in range(groups)]

    saved = []
    for g in range(groups):
        index_row = lax.dynamic_index_in_dim(mask_index, g * tm + me, 0, keepdims=False)
        count = lax.dynamic_index_in_dim(mask_count, g * tm + me, 0, keepdims=False)
        live = slots < count
        masked = jnp.any((places[:, None] == index_row[None, :]) & live[None, :], axis=1)[:, None]
        filled = jnp.where(masked, embed[None, :], jnp.concatenate(parts[g], 0).astype(F32)) + pos
        normed_one, unit_one, inverse_one = norm_forward(filled, gain1, shift1)
        normed_one = normed_one.astype(BF16)
        joint = dot(normed_one, w_qkv)
        queries = (joint[:, :width] + q_bias).astype(BF16)
        keys = joint[:, width : 2 * width].astype(BF16)
        values = (joint[:, 2 * width :] + v_bias).astype(BF16)
        attended, log_sum = attend(queries, keys, values)
        hidden = filled + dot(attended, w_out) + out_bias
        normed_two, unit_two, inverse_two = norm_forward(hidden, gain2, shift2)
        normed_two = normed_two.astype(BF16)
        up_proj = dot(normed_two, w_up) + up_bias
        cumulative = 0.5 * (1.0 + lax.erf(up_proj * ROOT_HALF))
        activated = (up_proj * cumulative).astype(BF16)
        slope = cumulative + up_proj * jnp.exp(-0.5 * up_proj * up_proj) / ROOT_TWO_PI
        block_out = (hidden + dot(activated, w_down) + down_bias).astype(BF16)
        saved.append((masked, normed_one, unit_one, inverse_one, queries, keys, values, attended,
                      log_sum, normed_two, unit_two, inverse_two, activated, slope, block_out))
    (masked, normed_one, unit_one, inverse_one, queries, keys, values, attended, log_sum,
     normed_two, unit_two, inverse_two, activated, slope, block_out) = zip(*saved)
    block_out = give_back(block_out)

    cot = jnp.concatenate([jnp.concatenate(c, 0) for c in cots], 0)
    rows = lambda xs: jnp.concatenate(xs, 0)
    masked, normed_one, unit_one, inverse_one, attended, normed_two, unit_two, inverse_two, activated, slope = map(
        rows, (masked, normed_one, unit_one, inverse_one, attended, normed_two, unit_two, inverse_two, activated, slope))
    top = cot.astype(F32)
    grad_down = dot_tn(activated, cot).astype(BF16)
    grad_up_in = (dot_nt(cot, w_down) * slope).astype(BF16)
    grad_up = dot_tn(normed_two, grad_up_in).astype(BF16)
    flat_one = jnp.concatenate([grad_down] + jnp.split(grad_up, ff // width, 1), 0)
    sum_one = sum_all(flat_one)

    grad_norm_two = dot_nt(grad_up_in, w_up)
    grad_hidden = top + norm_backward(grad_norm_two, unit_two, inverse_two, gain2)
    branch = grad_hidden.astype(BF16)
    grad_out = dot_tn(attended, branch).astype(BF16)
    mix = dot_nt(branch, w_out).astype(BF16)
    back = [
        attend_back(queries[g], keys[g], values[g], mix[g * length : (g + 1) * length], log_sum[g])
        for g in range(groups)
    ]
    grad_joint = jnp.concatenate([jnp.concatenate(b, 1) for b in back], 0)
    grad_qkv = dot_tn(normed_one, grad_joint).astype(BF16)
    grad_norm_one = dot_nt(grad_joint, w_qkv)
    grad_filled = grad_hidden + norm_backward(grad_norm_one, unit_one, inverse_one, gain1)
    input_grad = jnp.where(masked, 0.0, grad_filled).astype(BF16)
    input_grad = give_back(jnp.split(input_grad, groups, 0))

    joint_sums = jnp.sum(grad_joint.astype(F32), 0)
    pos_sum = jnp.sum(grad_filled.reshape(groups, length, width), 0)
    pos_sum = jnp.concatenate(unshuffle(jnp.split(pos_sum, tm, 0), "tm"), 0)
    small = [
        joint_sums[:width],
        joint_sums[2 * width :],
        jnp.sum(branch.astype(F32), 0),
        jnp.sum(grad_up_in.astype(F32), 0),
        jnp.sum(top, 0),
        jnp.sum(grad_norm_one * unit_one, 0),
        jnp.sum(grad_norm_one, 0),
        jnp.sum(grad_norm_two * unit_two, 0),
        jnp.sum(grad_norm_two, 0),
        jnp.sum(jnp.where(masked, grad_filled, 0.0), 0),
    ]
    small = jnp.concatenate([x.reshape(-1, width) for x in small], 0)
    used = 4 * width + length + small.shape[0]
    devices = tm * lax.axis_size("clips")
    step = 8 * devices
    spare = -used % step
    flat_two = jnp.concatenate(
        [
            grad_out,
            *jnp.split(grad_qkv, 3, 1),
            pos_sum.astype(BF16),
            small.astype(BF16),
            jnp.zeros((spare, width), BF16),
        ],
        0,
    )
    sum_two = sum_all(flat_two).astype(F32)
    sum_one = sum_one.astype(F32)
    w_down_sum = sum_one[:ff]
    w_up_sum = jnp.concatenate(jnp.split(sum_one[ff:], ff // width, 0), 1)
    w_out_sum = sum_two[:width]
    w_qkv_sum = jnp.concatenate(jnp.split(sum_two[width : 4 * width], 3, 0), 1)
    at = 4 * width
    pos_total = sum_two[at : at + length]
    at += length
    vectors = []
    for n in (1, 1, 1, ff // width, 1, 1, 1, 1, 1, 1):
        vectors.append(sum_two[at : at + n].reshape(-1))
        at += n
    v = vectors
    return (block_out, input_grad, w_qkv_sum, v[0], v[1], w_out_sum, v[2], w_up_sum, v[3], w_down_sum, v[4],
            v[5], v[6], v[7], v[8], v[9], pos_total)


def solution(mesh):
    rows = P("clips", "tm", None)
    in_specs = (rows, P("clips", None), P("clips")) + (P(),) * 15 + (rows,)
    out_specs = (rows, rows) + (P(),) * 15
    return jax.shard_map(on_device, mesh=mesh, in_specs=in_specs, out_specs=out_specs, check_vma=False)
```

```python
import functools

import jax
import jax.numpy as jnp
from jax import lax
from jax.experimental import pallas as pl
from jax.experimental.pallas import tpu as pltpu
from jax.sharding import PartitionSpec as P

HEADS = 12
LANES = 128
NORM_EPS = 1e-06
ROOT_HALF = 0.7071067811865476
ROOT_TWO_PI = 2.5066282746310002
LOG2_E = 1.4426950408889634
F32 = jnp.float32
BF16 = jnp.bfloat16


def bits_of(size):
    return size.bit_length() - 1


def hop(value, axis, bit):
    size = lax.axis_size(axis)
    return lax.ppermute(value, axis, [(i, i ^ bit) for i in range(size)])


def tie(*values):
    return lax.optimization_barrier(values)


def take_clips(values):
    tm = lax.axis_size("tm")
    me = lax.axis_index("tm")
    out = []
    for d in range(tm):
        block = lax.dynamic_index_in_dim(values, me ^ d, 1, keepdims=False)
        out.append(hop(block, "tm", d) if d else block)
    return jnp.concatenate(out, 1)


def give_clips(values):
    tm = lax.axis_size("tm")
    blocks = jnp.split(values, tm, 1)
    blocks = [hop(block, "tm", d) if d else block for d, block in enumerate(blocks)]
    return jnp.stack(unshuffle(blocks), 1)


def unshuffle(blocks):
    me = lax.axis_index("tm")
    blocks = list(blocks)
    for b in range(bits_of(len(blocks))):
        odd = ((me >> b) & 1) == 1
        blocks = [jnp.where(odd, blocks[i ^ (1 << b)], blocks[i]) for i in range(len(blocks))]
    return blocks


def axis_bits(axis):
    return [(axis, 1 << b) for b in range(bits_of(lax.axis_size(axis)))]


def own_bit(axis, bit):
    return (lax.axis_index(axis) // bit) % 2


def add_low(a, b):
    return (a.astype(F32) + b.astype(F32)).astype(BF16)


def halve(value, names, name):
    at = names.index(name)
    mine = own_bit(*name)
    away = lax.dynamic_index_in_dim(value, 1 - mine, at, keepdims=False)
    kept = lax.dynamic_index_in_dim(value, mine, at, keepdims=False)
    return add_low(kept, hop(away, *name)), names[:at] + names[at + 1 :]


def scatter_rounds(merge):
    clip_bits, time_bits = axis_bits("clips")[1:], axis_bits("tm")
    names = clip_bits[::-1] + time_bits[::-1]
    swapped = clip_bits[1:] + clip_bits[:1]

    def sides(index):
        def step(state):
            out = []
            for side, order in zip(state, (clip_bits, swapped)):
                now = [n for n in names if n not in order[:index]]
                out.append(halve(side, now, order[index])[0])
            return (merge(*out),) if index == len(clip_bits) - 1 else tuple(out)

        return step

    def last(index):
        def step(state):
            return (halve(state[0], time_bits[index:][::-1], time_bits[index])[0],)

        return step

    return [sides(i) for i in range(len(clip_bits))] + [last(i) for i in range(len(time_bits))]


def split_share(value):
    count = bits_of(lax.axis_size("clips")) + bits_of(lax.axis_size("tm")) - 1
    rows = value.shape[0] + -value.shape[0] % (1 << count)
    value = jnp.pad(value, ((0, rows - value.shape[0]), (0, 0)))
    return value.reshape((2,) * count + (rows >> count, value.shape[1]))


def fold(value, width):
    return jnp.concatenate(jnp.split(value, value.shape[-1] // width, -1), -2)


def gather(share):
    return lax.all_gather(share, ("clips", "tm"), axis=0, tiled=False)


def by_core(whole):
    whole = whole.reshape((-1, 2, lax.axis_size("tm")) + whole.shape[1:])
    return jnp.swapaxes(whole, 0, 1)


def unfold(whole, parts):
    others, tm, rows, width = whole.shape
    whole = whole.reshape(others, tm, parts, rows // parts, width)
    return jnp.swapaxes(whole, 2, 3).reshape(others * tm * rows // parts, parts * width)


def place_kernel(in_ref, *out_refs):
    share = in_ref[0].astype(F32)
    width = share.shape[1]
    at = 0
    for out_ref in out_refs:
        rows, columns = out_ref.shape
        for part in range(columns // width):
            out_ref[:, part * width : (part + 1) * width] = share[at : at + rows]
            at += rows


def place(whole, blocks):
    devices, rows, width = whole.shape
    tm = lax.axis_size("tm")
    half = devices // 2

    def spot(d):
        return (d // (2 * tm)) * tm + d % tm, (d // tm) % 2

    def by_row(d):
        other, core = spot(d)
        return core * half + other, 0

    return pl.pallas_call(
        place_kernel,
        grid=(devices,),
        in_specs=[pl.BlockSpec((1, rows, width), lambda d: (d, 0, 0))],
        out_specs=[pl.BlockSpec((n, p * width), spot if column else by_row) for n, p, column in blocks],
        out_shape=[
            jax.ShapeDtypeStruct((n * half, 2 * p * width) if column else (n * devices, p * width), F32)
            for n, p, column in blocks
        ],
        cost_estimate=pl.CostEstimate(flops=0, bytes_accessed=6 * devices * rows * width, transcendentals=0),
    )(whole)


def contract(a, b, da, db):
    return lax.dot_general(a, b, (((da,), (db,)), ((), ())), preferred_element_type=F32)


def own_lanes(value, i, head):
    lane = lax.broadcasted_iota(jnp.int32, value.shape, 1)
    return jnp.where((lane >= i * head) & (lane < (i + 1) * head), value, jnp.zeros_like(value))


def attend_kernel(q_ref, k_ref, v_ref, o_ref, log_ref, *, head):
    q, k, v = q_ref[...], k_ref[...], v_ref[...]
    factor = head**-0.5 * LOG2_E
    outs = []
    for i in range(q.shape[1] // head):
        scores = contract(k, own_lanes(q, i, head), 1, 1)
        peak = jnp.max(scores, 0, keepdims=True)
        raised = jnp.exp2((scores - peak) * factor)
        total = jnp.sum(raised, 0, keepdims=True)
        mixed = contract(v, raised.astype(BF16), 0, 0)
        outs.append(mixed[i * head : (i + 1) * head] * (1.0 / total))
        log_ref[0, i : i + 1, :] = peak * factor + jnp.log2(total)
    o_ref[...] = jnp.concatenate(outs, 0).T.astype(BF16)


def attend_back_kernel(q_ref, k_ref, v_ref, g_ref, log_ref, dq_ref, dk_ref, dv_ref, *, head):
    q, k, v, g = q_ref[...], k_ref[...], v_ref[...], g_ref[...]
    scale = head**-0.5
    grad_q, grad_k, grad_v = [], 0.0, 0.0
    for i in range(q.shape[1] // head):
        q_own, g_own = own_lanes(q, i, head), own_lanes(g, i, head)
        scores = contract(k, q_own, 1, 1)
        probs = jnp.exp2(scores * (scale * LOG2_E) - log_ref[0, i : i + 1, :])
        grad_probs = contract(v, g_own, 1, 1)
        delta = jnp.sum(probs * grad_probs, 0, keepdims=True)
        grad_scores = (probs * (grad_probs - delta)).astype(BF16)
        grad_q.append(contract(k, grad_scores, 0, 0)[i * head : (i + 1) * head])
        grad_k = grad_k + contract(grad_scores, q_own, 1, 0)
        grad_v = grad_v + contract(probs.astype(BF16), g_own, 1, 0)
    dq_ref[...] = (jnp.concatenate(grad_q, 0) * scale).T.astype(BF16)
    dk_ref[...] = (grad_k * scale).astype(BF16)
    dv_ref[...] = grad_v.astype(BF16)


def attend(joint, width):
    rows = joint.shape[0]
    head = width // HEADS
    pairs, per = width // LANES, LANES // head
    block = lambda off: pl.BlockSpec((rows, LANES), lambda h: (0, h + off))
    return pl.pallas_call(
        functools.partial(attend_kernel, head=head),
        grid=(pairs,),
        in_specs=[block(0), block(pairs), block(2 * pairs)],
        out_specs=[block(0), pl.BlockSpec((1, per, rows), lambda h: (h, 0, 0))],
        out_shape=[
            jax.ShapeDtypeStruct((rows, width), BF16),
            jax.ShapeDtypeStruct((pairs, per, rows), F32),
        ],
        cost_estimate=pl.CostEstimate(
            flops=16 * rows * rows * width, bytes_accessed=8 * rows * width, transcendentals=rows * rows * HEADS
        ),
        compiler_params=pltpu.CompilerParams(vmem_limit_bytes=32 * 2**20),
    )(joint, joint, joint)


def attend_back(joint, mix, log_sum):
    rows, width = mix.shape
    head = width // HEADS
    pairs, per = width // LANES, LANES // head
    block = lambda off: pl.BlockSpec((rows, LANES), lambda h: (0, h + off))
    return pl.pallas_call(
        functools.partial(attend_back_kernel, head=head),
        grid=(pairs,),
        in_specs=[
            block(0),
            block(pairs),
            block(2 * pairs),
            block(0),
            pl.BlockSpec((1, per, rows), lambda h: (h, 0, 0)),
        ],
        out_specs=[block(0)] * 3,
        out_shape=[jax.ShapeDtypeStruct((rows, width), BF16)] * 3,
        cost_estimate=pl.CostEstimate(
            flops=40 * rows * rows * width, bytes_accessed=16 * rows * width, transcendentals=rows * rows * HEADS
        ),
        compiler_params=pltpu.CompilerParams(vmem_limit_bytes=32 * 2**20),
    )(joint, joint, joint, mix, log_sum)


def norm_parts(values):
    centred = values - jnp.mean(values, -1, keepdims=True)
    spread = jnp.mean(centred * centred, -1, keepdims=True)
    inverse = lax.rsqrt(spread + NORM_EPS)
    return centred * inverse, inverse


def norm_backward(grad_norm, unit, inverse, gains):
    scaled = grad_norm * gains
    return inverse * (
        scaled
        - jnp.mean(scaled, -1, keepdims=True)
        - unit * jnp.mean(scaled * unit, -1, keepdims=True)
    )


def dot(a, b):
    return jnp.dot(a, b, preferred_element_type=F32)


def dot_nt(a, b):
    return contract(a, b, 1, 1)


def dot_tn(a, b):
    return contract(a, b, 0, 0)


def on_device(
    patches, mask_index, mask_count, w_qkv, q_bias, v_bias, w_out, out_bias, w_up, up_bias,
    w_down, down_bias, norm1_scale, norm1_shift, norm2_scale, norm2_shift, mask_embed, pos_embed,
    cotangent,
):
    clip_count, seg, width = patches.shape
    ff = w_up.shape[1]
    tm = lax.axis_size("tm")
    me = lax.axis_index("tm")
    devices = tm * lax.axis_size("clips")
    length = seg * tm
    groups = clip_count // tm
    joint_bias = jnp.concatenate([q_bias, jnp.zeros_like(q_bias), v_bias]).astype(F32)
    out_bias, up_bias, down_bias = (x.astype(F32) for x in (out_bias, up_bias, down_bias))
    gain1, shift1, gain2, shift2, embed = (
        x.astype(F32) for x in (norm1_scale, norm1_shift, norm2_scale, norm2_shift, mask_embed)
    )

    by_group = (groups, tm, seg, width)
    arrived = [take_clips(patches.reshape(by_group)[g : g + 1])[0] for g in range(groups)]
    cot = take_clips(cotangent.reshape(by_group))

    starts = (me ^ jnp.arange(tm, dtype=jnp.int32)) * seg
    places = (starts[:, None] + jnp.arange(seg, dtype=jnp.int32)[None, :]).reshape(length)
    pos = jnp.concatenate(
        [lax.dynamic_slice_in_dim(pos_embed, (me ^ d) * seg, seg, 0) for d in range(tm)], 0
    ).astype(F32)
    slots = jnp.arange(mask_index.shape[1], dtype=jnp.int32)

    saved = []
    for g in range(groups):
        index_row = lax.dynamic_index_in_dim(mask_index, g * tm + me, 0, keepdims=False)
        count = lax.dynamic_index_in_dim(mask_count, g * tm + me, 0, keepdims=False)
        live = slots < count
        masked = jnp.any((places[:, None] == index_row[None, :]) & live[None, :], axis=1)[:, None]
        filled = jnp.where(masked, embed[None, :], arrived[g].astype(F32)) + pos
        unit_one, inverse_one = norm_parts(filled)
        normed_one = (unit_one * gain1 + shift1).astype(BF16)
        joint = (dot(normed_one, w_qkv) + joint_bias).astype(BF16)
        attended, log_sum = attend(joint, width)
        hidden = filled + dot(attended, w_out) + out_bias
        unit_two, inverse_two = norm_parts(hidden)
        normed_two = (unit_two * gain2 + shift2).astype(BF16)
        saved.append((masked, unit_one, inverse_one, normed_one, joint, attended, log_sum, hidden,
                      unit_two, inverse_two, normed_two))
    masked, unit_one, inverse_one, normed_one, joint, attended, log_sum, hidden, unit_two, inverse_two, normed_two = (
        zip(*saved)
    )
    rows = lambda xs: jnp.concatenate(xs, 0)
    masked, unit_one, inverse_one, normed_one, attended, hidden, unit_two, inverse_two, normed_two = map(
        rows, (masked, unit_one, inverse_one, normed_one, attended, hidden, unit_two, inverse_two, normed_two)
    )
    cot = cot.reshape(groups * length, width)
    up_proj = dot(normed_two, w_up) + up_bias
    cumulative = 0.5 * (1.0 + lax.erf(up_proj * ROOT_HALF))
    activated = (up_proj * cumulative).astype(BF16)
    slope = cumulative + up_proj * jnp.exp(-0.5 * up_proj * up_proj) / ROOT_TWO_PI
    grad_up_in = (dot_nt(cot, w_down) * slope).astype(BF16)
    core = own_bit("clips", 1)

    def half(values, side):
        return lax.dynamic_slice_in_dim(values, side * (values.shape[1] // 2), values.shape[1] // 2, 1)

    down_got = hop(dot_tn(half(activated, 1 - core), cot).astype(BF16), "clips", 1)
    up_got = hop(dot_tn(normed_two, half(grad_up_in, 1 - core)).astype(BF16), "clips", 1)
    down = (dot_tn(half(activated, core), cot) + down_got.astype(F32)).astype(BF16)
    up = (dot_tn(normed_two, half(grad_up_in, core)) + up_got.astype(F32)).astype(BF16)
    rounds = iter(
        scatter_rounds(lambda a, b: jnp.concatenate([a, fold(b, width)], -2))
    )
    state = next(rounds)((split_share(down), split_share(up)))

    block_out = (hidden + dot(activated, w_down) + down_bias).astype(BF16)
    top = cot.astype(F32)
    grad_norm_two = dot_nt(grad_up_in, w_up)
    grad_hidden = top + norm_backward(grad_norm_two, unit_two, inverse_two, gain2)
    branch = grad_hidden.astype(BF16)
    grad_out = dot_tn(attended, branch).astype(BF16)
    mix = dot_nt(branch, w_out).astype(BF16)
    mix, block_out = tie(mix, block_out)
    block_out = give_clips(block_out.reshape(groups, length, width)).reshape(patches.shape)

    back = []
    for g in range(groups):
        back.append(attend_back(joint[g], mix[g * length : (g + 1) * length], log_sum[g]))
        if g < groups - 1:
            mix, *state = tie(mix, *state)
            state = next(rounds)(state)
    grad_joint = jnp.concatenate([jnp.concatenate(b, 1) for b in back], 0)
    grad_joint, block_out, *state = tie(grad_joint, block_out, *state)
    state = next(rounds)(state)

    qkv_got = hop(dot_tn(half(normed_one, 1 - core), grad_joint).astype(BF16), "clips", 1)
    qkv = (dot_tn(half(normed_one, core), grad_joint) + qkv_got.astype(F32)).astype(BF16)
    grad_norm_one = dot_nt(grad_joint, w_qkv)
    grad_norm_one, qkv, *state = tie(grad_norm_one, qkv, *state)
    for step in rounds:
        state = step(state)
    grad_filled = grad_hidden + norm_backward(grad_norm_one, unit_one, inverse_one, gain1)
    input_grad = jnp.where(masked, 0.0, grad_filled).astype(BF16)

    joint_sums = jnp.sum(grad_joint.astype(F32), 0)
    pos_sum = jnp.sum(grad_filled.reshape(groups, length, width), 0)
    pos_sum = jnp.concatenate(unshuffle(jnp.split(pos_sum.astype(BF16), tm, 0)), 0)
    small = [
        joint_sums[:width],
        joint_sums[2 * width :],
        jnp.sum(branch.astype(F32), 0),
        jnp.sum(grad_up_in.astype(F32), 0),
        jnp.sum(top, 0),
        jnp.sum(grad_norm_one * unit_one, 0),
        jnp.sum(grad_norm_one, 0),
        jnp.sum(grad_norm_two * unit_two, 0),
        jnp.sum(grad_norm_two, 0),
        jnp.sum(jnp.where(masked, grad_filled, 0.0), 0),
    ]
    small = jnp.concatenate([x.reshape(-1, width) for x in small], 0).astype(BF16)
    small = jnp.pad(small, ((0, width - length - small.shape[0]), (0, 0)))
    rest = jnp.concatenate([pos_sum, small], 0)
    rest_got = hop(jnp.where(core == 1, grad_out, rest), "clips", 1)
    rest = add_low(jnp.where(core == 1, rest, grad_out), rest_got)
    input_grad, rest, qkv, *state = tie(input_grad, rest, qkv, *state)
    whole_one = gather(state[0])
    input_grad = give_clips(input_grad.reshape(groups, length, width)).reshape(patches.shape)
    state = (split_share(qkv), split_share(rest))
    for step in scatter_rounds(lambda a, b: jnp.concatenate([fold(a, width), b], -2)):
        state = step(state)
    share_two, whole_one = tie(state[0], whole_one)
    whole_two = gather(share_two)

    rows_one, rows_two = ff // devices, width // devices
    up_rows = width // (devices // 2)
    if rows_two % 8 == 0:
        w_down_sum, w_up_sum = place(whole_one, ((rows_one, 1, False), (up_rows, ff // (2 * width), True)))
        w_qkv_sum, rest = place(whole_two, ((rows_two, 3, False), (up_rows, 1, False)))
    else:
        whole_one, whole_two = by_core(whole_one), by_core(whole_two)
        w_down_sum = whole_one[..., :rows_one, :].reshape(ff, width).astype(F32)
        w_up_sum = jnp.concatenate([unfold(x[..., rows_one:, :], ff // (2 * width)) for x in whole_one], 1)
        w_up_sum = w_up_sum.astype(F32)
        w_qkv_sum = jnp.concatenate([unfold(x[..., : 3 * rows_two, :], 3) for x in whole_two], 0).astype(F32)
        rest = whole_two[..., 3 * rows_two :, :].reshape(2 * width, width).astype(F32)
    w_out_sum, rest = rest[:width], rest[width:]
    pos_total = rest[:length]
    v = []
    at = length
    for n in (1, 1, 1, ff // width, 1, 1, 1, 1, 1, 1):
        v.append(rest[at : at + n].reshape(-1))
        at += n
    return (block_out, input_grad, w_qkv_sum, v[0], v[1], w_out_sum, v[2], w_up_sum, v[3], w_down_sum, v[4],
            v[5], v[6], v[7], v[8], v[9], pos_total)


def solution(mesh):
    rows = P("clips", "tm", None)
    in_specs = (rows, P("clips", None), P("clips")) + (P(),) * 15 + (rows,)
    out_specs = (rows, rows) + (P(),) * 15
    return jax.shard_map(on_device, mesh=mesh, in_specs=in_specs, out_specs=out_specs, check_vma=False)
```

```python
import functools

import jax
import jax.numpy as jnp
from jax import lax
from jax.experimental import pallas as pl
from jax.experimental.pallas import tpu as pltpu
from jax.sharding import PartitionSpec as P

HEADS = 12
LANES = 128
NORM_EPS = 1e-06
ROOT_HALF = 0.7071067811865476
ROOT_TWO_PI = 2.5066282746310002
LOG2_E = 1.4426950408889634
F32 = jnp.float32
BF16 = jnp.bfloat16
VMEM_LIMIT = 60 * 2**20


def contract(a, b, da, db):
    return lax.dot_general(a, b, (((da,), (db,)), ((), ())), preferred_element_type=F32)


def call(kernel, *, grid, in_specs, out_specs, out_shape, scratch=(), prefetch=0, flops=0, moved=0, exps=0, share=1):
    return pl.pallas_call(
        kernel,
        grid_spec=pltpu.PrefetchScalarGridSpec(
            num_scalar_prefetch=prefetch,
            grid=grid,
            in_specs=in_specs,
            out_specs=out_specs,
            scratch_shapes=scratch,
        ),
        out_shape=out_shape,
        cost_estimate=pl.CostEstimate(
            flops=int(flops) // share, bytes_accessed=int(moved) // share, transcendentals=int(exps) // share
        ),
        compiler_params=pltpu.CompilerParams(vmem_limit_bytes=VMEM_LIMIT),
    )


def fixed(shape):
    return pl.BlockSpec(shape, lambda *_: (0,) * len(shape), pipeline_mode=pl.Buffered(1))


def shaped(shape, dtype):
    return jax.ShapeDtypeStruct(shape, dtype)


def norm_parts(values):
    centred = values - jnp.mean(values, -1, keepdims=True)
    spread = jnp.mean(centred * centred, -1, keepdims=True)
    inverse = lax.rsqrt(spread + NORM_EPS)
    return centred * inverse, inverse


def norm_backward(grad_norm, unit, inverse, gains):
    scaled = grad_norm * gains
    return inverse * (
        scaled
        - jnp.mean(scaled, -1, keepdims=True)
        - unit * jnp.mean(scaled * unit, -1, keepdims=True)
    )


def project_kernel(*refs, tm):
    blocks = refs[:tm]
    mask_ref, embed_ref, pos_ref, gain_ref, shift_ref, w_ref, bias_ref, filled_ref, turned_ref, joint_ref, normed_s = refs[tm:]

    @pl.when(pl.program_id(0) == 0)
    def _():
        seg = blocks[0].shape[0]
        embed, gain, shift = (r[...].astype(F32) for r in (embed_ref, gain_ref, shift_ref))
        for d in range(tm):
            rows = slice(d * seg, (d + 1) * seg)
            filled = jnp.where(mask_ref[rows] > 0.5, embed, blocks[d][...].astype(F32)) + pos_ref[rows].astype(F32)
            unit, _ = norm_parts(filled)
            normed = (unit * gain + shift).astype(BF16)
            filled_ref[rows] = filled
            normed_s[rows] = normed
            turned_ref[:, rows] = normed.T

    joint_ref[...] = (contract(normed_s[...], w_ref[...], 1, 0) + bias_ref[...].astype(F32)).astype(BF16)


def project(blocks, mask, embed, pos, gain, shift, w_qkv, bias):
    tm = len(blocks)
    seg, width = blocks[0].shape
    rows = tm * seg
    return call(
        functools.partial(project_kernel, tm=tm),
        grid=(3,),
        in_specs=[fixed((seg, width))] * tm
        + [fixed((rows, 1)), fixed((1, width)), fixed((rows, width)), fixed((1, width)), fixed((1, width))]
        + [pl.BlockSpec((width, width), lambda j: (0, j)), pl.BlockSpec((1, width), lambda j: (0, j))],
        out_specs=[
            pl.BlockSpec((rows, width), lambda j: (0, 0)),
            pl.BlockSpec((width, rows), lambda j: (0, 0)),
            pl.BlockSpec((rows, width), lambda j: (0, j)),
        ],
        out_shape=[shaped((rows, width), F32), shaped((width, rows), BF16), shaped((rows, 3 * width), BF16)],
        scratch=[pltpu.VMEM((rows, width), BF16)],
        flops=6 * rows * width * width,
        moved=20 * rows * width,
    )(*blocks, mask, embed, pos, gain, shift, w_qkv, bias)


def own_lanes(value, i, head):
    lane = lax.broadcasted_iota(jnp.int32, value.shape, 1)
    return jnp.where((lane >= i * head) & (lane < (i + 1) * head), value, jnp.zeros_like(value))


def attend_kernel(q_ref, k_ref, v_ref, o_ref, turned_ref, log_ref, *, head):
    factor = head**-0.5 * LOG2_E
    for pair in range(q_ref.shape[1] // LANES):
        lanes = slice(pair * LANES, (pair + 1) * LANES)
        q, k, v = q_ref[:, lanes], k_ref[:, lanes], v_ref[:, lanes]
        outs = []
        for i in range(LANES // head):
            scores = contract(k, own_lanes(q, i, head), 1, 1)
            peak = jnp.max(scores, 0, keepdims=True)
            raised = jnp.exp2((scores - peak) * factor)
            total = jnp.sum(raised, 0, keepdims=True)
            mixed = contract(v, raised.astype(BF16), 0, 0)
            outs.append(mixed[i * head : (i + 1) * head] * (1.0 / total))
            log_ref[pair, i : i + 1, :] = peak * factor + jnp.log2(total)
        turned = jnp.concatenate(outs, 0)
        turned_ref[lanes] = turned.astype(BF16)
        o_ref[:, lanes] = turned.T.astype(BF16)


def attend(joint, width):
    rows = joint.shape[0]
    head = width // HEADS
    pairs, per = width // LANES, LANES // head
    some = 2 if pairs % 2 == 0 else 1
    steps = pairs // some
    block = lambda off: pl.BlockSpec((rows, some * LANES), lambda h: (0, h + off))
    return call(
        functools.partial(attend_kernel, head=head),
        grid=(steps,),
        in_specs=[block(0), block(steps), block(2 * steps)],
        out_specs=[
            block(0),
            pl.BlockSpec((some * LANES, rows), lambda h: (h, 0)),
            pl.BlockSpec((some, per, rows), lambda h: (h, 0, 0)),
        ],
        out_shape=[shaped((rows, width), BF16), shaped((width, rows), BF16), shaped((pairs, per, rows), F32)],
        flops=16 * rows * rows * width,
        moved=8 * rows * width,
        exps=rows * rows * HEADS,
    )(joint, joint, joint)


def attend_back_kernel(side_ref, *refs, head, groups):
    per_clip = [refs[4 * c : 4 * c + 4] for c in range(groups)]
    g_ref, out_ref = refs[4 * groups :]
    scale = head**-0.5
    for c, (q_ref, k_ref, v_ref, log_ref) in enumerate(per_clip):
        rows = slice(c * q_ref.shape[0], (c + 1) * q_ref.shape[0])
        q, k, v, g = q_ref[...], k_ref[...], v_ref[...], g_ref[rows]
        grad_q, grad_k, grad_v = [], 0.0, 0.0
        for i in range(q.shape[1] // head):
            q_own, g_own = own_lanes(q, i, head), own_lanes(g, i, head)
            scores = contract(k, q_own, 1, 1)
            probs = jnp.exp2(scores * (scale * LOG2_E) - log_ref[0, i : i + 1, :])
            grad_probs = contract(v, g_own, 1, 1)
            delta = jnp.sum(probs * grad_probs, 0, keepdims=True)
            grad_scores = (probs * (grad_probs - delta)).astype(BF16)
            grad_q.append(contract(k, grad_scores, 0, 0)[i * head : (i + 1) * head])
            grad_k = grad_k + contract(grad_scores, q_own, 1, 0)
            grad_v = grad_v + contract(probs.astype(BF16), g_own, 1, 0)
        out_ref[0, rows] = (jnp.concatenate(grad_q, 0) * scale).T.astype(BF16)
        out_ref[1, rows] = (grad_k * scale).astype(BF16)
        out_ref[2, rows] = grad_v.astype(BF16)


def attend_back(side, joints, mix, logs):
    rows, width = mix.shape
    groups = len(joints)
    length = rows // groups
    head = width // HEADS
    pairs, per = width // LANES, LANES // head
    half = pairs // 2

    def block(off):
        return pl.BlockSpec((length, LANES), lambda h, s: (0, off + s[0] * half + h))

    clip = [block(0), block(pairs), block(2 * pairs), pl.BlockSpec((1, per, length), lambda h, s: (s[0] * half + h, 0, 0))]
    operands = []
    for joint, log_sum in zip(joints, logs):
        operands += [joint, joint, joint, log_sum]
    return call(
        functools.partial(attend_back_kernel, head=head, groups=groups),
        prefetch=1,
        share=16,
        grid=(half,),
        in_specs=clip * groups + [pl.BlockSpec((rows, LANES), lambda h, s: (0, s[0] * half + h))],
        out_specs=pl.BlockSpec((3, rows, LANES), lambda h, s: (0, 0, h)),
        out_shape=shaped((3, rows, width // 2), BF16),
        flops=20 * rows * length * width,
        moved=8 * rows * width,
        exps=rows * length * HEADS // 2,
    )(side, *operands, mix)


def gelu_parts(u):
    phi = 0.5 * (1.0 + lax.erf(u * ROOT_HALF))
    return u * phi, phi + u * jnp.exp(-0.5 * u * u) * (1.0 / ROOT_TWO_PI)


def forward_kernel(*refs, groups, chunk):
    filled, attended = refs[:groups], refs[groups : 2 * groups]
    (w_out_ref, out_bias_ref, gain_ref, shift_ref, down_bias_ref, w_up_ref, up_bias_ref, w_down_ref,
     hidden_ref, turned_ref, act_ref, slope_ref, block_ref, out_s, normed_s) = refs[2 * groups :]
    rows_all = out_s.shape[0]
    step, last = pl.program_id(0), pl.num_programs(0) - 1

    @pl.when(step == 0)
    def _():
        gain, shift = gain_ref[...].astype(F32), shift_ref[...].astype(F32)
        out_bias, down_bias = out_bias_ref[...].astype(F32), down_bias_ref[...].astype(F32)
        length = filled[0].shape[0]
        for c in range(groups):
            rows = slice(c * length, (c + 1) * length)
            hidden = filled[c][...] + contract(attended[c][...], w_out_ref[...], 1, 0) + out_bias
            unit, _ = norm_parts(hidden)
            normed = (unit * gain + shift).astype(BF16)
            hidden_ref[rows] = hidden
            normed_s[rows] = normed
            turned_ref[:, rows] = normed.T
            out_s[rows] = hidden + down_bias

    w_up, w_down = w_up_ref[...], w_down_ref[...]
    bias = up_bias_ref[...].astype(F32)
    for r in range(rows_all // chunk):
        rows = slice(r * chunk, (r + 1) * chunk)
        value, slope = gelu_parts(contract(normed_s[rows], w_up, 1, 0) + bias)
        act = value.astype(BF16)
        act_ref[:, rows] = act.T
        slope_ref[rows] = slope.astype(BF16)
        out_s[rows] += contract(act, w_down, 1, 0)

    @pl.when(step == last)
    def _():
        block_ref[...] = out_s[...].astype(BF16)


def forward(filled, attended, w_out, out_bias, gain, shift, down_bias, w_up, up_bias, w_down, tile, chunk):
    groups, (length, width) = len(filled), filled[0].shape
    rows, ff = groups * length, w_up.shape[1]
    vec = fixed((1, width))
    whole = pl.BlockSpec((rows, width), lambda j: (0, 0), pipeline_mode=pl.Buffered(1))
    column = pl.BlockSpec((rows, tile), lambda j: (0, j))
    return call(
        functools.partial(forward_kernel, groups=groups, chunk=chunk),
        grid=(ff // tile,),
        in_specs=[fixed((length, width))] * (2 * groups)
        + [fixed((width, width)), vec, vec, vec, vec]
        + [
            pl.BlockSpec((width, tile), lambda j: (0, j)),
            pl.BlockSpec((1, tile), lambda j: (0, j)),
            pl.BlockSpec((tile, width), lambda j: (j, 0)),
        ],
        out_specs=[whole, fixed((width, rows)), pl.BlockSpec((tile, rows), lambda j: (j, 0)), column, whole],
        out_shape=[shaped((rows, width), F32), shaped((width, rows), BF16)]
        + [shaped((ff, rows), BF16), shaped((rows, ff), BF16)]
        + [shaped((rows, width), BF16)],
        scratch=[pltpu.VMEM((rows, width), F32), pltpu.VMEM((rows, width), BF16)],
        flops=4 * rows * width * ff + 2 * rows * width * width,
        moved=14 * rows * width + 4 * rows * ff + 4 * width * ff,
        exps=rows * ff,
    )(*filled, *attended, w_out, out_bias, gain, shift, down_bias, w_up, up_bias, w_down)


def tile_back(turned_ref, cot_ref, act_ref, slope_ref, w_up_ref, w_down_ref, gup_s, norm_s, down_ref, up_ref, bias_ref, chunk):
    w_up, w_down = w_up_ref[...], w_down_ref[...]
    total = jnp.zeros(bias_ref.shape, F32)
    for r in range(cot_ref.shape[0] // chunk):
        rows = slice(r * chunk, (r + 1) * chunk)
        gup = (contract(cot_ref[rows], w_down, 1, 1) * slope_ref[rows].astype(F32)).astype(BF16)
        gup_s[rows] = gup
        total = total + jnp.sum(gup.astype(F32), 0, keepdims=True)
        norm_s[rows] += contract(gup, w_up, 1, 1)
    bias_ref[...] = total
    down_ref[...] = contract(act_ref[...], cot_ref[...], 1, 0).astype(BF16)
    up_ref[...] = contract(turned_ref[...], gup_s[...], 1, 0).astype(BF16)


def back_first_kernel(side_ref, turned_ref, cot_ref, act_ref, slope_ref, w_up_ref, w_down_ref, norm_ref, down_ref, up_ref, bias_ref, gup_s, *, chunk):
    @pl.when(pl.program_id(0) == 0)
    def _():
        norm_ref[...] = jnp.zeros_like(norm_ref)

    tile_back(turned_ref, cot_ref, act_ref, slope_ref, w_up_ref, w_down_ref, gup_s, norm_ref, down_ref, up_ref, bias_ref, chunk)


def back_last_kernel(side_ref, *refs, groups, chunk):
    attended = refs[:groups]
    (turned_ref, cot_ref, act_ref, slope_ref, w_up_ref, w_down_ref, w_out_ref, gain_ref, hidden_ref, norm_ref,
     down_ref, up_ref, bias_ref, grad_hidden_ref, mix_ref, grad_out_ref, sums_ref, gup_s, norm_s, branch_s) = refs[groups:]

    @pl.when(pl.program_id(0) == 0)
    def _():
        norm_s[...] = norm_ref[...]

    tile_back(turned_ref, cot_ref, act_ref, slope_ref, w_up_ref, w_down_ref, gup_s, norm_s, down_ref, up_ref, bias_ref, chunk)

    @pl.when(pl.program_id(0) == pl.num_programs(0) - 1)
    def _():
        gain = gain_ref[...].astype(F32)
        total = [jnp.zeros_like(gain) for _ in range(4)]
        w_out = w_out_ref[...]
        for r in range(norm_s.shape[0] // chunk):
            rows = slice(r * chunk, (r + 1) * chunk)
            unit, inverse = norm_parts(hidden_ref[rows])
            top, grad_norm = cot_ref[rows].astype(F32), norm_s[rows]
            grad_hidden = top + norm_backward(grad_norm, unit, inverse, gain)
            grad_hidden_ref[rows] = grad_hidden
            branch = grad_hidden.astype(BF16)
            branch_s[rows] = branch
            mix_ref[rows] = contract(branch, w_out, 1, 1).astype(BF16)
            parts = (branch.astype(F32), top, grad_norm * unit, grad_norm)
            total = [t + jnp.sum(p, 0, keepdims=True) for t, p in zip(total, parts)]
        sums_ref[...] = jnp.concatenate(total + [jnp.zeros_like(gain)] * 4, 0)
        length = attended[0].shape[1]
        grad_out = 0.0
        for c in range(groups):
            grad_out = grad_out + contract(attended[c][...], branch_s[c * length : (c + 1) * length], 1, 0)
        grad_out_ref[...] = grad_out.astype(BF16)


def back_specs(rows, width, half, tile):
    steps = half // tile
    column = lambda n: pl.BlockSpec((n, tile), lambda j, s: (0, s[0] * steps + j))
    ins = [fixed((width, rows)), fixed((rows, width))]
    ins += [pl.BlockSpec((tile, rows), lambda j, s: (s[0] * steps + j, 0)), column(rows), column(width)]
    ins.append(pl.BlockSpec((tile, width), lambda j, s: (s[0] * steps + j, 0)))
    outs = [
        pl.BlockSpec((tile, width), lambda j, s: (j, 0)),
        pl.BlockSpec((width, tile), lambda j, s: (0, j)),
        pl.BlockSpec((1, tile), lambda j, s: (0, j)),
    ]
    return ins, outs, [shaped((half, width), BF16), shaped((width, half), BF16), shaped((1, half), F32)]


def back_first(side, normed, cot, act, slope, w_up, w_down, tile, chunk):
    rows, width = cot.shape
    half = w_up.shape[1] // 2
    ins, outs, shapes = back_specs(rows, width, half, tile)
    return call(
        functools.partial(back_first_kernel, chunk=chunk),
        prefetch=1,
        grid=(half // tile,),
        in_specs=ins,
        out_specs=[fixed((rows, width))] + outs,
        out_shape=[shaped((rows, width), F32)] + shapes,
        scratch=[pltpu.VMEM((rows, tile), BF16)],
        flops=8 * rows * width * half,
        moved=8 * rows * width + 4 * rows * half + 8 * width * half,
    )(side, normed, cot, act, slope, w_up, w_down)


def back_last(side, attended, normed, cot, act, slope, w_up, w_down, w_out, gain, hidden, norm, tile, chunk):
    rows, width = cot.shape
    groups = len(attended)
    half = w_up.shape[1] // 2
    ins, outs, shapes = back_specs(rows, width, half, tile)
    whole = lambda n: fixed((n, width))
    return call(
        functools.partial(back_last_kernel, groups=groups, chunk=chunk),
        prefetch=1,
        grid=(half // tile,),
        in_specs=[fixed((width, rows // groups))] * groups + ins + [whole(width), whole(1), whole(rows), whole(rows)],
        out_specs=outs + [whole(rows), whole(rows), whole(width), whole(8)],
        out_shape=shapes
        + [shaped((rows, width), F32), shaped((rows, width), BF16), shaped((width, width), BF16), shaped((8, width), F32)],
        scratch=[pltpu.VMEM((rows, tile), BF16), pltpu.VMEM((rows, width), F32), pltpu.VMEM((rows, width), BF16)],
        flops=8 * rows * width * half + 4 * rows * width * width,
        moved=20 * rows * width + 4 * rows * half + 8 * width * half,
    )(side, *attended, normed, cot, act, slope, w_up, w_down, w_out, gain, hidden, norm)


def joint_part(normed, grad_ref, grad_w_ref, bias_ref):
    length = normed[0].shape[1]
    grad_w = 0.0
    for c, normed_ref in enumerate(normed):
        grad_w = grad_w + contract(normed_ref[...], grad_ref[0, c * length : (c + 1) * length], 1, 0)
    grad_w_ref[...] = grad_w.astype(BF16)
    bias_ref[0] = jnp.sum(grad_ref[0].astype(F32), 0, keepdims=True)


def joint_first_kernel(side_ref, *refs, groups):
    normed, (grad_ref, weight_ref, grad_w_ref, bias_ref, acc_ref) = refs[:groups], refs[groups:]
    joint_part(normed, grad_ref, grad_w_ref, bias_ref)
    part = contract(grad_ref[0], weight_ref[...], 1, 1)

    @pl.when(pl.program_id(0) == 0)
    def _():
        acc_ref[...] = part

    @pl.when(pl.program_id(0) > 0)
    def _():
        acc_ref[...] += part


def joint_last_kernel(side_ref, *refs, groups, chunk, tm):
    normed, (grad_ref, weight_ref, acc_ref, grad_hidden_ref, gain_ref) = refs[:groups], refs[groups : groups + 5]
    refs = refs[groups + 5 :]
    filled, masks = refs[:groups], refs[groups : 2 * groups]
    (other_bias_ref, sums_ref, up_other_ref, up_own_ref, grad_w_ref, input_ref, rest_ref,
     acc_s, pos_s, bias_s) = refs[2 * groups :]
    core, me = side_ref[0], side_ref[1]
    length, half = normed[0].shape[1], grad_w_ref.shape[1]
    step = pl.program_id(0)
    joint_part(normed, grad_ref, grad_w_ref, bias_s.at[pl.ds(step, 1)])

    @pl.when(step == 0)
    def _():
        acc_s[...] = acc_ref[...] + contract(grad_ref[0], weight_ref[...], 1, 1)

    @pl.when(step == 1)
    def _():
        acc_s[...] += contract(grad_ref[0], weight_ref[...], 1, 1)

    @pl.when(step == 2)
    def _():
        gain = gain_ref[...].astype(F32)
        weight = weight_ref[...]
        total = [jnp.zeros_like(gain) for _ in range(3)]
        for c in range(groups):
            for r in range(length // chunk):
                clip = slice(r * chunk, (r + 1) * chunk)
                rows = slice(c * length + r * chunk, c * length + (r + 1) * chunk)
                grad_norm = acc_s[rows] + contract(grad_ref[0, rows], weight, 1, 1)
                unit, inverse = norm_parts(filled[c][clip])
                grad_filled = grad_hidden_ref[rows] + norm_backward(grad_norm, unit, inverse, gain)
                masked = masks[c][clip] > 0.5
                input_ref[rows] = jnp.where(masked, 0.0, grad_filled).astype(BF16)
                parts = (grad_norm * unit, grad_norm, jnp.where(masked, grad_filled, 0.0))
                total = [t + jnp.sum(p, 0, keepdims=True) for t, p in zip(total, parts)]
                pos_s[clip] = grad_filled if c == 0 else pos_s[clip] + grad_filled
        seg = length // tm
        for d in range(tm):
            at = pl.multiple_of((me ^ d) * seg, seg)
            rest_ref[pl.ds(at, seg)] = pos_s[d * seg : (d + 1) * seg].astype(BF16)

        def both(other, mine):
            return jnp.where(core == 0, jnp.concatenate([mine, other], 1), jnp.concatenate([other, mine], 1))

        width = gain.shape[1]
        up = both(up_other_ref[...], up_own_ref[...])
        sums = sums_ref[...]
        lines = [both(other_bias_ref[i], bias_s[i]) for i in (0, 2)] + [sums[0:1]]
        lines += [up[:, i * width : (i + 1) * width] for i in range(up.shape[1] // width)]
        lines += [sums[1:2], total[0], total[1], sums[2:3], sums[3:4], total[2]]
        lines.append(jnp.zeros((rest_ref.shape[0] - length - len(lines), width), F32))
        rest_ref[length:] = jnp.concatenate(lines, 0).astype(BF16)


def joint_specs(groups, rows, width):
    half = width // 2
    return [fixed((width, rows // groups))] * groups + [
        pl.BlockSpec((1, rows, half), lambda i, s: (i, 0, 0)),
        pl.BlockSpec((width, half), lambda i, s: (0, 2 * i + s[0])),
    ]


def joint_first(side, normed, grads, w_qkv):
    _, rows, half = grads.shape
    groups, width = len(normed), 2 * half
    return call(
        functools.partial(joint_first_kernel, groups=groups),
        prefetch=1,
        share=16,
        grid=(3,),
        in_specs=joint_specs(groups, rows, width),
        out_specs=[
            pl.BlockSpec((width, half), lambda i, s: (0, i)),
            pl.BlockSpec((1, 1, half), lambda i, s: (i, 0, 0)),
            fixed((rows, width)),
        ],
        out_shape=[shaped((width, 3 * half), BF16), shaped((3, 1, half), F32), shaped((rows, width), F32)],
        flops=6 * rows * width * width,
        moved=12 * rows * width,
    )(side, *normed, grads, w_qkv)


def joint_last(side, normed, grads, w_qkv, acc, grad_hidden, gain, filled, masks, bias, sums, up_other, up_own, tm, chunk):
    _, rows, half = grads.shape
    groups, width = len(normed), 2 * half
    length = rows // groups
    return call(
        functools.partial(joint_last_kernel, groups=groups, chunk=chunk, tm=tm),
        prefetch=1,
        share=16,
        grid=(3,),
        in_specs=joint_specs(groups, rows, width)
        + [fixed((rows, width))] * 2
        + [fixed((1, width))]
        + [fixed((length, width))] * groups
        + [fixed((length, 1))] * groups
        + [fixed((3, 1, half)), fixed((8, width)), fixed(up_other.shape), fixed(up_own.shape)],
        out_specs=[pl.BlockSpec((width, half), lambda i, s: (0, i)), fixed((rows, width)), fixed((width, width))],
        out_shape=[shaped((width, 3 * half), BF16), shaped((rows, width), BF16), shaped((width, width), BF16)],
        scratch=[
            pltpu.VMEM((rows, width), F32),
            pltpu.VMEM((length, width), F32),
            pltpu.VMEM((3, 1, half), F32),
        ],
        flops=6 * rows * width * width,
        moved=24 * rows * width,
    )(side, *normed, grads, w_qkv, acc, grad_hidden, gain, *filled, *masks, bias, sums, up_other, up_own)


def cores_in_order(here_ref, own_ref, other_ref):
    low = here_ref[1] == 0
    own, other = own_ref[0], other_ref[0]
    return [jnp.where(low, own, other).astype(F32), jnp.where(low, other, own).astype(F32)]


def place_one_kernel(here_ref, down_own_ref, up_own_ref, down_other_ref, up_other_ref, down_ref, up_ref):
    width = down_ref.shape[2]
    for core, share in enumerate(cores_in_order(here_ref, down_own_ref, down_other_ref)):
        for part in range(share.shape[1] // width):
            down_ref[core, part * share.shape[0] : (part + 1) * share.shape[0]] = share[:, part * width : (part + 1) * width]
    for core, share in enumerate(cores_in_order(here_ref, up_own_ref, up_other_ref)):
        up_ref[:, core * share.shape[1] : (core + 1) * share.shape[1]] = share


def place_two_kernel(here_ref, qkv_own_ref, own_ref, qkv_other_ref, other_ref, qkv_ref, out_ref, rest_ref):
    width = out_ref.shape[1]
    half = width // 2
    for core, share in enumerate(cores_in_order(here_ref, qkv_own_ref, qkv_other_ref)):
        for i in range(3):
            qkv_ref[:, i * width + core * half : i * width + (core + 1) * half] = share[:, i * half : (i + 1) * half]
    out_ref[...], rest_ref[...] = cores_in_order(here_ref, own_ref, other_ref)


def spot_bits(order, tm):
    return [bits_of(bit) if axis == "tm" else bits_of(tm) + bits_of(bit) - 1 for axis, bit in order]


def place(kernel, here, gathered, orders, tm, shapes):
    steps = gathered[0].shape[0]

    def share(value, order):
        bits = spot_bits(order, tm)

        def index(j, here):
            away = j ^ here[0]
            return sum(((away >> b) & 1) << k for k, b in enumerate(bits)), 0, 0

        return pl.BlockSpec((1,) + value.shape[1:], index)

    def cut(shape):
        block = shape[:-2] + (shape[-2] // steps, shape[-1])
        return pl.BlockSpec(block, lambda j, here: (0,) * (len(shape) - 2) + (j, 0))

    return call(
        kernel,
        prefetch=1,
        grid=(steps,),
        in_specs=[share(v, o) for v, o in zip(gathered, orders * 2)],
        out_specs=[cut(s) for s in shapes],
        out_shape=[shaped(s, F32) for s in shapes],
        moved=sum(6 * v.size for v in gathered),
    )(here, *gathered)


def in_order(here, gathered, orders, tm):
    out = []
    half = len(gathered) // 2
    for own, other, order in zip(gathered[:half], gathered[half:], orders):
        bits = spot_bits(order, tm)
        away = jnp.arange(own.shape[0], dtype=jnp.int32) ^ here[0]
        index = sum(((away >> b) & 1) << k for k, b in enumerate(bits))
        own, other = (jnp.take(x, index, axis=0).astype(F32) for x in (own, other))
        low = here[1] == 0
        out.append(jnp.stack([jnp.where(low, own, other), jnp.where(low, other, own)]))
    return out


def bits_of(size):
    return size.bit_length() - 1


def axis_bits(axis):
    return [(axis, 1 << b) for b in range(bits_of(lax.axis_size(axis)))]


def own_bit(axis, bit):
    return (lax.axis_index(axis) // bit) % 2


def hop(value, axis, bit):
    size = lax.axis_size(axis)
    return lax.ppermute(value, axis, [(i, i ^ bit) for i in range(size)])


def tie(*values):
    return lax.optimization_barrier(values)


def take_clips(values):
    tm = lax.axis_size("tm")
    me = lax.axis_index("tm")
    out = []
    for d in range(tm):
        block = lax.dynamic_index_in_dim(values, me ^ d, 1, keepdims=False)
        out.append(hop(block, "tm", d) if d else block)
    return out


def send_clips(values):
    blocks = jnp.split(values, lax.axis_size("tm"), 1)
    return [hop(block, "tm", d) if d else block for d, block in enumerate(blocks)]


def all_clips(blocks, shape):
    return jnp.stack(unshuffle(blocks), 1).reshape(shape)


def unshuffle(blocks):
    me = lax.axis_index("tm")
    blocks = list(blocks)
    for b in range(bits_of(len(blocks))):
        odd = ((me >> b) & 1) == 1
        blocks = [jnp.where(odd, blocks[i ^ (1 << b)], blocks[i]) for i in range(len(blocks))]
    return blocks


def add_low(a, b):
    return (a.astype(F32) + b.astype(F32)).astype(BF16)


def split_share(value):
    count = bits_of(lax.axis_size("clips")) + bits_of(lax.axis_size("tm")) - 1
    return value.reshape((2,) * count + (value.shape[0] >> count, value.shape[1]))


def side_by_side(value, parts):
    return jnp.concatenate(jnp.split(value, parts, -2), -1)


class Sum:
    def __init__(self, folds):
        self.folds = folds
        clip_bits, self.time_bits = axis_bits("clips")[1:], axis_bits("tm")
        self.names = clip_bits[::-1] + self.time_bits[::-1]
        self.orders = (clip_bits, clip_bits[1:] + clip_bits[:1])
        self.rounds = len(clip_bits) + len(self.time_bits)

    def halves(self, pair, names, name):
        at = names.index(name)
        mine = own_bit(*name)
        pick = lambda x, i: lax.dynamic_index_in_dim(x, i, at, keepdims=False)
        return [add_low(*(pick(x, i) for x in pair)) for i in (1 - mine, mine)]

    def split(self, index, state):
        sides = len(self.orders[0])
        if index < sides:
            out = []
            for pair, order in zip(state, self.orders):
                names = [n for n in self.names if n not in order[:index]]
                away, kept = self.halves(pair, names, order[index])
                out.append((kept, away))
            return out
        name = self.time_bits[index - sides]
        names = self.time_bits[index - sides :][::-1]
        parts = [self.halves(pair, names, name) for pair in state]
        if len(state) > 1:
            parts = [[side_by_side(x, n) if n > 1 else x for x in p] for p, n in zip(parts, self.folds)]
        away, kept = (jnp.concatenate(x, -1) if len(x) > 1 else x[0] for x in zip(*parts))
        return [(kept, away)]

    def send(self, index, state):
        sides = len(self.orders[0])
        names = [o[index] for o in self.orders] if index < sides else [self.time_bits[index - sides]]
        return [(kept, hop(away, *name)) for (kept, away), name in zip(state, names)]

    def scatter(self, index, state):
        return self.send(index, self.split(index, state))

    def share(self, state):
        return add_low(*state[0])

    def gather_orders(self):
        return [self.time_bits[::-1] + order[::-1] for order in self.orders]

    def gather(self, index, state, cut):
        if index < len(self.time_bits):
            return [(state[0], hop(state[0], *self.time_bits[::-1][index]))]
        names = [order[::-1][index - len(self.time_bits)] for order in self.orders]
        return [(value, hop(value, *name)) for value, name in zip(state, names)]

    def join(self, index, state, cut):
        out = [jnp.concatenate(pair, 0) for pair in state]
        if index == len(self.time_bits) - 1:
            return [out[0][..., :cut], out[0][..., cut:]]
        return out


def on_device(
    patches, mask_index, mask_count, w_qkv, q_bias, v_bias, w_out, out_bias, w_up, up_bias,
    w_down, down_bias, norm1_scale, norm1_shift, norm2_scale, norm2_shift, mask_embed, pos_embed,
    cotangent,
):
    clip_count, seg, width = patches.shape
    ff = w_up.shape[1]
    tm = lax.axis_size("tm")
    me = lax.axis_index("tm")
    length = seg * tm
    groups = clip_count // tm
    by_group = (groups, tm, seg, width)
    tile, chunk = 512, 512

    arrived = [[b[0] for b in take_clips(patches.reshape(by_group)[g : g + 1])] for g in range(groups)]

    row = lambda x: x.reshape(1, -1)
    joint_bias = row(jnp.concatenate([q_bias, jnp.zeros_like(q_bias), v_bias]))
    out_bias, up_bias, down_bias, gain1, shift1, gain2, shift2, embed = map(
        row, (out_bias, up_bias, down_bias, norm1_scale, norm1_shift, norm2_scale, norm2_shift, mask_embed)
    )
    starts = (me ^ jnp.arange(tm, dtype=jnp.int32)) * seg
    places = (starts[:, None] + jnp.arange(seg, dtype=jnp.int32)[None, :]).reshape(length)
    pos = jnp.concatenate([lax.dynamic_slice_in_dim(pos_embed, (me ^ d) * seg, seg, 0) for d in range(tm)], 0)
    slots = jnp.arange(mask_index.shape[1], dtype=jnp.int32)
    masks = []
    for g in range(groups):
        index_row = lax.dynamic_index_in_dim(mask_index, g * tm + me, 0, keepdims=False)
        count = lax.dynamic_index_in_dim(mask_count, g * tm + me, 0, keepdims=False)
        hit = (places[:, None] == index_row[None, :]) & (slots < count)[None, :]
        masks.append(jnp.any(hit, axis=1, keepdims=True).astype(F32))

    filled, normed_one, joints, attended, turned, logs = [], [], [], [], [], []
    for g in range(groups):
        if g:
            *blocks, last = tie(*arrived[g], attended[-1])
            attended[-1] = last
        else:
            blocks = arrived[g]
        f, n, j = project(blocks, masks[g], embed, pos, gain1, shift1, w_qkv, joint_bias)
        a, a_turned, log_sum = attend(j, width)
        for kept, value in zip((filled, normed_one, joints, attended, turned, logs), (f, n, j, a, a_turned, log_sum)):
            kept.append(value)
        if not g:
            tied, joints[0] = tie(cotangent, j)
            cot = take_clips(tied.reshape(by_group))

    core = own_bit("clips", 1).astype(jnp.int32)
    kept_side = jnp.stack([core, me.astype(jnp.int32)])
    away_side = jnp.stack([1 - core, me.astype(jnp.int32)])
    here = jnp.stack([(lax.axis_index("clips") // 2 * tm + me).astype(jnp.int32), core])
    hidden, normed_two, act, slope, block_out = forward(
        filled, attended, w_out, out_bias, gain2, shift2, down_bias, w_up, up_bias, w_down, 768, length * groups
    )
    cot = jnp.concatenate(cot, 1).reshape(groups * length, width)
    cot, block_out = tie(cot, block_out)
    norm_acc, down, up, up_sums_away = back_first(away_side, normed_two, cot, act, slope, w_up, w_down, tile, chunk)
    down_got, up_got = hop(down, "clips", 1), hop(up, "clips", 1)
    down, up, up_sums, grad_hidden, mix, grad_out, sums_two = back_last(
        kept_side, turned, normed_two, cot, act, slope, w_up, w_down, w_out, gain2, hidden, norm_acc, tile, chunk
    )
    one = Sum((2, 1))

    def after(values, *states):
        flat = [x for state in states for pair in state for x in pair]
        tied = list(tie(*values, *flat))
        values, flat = tied[: len(values)], tied[len(values) :]
        back = [[tuple(flat.pop(0) for _ in pair) for pair in state] for state in states]
        return (values, *back)

    state = [tuple(split_share(x) for x in pair) for pair in ((down, down_got), (up, up_got))]
    state = one.split(0, state)
    (mix, block_out), state = after((mix, block_out), state)
    state = one.send(0, state)
    block_out = send_clips(block_out.reshape(groups, length, width))
    grads = attend_back(away_side, joints, mix, logs)
    qkv, bias_sums, acc = joint_first(away_side, normed_one, grads, w_qkv)
    qkv_got = hop(qkv, "clips", 1)
    (acc,), state = after((acc,), state)
    state = one.split(1, state)
    (mix, acc), state = after((mix, acc), state)
    state = one.send(1, state)
    grads = attend_back(kept_side, joints, mix, logs)
    (grads,), state = after((grads,), state)
    state = one.split(2, state)
    tied, state = after((grads, *block_out), state)
    grads, block_out = tied[0], tied[1:]
    state = one.send(2, state)
    qkv, input_grad, rest = joint_last(
        kept_side, normed_one, grads, w_qkv, acc, grad_hidden, gain1, filled, masks, bias_sums, sums_two,
        up_sums_away, up_sums, tm, chunk
    )
    rest_away = jnp.where(core == 1, grad_out, rest)
    rest_kept = jnp.where(core == 1, rest, grad_out)
    rest_got = hop(rest_away, "clips", 1)
    two = Sum((1, 1))
    pairs = [tuple(split_share(x) for x in pair) for pair in ((qkv, qkv_got), (rest_kept, rest_got))]
    cut_one, cut_two = ff // 2, 3 * width // 2
    share_rows = pairs[0][0].shape[-2]

    def scatter_steps(group, first):
        steps = [lambda s, i=i: group.split(i, s) for i in range(first, group.rounds)]
        return [(split, lambda s, i=i: group.send(i, s)) for i, split in zip(range(first, group.rounds), steps)]

    def gather_steps(group, cut):
        def prepare(i):
            if i == 0:
                return lambda s: [(group.share(s)[None],)]
            return lambda s: [(x,) for x in group.join(i - 1, s, cut)]

        return [
            (prepare(i), lambda s, i=i: group.gather(i, [x for (x,) in s], cut)) for i in range(group.rounds)
        ]

    def core_steps(group, cut):
        return [
            (
                lambda s: [(x,) for x in group.join(group.rounds - 1, s, cut)],
                lambda s: [(x, hop(x, "clips", 1)) for (x,) in s],
            )
        ]

    steps_one = scatter_steps(one, 3) + gather_steps(one, cut_one) + core_steps(one, cut_one)
    steps_two = scatter_steps(two, 0) + gather_steps(two, cut_two) + core_steps(two, cut_two)
    outputs = []
    for index in range(max(len(steps_one), len(steps_two))):
        active = [steps[index] if index < len(steps) else None for steps in (steps_one, steps_two)]
        states = [step[0](x) if step else x for step, x in zip(active, (state, pairs))]
        live = [x for x, step in zip(states, active) if step]
        if index == 3:
            (input_grad,), *live = after((input_grad,), *live)
            sent = send_clips(input_grad.reshape(groups, length, width))
        elif index == len(steps_two) - 1:
            tied, *live = after((*sent, *outputs), *live)
            sent, outputs = tied[: len(sent)], tied[len(sent) :]
        else:
            _, *live = after((), *live)
        live = iter(live)
        state, pairs = (step[1](next(live)) if step else x for step, x in zip(active, states))
        if index == len(steps_one) - 1:
            one_all = [own for own, _ in state] + [other for _, other in state]
            if share_rows % 8 == 0:
                outputs = place(
                    place_one_kernel, here, one_all, one.gather_orders(), tm, ((2, ff // 2, width), (width, ff))
                )
    two_all = [own for own, _ in pairs] + [other for _, other in pairs]
    block_out, input_grad = all_clips(block_out, patches.shape), all_clips(sent, patches.shape)

    orders_one, orders_two = one.gather_orders(), two.gather_orders()
    if share_rows % 8 == 0:
        down_sum, up_sum = outputs
        qkv_sum, out_sum, rest = place(
            place_two_kernel, here, two_all, orders_two, tm, ((width, 3 * width), (width, width), (width, width))
        )
        down_sum = down_sum.reshape(ff, width)
    else:
        downs, ups = in_order(here, one_all, orders_one, tm)
        qkvs, rests = in_order(here, two_all, orders_two, tm)
        down_sum = jnp.stack(jnp.split(downs, 2, -1), 2).reshape(ff, width)
        up_sum = jnp.concatenate(list(ups.reshape(2, width, ff // 2)), 1)
        qkv_sum = jnp.stack(list(qkvs.reshape(2, width, 3, width // 2)), 2).reshape(width, 3 * width)
        out_sum, rest = rests.reshape(2, width, width)
    v = []
    at = length
    for n in (1, 1, 1, ff // width, 1, 1, 1, 1, 1, 1):
        v.append(rest[at : at + n].reshape(-1))
        at += n
    return (block_out, input_grad, qkv_sum, v[0], v[1], out_sum, v[2], up_sum, v[3], down_sum, v[4],
            v[5], v[6], v[7], v[8], v[9], rest[:length])


def solution(mesh):
    rows = P("clips", "tm", None)
    in_specs = (rows, P("clips", None), P("clips")) + (P(),) * 15 + (rows,)
    out_specs = (rows, rows) + (P(),) * 15
    return jax.shard_map(on_device, mesh=mesh, in_specs=in_specs, out_specs=out_specs, check_vma=False)
```

```python
import functools

import jax
import jax.numpy as jnp
from jax import lax
from jax.experimental import pallas as pl
from jax.experimental.pallas import tpu as pltpu
from jax.sharding import PartitionSpec as P

HEADS = 12
LANES = 128
NORM_EPS = 1e-06
ROOT_HALF = 0.7071067811865476
ROOT_TWO_PI = 2.5066282746310002
LOG2_E = 1.4426950408889634
F32 = jnp.float32
BF16 = jnp.bfloat16
VMEM_LIMIT = 60 * 2**20


def contract(a, b, da, db):
    return lax.dot_general(a, b, (((da,), (db,)), ((), ())), preferred_element_type=F32)


def call(kernel, *, grid, in_specs, out_specs, out_shape, scratch=(), prefetch=0, flops=0, moved=0, exps=0, share=1):
    return pl.pallas_call(
        kernel,
        grid_spec=pltpu.PrefetchScalarGridSpec(
            num_scalar_prefetch=prefetch,
            grid=grid,
            in_specs=in_specs,
            out_specs=out_specs,
            scratch_shapes=scratch,
        ),
        out_shape=out_shape,
        cost_estimate=pl.CostEstimate(
            flops=int(flops) // share, bytes_accessed=int(moved) // share, transcendentals=int(exps) // share
        ),
        compiler_params=pltpu.CompilerParams(vmem_limit_bytes=VMEM_LIMIT),
    )


def fixed(shape):
    return pl.BlockSpec(shape, lambda *_: (0,) * len(shape), pipeline_mode=pl.Buffered(1))


def shaped(shape, dtype):
    return jax.ShapeDtypeStruct(shape, dtype)


def norm_parts(values):
    centred = values - jnp.mean(values, -1, keepdims=True)
    spread = jnp.mean(centred * centred, -1, keepdims=True)
    inverse = lax.rsqrt(spread + NORM_EPS)
    return centred * inverse, inverse


def norm_backward(grad_norm, unit, inverse, gains):
    scaled = grad_norm * gains
    return inverse * (
        scaled
        - jnp.mean(scaled, -1, keepdims=True)
        - unit * jnp.mean(scaled * unit, -1, keepdims=True)
    )


def project_kernel(*refs, tm):
    blocks = refs[:tm]
    mask_ref, embed_ref, pos_ref, gain_ref, shift_ref, w_ref, bias_ref, filled_ref, turned_ref, joint_ref, normed_s = refs[tm:]

    @pl.when(pl.program_id(0) == 0)
    def _():
        seg = blocks[0].shape[0]
        embed, gain, shift = (r[...].astype(F32) for r in (embed_ref, gain_ref, shift_ref))
        for d in range(tm):
            rows = slice(d * seg, (d + 1) * seg)
            filled = jnp.where(mask_ref[rows] > 0.5, embed, blocks[d][...].astype(F32)) + pos_ref[rows].astype(F32)
            unit, _ = norm_parts(filled)
            normed = (unit * gain + shift).astype(BF16)
            filled_ref[rows] = filled
            normed_s[rows] = normed
            turned_ref[:, rows] = normed.T

    joint_ref[...] = (contract(normed_s[...], w_ref[...], 1, 0) + bias_ref[...].astype(F32)).astype(BF16)


def project(blocks, mask, embed, pos, gain, shift, w_qkv, bias):
    tm = len(blocks)
    seg, width = blocks[0].shape
    rows = tm * seg
    return call(
        functools.partial(project_kernel, tm=tm),
        grid=(3,),
        in_specs=[fixed((seg, width))] * tm
        + [fixed((rows, 1)), fixed((1, width)), fixed((rows, width)), fixed((1, width)), fixed((1, width))]
        + [pl.BlockSpec((width, width), lambda j: (0, j)), pl.BlockSpec((1, width), lambda j: (0, j))],
        out_specs=[
            pl.BlockSpec((rows, width), lambda j: (0, 0)),
            pl.BlockSpec((width, rows), lambda j: (0, 0)),
            pl.BlockSpec((rows, width), lambda j: (0, j)),
        ],
        out_shape=[shaped((rows, width), F32), shaped((width, rows), BF16), shaped((rows, 3 * width), BF16)],
        scratch=[pltpu.VMEM((rows, width), BF16)],
        flops=6 * rows * width * width,
        moved=20 * rows * width,
    )(*blocks, mask, embed, pos, gain, shift, w_qkv, bias)


def own_lanes(value, i, head):
    lane = lax.broadcasted_iota(jnp.int32, value.shape, 1)
    return jnp.where((lane >= i * head) & (lane < (i + 1) * head), value, jnp.zeros_like(value))


def attend_kernel(q_ref, k_ref, v_ref, o_ref, turned_ref, log_ref, *, head):
    factor = head**-0.5 * LOG2_E
    for pair in range(q_ref.shape[1] // LANES):
        lanes = slice(pair * LANES, (pair + 1) * LANES)
        q, k, v = q_ref[:, lanes], k_ref[:, lanes], v_ref[:, lanes]
        outs = []
        for i in range(LANES // head):
            scores = contract(k, own_lanes(q, i, head), 1, 1)
            peak = jnp.max(scores, 0, keepdims=True)
            raised = jnp.exp2((scores - peak) * factor)
            total = jnp.sum(raised, 0, keepdims=True)
            mixed = contract(v, raised.astype(BF16), 0, 0)
            outs.append(mixed[i * head : (i + 1) * head] * (1.0 / total))
            log_ref[pair, i : i + 1, :] = peak * factor + jnp.log2(total)
        turned = jnp.concatenate(outs, 0)
        turned_ref[lanes] = turned.astype(BF16)
        o_ref[:, lanes] = turned.T.astype(BF16)


def attend(joint, width):
    rows = joint.shape[0]
    head = width // HEADS
    pairs, per = width // LANES, LANES // head
    some = 2 if pairs % 2 == 0 else 1
    steps = pairs // some
    block = lambda off: pl.BlockSpec((rows, some * LANES), lambda h: (0, h + off))
    return call(
        functools.partial(attend_kernel, head=head),
        grid=(steps,),
        in_specs=[block(0), block(steps), block(2 * steps)],
        out_specs=[
            block(0),
            pl.BlockSpec((some * LANES, rows), lambda h: (h, 0)),
            pl.BlockSpec((some, per, rows), lambda h: (h, 0, 0)),
        ],
        out_shape=[shaped((rows, width), BF16), shaped((width, rows), BF16), shaped((pairs, per, rows), F32)],
        flops=16 * rows * rows * width,
        moved=8 * rows * width,
        exps=rows * rows * HEADS,
    )(joint, joint, joint)


def attend_back_kernel(side_ref, *refs, head, groups):
    per_clip = [refs[4 * c : 4 * c + 4] for c in range(groups)]
    g_ref, out_ref = refs[4 * groups :]
    scale = head**-0.5
    for c, (q_ref, k_ref, v_ref, log_ref) in enumerate(per_clip):
        rows = slice(c * q_ref.shape[0], (c + 1) * q_ref.shape[0])
        q, k, v, g = q_ref[...], k_ref[...], v_ref[...], g_ref[rows]
        grad_q, grad_k, grad_v = [], 0.0, 0.0
        for i in range(q.shape[1] // head):
            q_own, g_own = own_lanes(q, i, head), own_lanes(g, i, head)
            scores = contract(k, q_own, 1, 1)
            probs = jnp.exp2(scores * (scale * LOG2_E) - log_ref[0, i : i + 1, :])
            grad_probs = contract(v, g_own, 1, 1)
            delta = jnp.sum(probs * grad_probs, 0, keepdims=True)
            grad_scores = (probs * (grad_probs - delta)).astype(BF16)
            grad_q.append(contract(k, grad_scores, 0, 0)[i * head : (i + 1) * head])
            grad_k = grad_k + contract(grad_scores, q_own, 1, 0)
            grad_v = grad_v + contract(probs.astype(BF16), g_own, 1, 0)
        out_ref[0, rows] = (jnp.concatenate(grad_q, 0) * scale).T.astype(BF16)
        out_ref[1, rows] = (grad_k * scale).astype(BF16)
        out_ref[2, rows] = grad_v.astype(BF16)


def attend_back(side, joints, mix, logs):
    rows, width = mix.shape
    groups = len(joints)
    length = rows // groups
    head = width // HEADS
    pairs, per = width // LANES, LANES // head
    half = pairs // 2

    def block(off):
        return pl.BlockSpec((length, LANES), lambda h, s: (0, off + s[0] * half + h))

    clip = [block(0), block(pairs), block(2 * pairs), pl.BlockSpec((1, per, length), lambda h, s: (s[0] * half + h, 0, 0))]
    operands = []
    for joint, log_sum in zip(joints, logs):
        operands += [joint, joint, joint, log_sum]
    return call(
        functools.partial(attend_back_kernel, head=head, groups=groups),
        prefetch=1,
        share=4096,
        grid=(half,),
        in_specs=clip * groups + [pl.BlockSpec((rows, LANES), lambda h, s: (0, s[0] * half + h))],
        out_specs=pl.BlockSpec((3, rows, LANES), lambda h, s: (0, 0, h)),
        out_shape=shaped((3, rows, width // 2), BF16),
        flops=20 * rows * length * width,
        moved=8 * rows * width,
        exps=rows * length * HEADS // 2,
    )(side, *operands, mix)


def gelu_parts(u):
    phi = 0.5 * (1.0 + lax.erf(u * ROOT_HALF))
    return u * phi, phi + u * jnp.exp(-0.5 * u * u) * (1.0 / ROOT_TWO_PI)


def forward_kernel(*refs, groups, chunk):
    filled, attended = refs[:groups], refs[groups : 2 * groups]
    (w_out_ref, out_bias_ref, gain_ref, shift_ref, down_bias_ref, w_up_ref, up_bias_ref, w_down_ref,
     hidden_ref, turned_ref, act_ref, slope_ref, block_ref, out_s, normed_s) = refs[2 * groups :]
    rows_all = out_s.shape[0]
    step, last = pl.program_id(0), pl.num_programs(0) - 1

    @pl.when(step == 0)
    def _():
        gain, shift = gain_ref[...].astype(F32), shift_ref[...].astype(F32)
        out_bias, down_bias = out_bias_ref[...].astype(F32), down_bias_ref[...].astype(F32)
        length = filled[0].shape[0]
        for c in range(groups):
            rows = slice(c * length, (c + 1) * length)
            hidden = filled[c][...] + contract(attended[c][...], w_out_ref[...], 1, 0) + out_bias
            unit, _ = norm_parts(hidden)
            normed = (unit * gain + shift).astype(BF16)
            hidden_ref[rows] = hidden
            normed_s[rows] = normed
            turned_ref[:, rows] = normed.T
            out_s[rows] = hidden + down_bias

    w_up, w_down = w_up_ref[...], w_down_ref[...]
    bias = up_bias_ref[...].astype(F32)
    for r in range(rows_all // chunk):
        rows = slice(r * chunk, (r + 1) * chunk)
        value, slope = gelu_parts(contract(normed_s[rows], w_up, 1, 0) + bias)
        act = value.astype(BF16)
        act_ref[:, rows] = act.T
        slope_ref[rows] = slope.astype(BF16)
        out_s[rows] += contract(act, w_down, 1, 0)

    @pl.when(step == last)
    def _():
        block_ref[...] = out_s[...].astype(BF16)


def forward(filled, attended, w_out, out_bias, gain, shift, down_bias, w_up, up_bias, w_down, tile, chunk):
    groups, (length, width) = len(filled), filled[0].shape
    rows, ff = groups * length, w_up.shape[1]
    vec = fixed((1, width))
    whole = pl.BlockSpec((rows, width), lambda j: (0, 0), pipeline_mode=pl.Buffered(1))
    column = pl.BlockSpec((rows, tile), lambda j: (0, j))
    return call(
        functools.partial(forward_kernel, groups=groups, chunk=chunk),
        grid=(ff // tile,),
        in_specs=[fixed((length, width))] * (2 * groups)
        + [fixed((width, width)), vec, vec, vec, vec]
        + [
            pl.BlockSpec((width, tile), lambda j: (0, j)),
            pl.BlockSpec((1, tile), lambda j: (0, j)),
            pl.BlockSpec((tile, width), lambda j: (j, 0)),
        ],
        out_specs=[whole, fixed((width, rows)), pl.BlockSpec((tile, rows), lambda j: (j, 0)), column, whole],
        out_shape=[shaped((rows, width), F32), shaped((width, rows), BF16)]
        + [shaped((ff, rows), BF16), shaped((rows, ff), BF16)]
        + [shaped((rows, width), BF16)],
        scratch=[pltpu.VMEM((rows, width), F32), pltpu.VMEM((rows, width), BF16)],
        flops=4 * rows * width * ff + 2 * rows * width * width,
        moved=14 * rows * width + 4 * rows * ff + 4 * width * ff,
        exps=rows * ff,
    )(*filled, *attended, w_out, out_bias, gain, shift, down_bias, w_up, up_bias, w_down)


def tile_back(turned_ref, cot_ref, act_ref, slope_ref, w_up_ref, w_down_ref, gup_s, norm_s, down_ref, up_ref, bias_ref, chunk):
    w_up, w_down = w_up_ref[...], w_down_ref[...]
    total = jnp.zeros(bias_ref.shape, F32)
    for r in range(cot_ref.shape[0] // chunk):
        rows = slice(r * chunk, (r + 1) * chunk)
        gup = (contract(cot_ref[rows], w_down, 1, 1) * slope_ref[rows].astype(F32)).astype(BF16)
        gup_s[rows] = gup
        total = total + jnp.sum(gup.astype(F32), 0, keepdims=True)
        norm_s[rows] += contract(gup, w_up, 1, 1)
    bias_ref[...] = total
    down_ref[...] = contract(act_ref[...], cot_ref[...], 1, 0).astype(BF16)
    up_ref[...] = contract(turned_ref[...], gup_s[...], 1, 0).astype(BF16)


def back_first_kernel(side_ref, turned_ref, cot_ref, act_ref, slope_ref, w_up_ref, w_down_ref, norm_ref, down_ref, up_ref, bias_ref, gup_s, *, chunk):
    @pl.when(pl.program_id(0) == 0)
    def _():
        norm_ref[...] = jnp.zeros_like(norm_ref)

    tile_back(turned_ref, cot_ref, act_ref, slope_ref, w_up_ref, w_down_ref, gup_s, norm_ref, down_ref, up_ref, bias_ref, chunk)


def back_last_kernel(side_ref, *refs, groups, chunk):
    attended = refs[:groups]
    (turned_ref, cot_ref, act_ref, slope_ref, w_up_ref, w_down_ref, w_out_ref, gain_ref, hidden_ref, norm_ref,
     down_ref, up_ref, bias_ref, grad_hidden_ref, mix_ref, grad_out_ref, sums_ref, gup_s, norm_s, branch_s) = refs[groups:]

    @pl.when(pl.program_id(0) == 0)
    def _():
        norm_s[...] = norm_ref[...]

    tile_back(turned_ref, cot_ref, act_ref, slope_ref, w_up_ref, w_down_ref, gup_s, norm_s, down_ref, up_ref, bias_ref, chunk)

    @pl.when(pl.program_id(0) == pl.num_programs(0) - 1)
    def _():
        gain = gain_ref[...].astype(F32)
        total = [jnp.zeros_like(gain) for _ in range(4)]
        w_out = w_out_ref[...]
        for r in range(norm_s.shape[0] // chunk):
            rows = slice(r * chunk, (r + 1) * chunk)
            unit, inverse = norm_parts(hidden_ref[rows])
            top, grad_norm = cot_ref[rows].astype(F32), norm_s[rows]
            grad_hidden = top + norm_backward(grad_norm, unit, inverse, gain)
            grad_hidden_ref[rows] = grad_hidden
            branch = grad_hidden.astype(BF16)
            branch_s[rows] = branch
            mix_ref[rows] = contract(branch, w_out, 1, 1).astype(BF16)
            parts = (branch.astype(F32), top, grad_norm * unit, grad_norm)
            total = [t + jnp.sum(p, 0, keepdims=True) for t, p in zip(total, parts)]
        sums_ref[...] = jnp.concatenate(total + [jnp.zeros_like(gain)] * 4, 0)
        length = attended[0].shape[1]
        grad_out = 0.0
        for c in range(groups):
            grad_out = grad_out + contract(attended[c][...], branch_s[c * length : (c + 1) * length], 1, 0)
        grad_out_ref[...] = grad_out.astype(BF16)


def back_specs(rows, width, half, tile):
    steps = half // tile
    column = lambda n: pl.BlockSpec((n, tile), lambda j, s: (0, s[0] * steps + j))
    ins = [fixed((width, rows)), fixed((rows, width))]
    ins += [pl.BlockSpec((tile, rows), lambda j, s: (s[0] * steps + j, 0)), column(rows), column(width)]
    ins.append(pl.BlockSpec((tile, width), lambda j, s: (s[0] * steps + j, 0)))
    outs = [
        pl.BlockSpec((tile, width), lambda j, s: (j, 0)),
        pl.BlockSpec((width, tile), lambda j, s: (0, j)),
        pl.BlockSpec((1, tile), lambda j, s: (0, j)),
    ]
    return ins, outs, [shaped((half, width), BF16), shaped((width, half), BF16), shaped((1, half), F32)]


def back_first(side, normed, cot, act, slope, w_up, w_down, tile, chunk):
    rows, width = cot.shape
    half = w_up.shape[1] // 2
    ins, outs, shapes = back_specs(rows, width, half, tile)
    return call(
        functools.partial(back_first_kernel, chunk=chunk),
        prefetch=1,
        grid=(half // tile,),
        in_specs=ins,
        out_specs=[fixed((rows, width))] + outs,
        out_shape=[shaped((rows, width), F32)] + shapes,
        scratch=[pltpu.VMEM((rows, tile), BF16)],
        flops=8 * rows * width * half,
        moved=8 * rows * width + 4 * rows * half + 8 * width * half,
    )(side, normed, cot, act, slope, w_up, w_down)


def back_last(side, attended, normed, cot, act, slope, w_up, w_down, w_out, gain, hidden, norm, tile, chunk):
    rows, width = cot.shape
    groups = len(attended)
    half = w_up.shape[1] // 2
    ins, outs, shapes = back_specs(rows, width, half, tile)
    whole = lambda n: fixed((n, width))
    return call(
        functools.partial(back_last_kernel, groups=groups, chunk=chunk),
        prefetch=1,
        grid=(half // tile,),
        in_specs=[fixed((width, rows // groups))] * groups + ins + [whole(width), whole(1), whole(rows), whole(rows)],
        out_specs=outs + [whole(rows), whole(rows), whole(width), whole(8)],
        out_shape=shapes
        + [shaped((rows, width), F32), shaped((rows, width), BF16), shaped((width, width), BF16), shaped((8, width), F32)],
        scratch=[pltpu.VMEM((rows, tile), BF16), pltpu.VMEM((rows, width), F32), pltpu.VMEM((rows, width), BF16)],
        flops=8 * rows * width * half + 4 * rows * width * width,
        moved=20 * rows * width + 4 * rows * half + 8 * width * half,
    )(side, *attended, normed, cot, act, slope, w_up, w_down, w_out, gain, hidden, norm)


def joint_part(normed, grad_ref, grad_w_ref, bias_ref):
    length = normed[0].shape[1]
    grad_w = 0.0
    for c, normed_ref in enumerate(normed):
        grad_w = grad_w + contract(normed_ref[...], grad_ref[0, c * length : (c + 1) * length], 1, 0)
    grad_w_ref[...] = grad_w.astype(BF16)
    bias_ref[0] = jnp.sum(grad_ref[0].astype(F32), 0, keepdims=True)


def joint_first_kernel(side_ref, *refs, groups):
    normed, (grad_ref, weight_ref, grad_w_ref, bias_ref, acc_ref) = refs[:groups], refs[groups:]
    joint_part(normed, grad_ref, grad_w_ref, bias_ref)
    part = contract(grad_ref[0], weight_ref[...], 1, 1)

    @pl.when(pl.program_id(0) == 0)
    def _():
        acc_ref[...] = part

    @pl.when(pl.program_id(0) > 0)
    def _():
        acc_ref[...] += part


def joint_last_kernel(side_ref, *refs, groups, chunk, tm):
    normed, (grad_ref, weight_ref, acc_ref, grad_hidden_ref, gain_ref) = refs[:groups], refs[groups : groups + 5]
    refs = refs[groups + 5 :]
    filled, masks = refs[:groups], refs[groups : 2 * groups]
    (other_bias_ref, sums_ref, up_other_ref, up_own_ref, grad_w_ref, input_ref, rest_ref,
     acc_s, pos_s, bias_s) = refs[2 * groups :]
    core, me = side_ref[0], side_ref[1]
    length, half = normed[0].shape[1], grad_w_ref.shape[1]
    step = pl.program_id(0)
    joint_part(normed, grad_ref, grad_w_ref, bias_s.at[pl.ds(step, 1)])

    @pl.when(step == 0)
    def _():
        acc_s[...] = acc_ref[...] + contract(grad_ref[0], weight_ref[...], 1, 1)

    @pl.when(step == 1)
    def _():
        acc_s[...] += contract(grad_ref[0], weight_ref[...], 1, 1)

    @pl.when(step == 2)
    def _():
        gain = gain_ref[...].astype(F32)
        weight = weight_ref[...]
        total = [jnp.zeros_like(gain) for _ in range(3)]
        for c in range(groups):
            for r in range(length // chunk):
                clip = slice(r * chunk, (r + 1) * chunk)
                rows = slice(c * length + r * chunk, c * length + (r + 1) * chunk)
                grad_norm = acc_s[rows] + contract(grad_ref[0, rows], weight, 1, 1)
                unit, inverse = norm_parts(filled[c][clip])
                grad_filled = grad_hidden_ref[rows] + norm_backward(grad_norm, unit, inverse, gain)
                masked = masks[c][clip] > 0.5
                input_ref[rows] = jnp.where(masked, 0.0, grad_filled).astype(BF16)
                parts = (grad_norm * unit, grad_norm, jnp.where(masked, grad_filled, 0.0))
                total = [t + jnp.sum(p, 0, keepdims=True) for t, p in zip(total, parts)]
                pos_s[clip] = grad_filled if c == 0 else pos_s[clip] + grad_filled
        seg = length // tm
        shares, share_rows, _ = rest_ref.shape
        pos_rows, some = length // shares, shares // tm
        for d in range(tm):
            own = pos_s[d * seg : (d + 1) * seg].reshape(some, pos_rows, pos_s.shape[1])
            rest_ref[pl.ds((me ^ d) * some, some), :pos_rows] = own.astype(BF16)

        def both(other, mine):
            return jnp.where(core == 0, jnp.concatenate([mine, other], 1), jnp.concatenate([other, mine], 1))

        width = gain.shape[1]
        up = both(up_other_ref[...], up_own_ref[...])
        sums = sums_ref[...]
        lines = [both(other_bias_ref[i], bias_s[i]) for i in (0, 2)] + [sums[0:1]]
        lines += [up[:, i * width : (i + 1) * width] for i in range(up.shape[1] // width)]
        lines += [sums[1:2], total[0], total[1], sums[2:3], sums[3:4], total[2]]
        lines.append(jnp.zeros((shares * (share_rows - pos_rows) - len(lines), width), F32))
        small = jnp.concatenate(lines, 0).reshape(shares, share_rows - pos_rows, width)
        rest_ref[:, pos_rows:] = small.astype(BF16)


def joint_specs(groups, rows, width):
    half = width // 2
    return [fixed((width, rows // groups))] * groups + [
        pl.BlockSpec((1, rows, half), lambda i, s: (i, 0, 0)),
        pl.BlockSpec((width, half), lambda i, s: (0, 2 * i + s[0])),
    ]


def joint_first(side, normed, grads, w_qkv):
    _, rows, half = grads.shape
    groups, width = len(normed), 2 * half
    return call(
        functools.partial(joint_first_kernel, groups=groups),
        prefetch=1,
        share=4096,
        grid=(3,),
        in_specs=joint_specs(groups, rows, width),
        out_specs=[
            pl.BlockSpec((width, half), lambda i, s: (0, i)),
            pl.BlockSpec((1, 1, half), lambda i, s: (i, 0, 0)),
            fixed((rows, width)),
        ],
        out_shape=[shaped((width, 3 * half), BF16), shaped((3, 1, half), F32), shaped((rows, width), F32)],
        flops=6 * rows * width * width,
        moved=12 * rows * width,
    )(side, *normed, grads, w_qkv)


def joint_last(side, normed, grads, w_qkv, acc, grad_hidden, gain, filled, masks, bias, sums, up_other, up_own, tm, chunk, shares):
    _, rows, half = grads.shape
    groups, width = len(normed), 2 * half
    length = rows // groups
    return call(
        functools.partial(joint_last_kernel, groups=groups, chunk=chunk, tm=tm),
        prefetch=1,
        share=4096,
        grid=(3,),
        in_specs=joint_specs(groups, rows, width)
        + [fixed((rows, width))] * 2
        + [fixed((1, width))]
        + [fixed((length, width))] * groups
        + [fixed((length, 1))] * groups
        + [fixed((3, 1, half)), fixed((8, width)), fixed(up_other.shape), fixed(up_own.shape)],
        out_specs=[
            pl.BlockSpec((width, half), lambda i, s: (0, i)),
            fixed((rows, width)),
            fixed((shares, width // shares, width)),
        ],
        out_shape=[
            shaped((width, 3 * half), BF16),
            shaped((rows, width), BF16),
            shaped((shares, width // shares, width), BF16),
        ],
        scratch=[
            pltpu.VMEM((rows, width), F32),
            pltpu.VMEM((length, width), F32),
            pltpu.VMEM((3, 1, half), F32),
        ],
        flops=6 * rows * width * width,
        moved=24 * rows * width,
    )(side, *normed, grads, w_qkv, acc, grad_hidden, gain, *filled, *masks, bias, sums, up_other, up_own)


def cores_in_order(here_ref, own_ref, other_ref):
    low = here_ref[1] == 0
    own, other = own_ref[0], other_ref[0]
    return [jnp.where(low, own, other).astype(F32), jnp.where(low, other, own).astype(F32)]


def place_one_kernel(here_ref, down_own_ref, up_own_ref, down_other_ref, up_other_ref, down_ref, up_ref):
    width = down_ref.shape[2]
    for core, share in enumerate(cores_in_order(here_ref, down_own_ref, down_other_ref)):
        for part in range(share.shape[1] // width):
            down_ref[core, part * share.shape[0] : (part + 1) * share.shape[0]] = share[:, part * width : (part + 1) * width]
    for core, share in enumerate(cores_in_order(here_ref, up_own_ref, up_other_ref)):
        up_ref[:, core * share.shape[1] : (core + 1) * share.shape[1]] = share


def place_two_kernel(here_ref, qkv_own_ref, own_ref, qkv_other_ref, other_ref, qkv_ref, out_ref, pos_ref, small_ref):
    width = out_ref.shape[1]
    half = width // 2
    for core, share in enumerate(cores_in_order(here_ref, qkv_own_ref, qkv_other_ref)):
        for i in range(3):
            qkv_ref[:, i * width + core * half : i * width + (core + 1) * half] = share[:, i * half : (i + 1) * half]
    out_ref[...], rest = cores_in_order(here_ref, own_ref, other_ref)
    pos_ref[...], small_ref[...] = rest[: pos_ref.shape[0]], rest[pos_ref.shape[0] :]


def spot_bits(order, tm):
    return [bits_of(bit) if axis == "tm" else bits_of(tm) + bits_of(bit) - 1 for axis, bit in order]


def place(kernel, here, gathered, orders, tm, shapes):
    steps = gathered[0].shape[0]

    def share(value, order):
        bits = spot_bits(order, tm)

        def index(j, here):
            away = j ^ here[0]
            return sum(((away >> b) & 1) << k for k, b in enumerate(bits)), 0, 0

        return pl.BlockSpec((1,) + value.shape[1:], index)

    def cut(shape):
        block = shape[:-2] + (shape[-2] // steps, shape[-1])
        return pl.BlockSpec(block, lambda j, here: (0,) * (len(shape) - 2) + (j, 0))

    return call(
        kernel,
        prefetch=1,
        grid=(steps,),
        in_specs=[share(v, o) for v, o in zip(gathered, orders * 2)],
        out_specs=[cut(s) for s in shapes],
        out_shape=[shaped(s, F32) for s in shapes],
        moved=sum(6 * v.size for v in gathered),
    )(here, *gathered)


def in_order(here, gathered, orders, tm):
    out = []
    half = len(gathered) // 2
    for own, other, order in zip(gathered[:half], gathered[half:], orders):
        bits = spot_bits(order, tm)
        away = jnp.arange(own.shape[0], dtype=jnp.int32) ^ here[0]
        index = sum(((away >> b) & 1) << k for k, b in enumerate(bits))
        own, other = (jnp.take(x, index, axis=0).astype(F32) for x in (own, other))
        low = here[1] == 0
        out.append(jnp.stack([jnp.where(low, own, other), jnp.where(low, other, own)]))
    return out


def bits_of(size):
    return size.bit_length() - 1


def axis_bits(axis):
    return [(axis, 1 << b) for b in range(bits_of(lax.axis_size(axis)))]


def own_bit(axis, bit):
    return (lax.axis_index(axis) // bit) % 2


def hop(value, axis, bit):
    size = lax.axis_size(axis)
    return lax.ppermute(value, axis, [(i, i ^ bit) for i in range(size)])


def tie(*values):
    return lax.optimization_barrier(values)


def take_clips(values):
    tm = lax.axis_size("tm")
    me = lax.axis_index("tm")
    out = []
    for d in range(tm):
        block = lax.dynamic_index_in_dim(values, me ^ d, 1, keepdims=False)
        out.append(hop(block, "tm", d) if d else block)
    return out


def send_clips(values):
    blocks = jnp.split(values, lax.axis_size("tm"), 1)
    return [hop(block, "tm", d) if d else block for d, block in enumerate(blocks)]


def all_clips(blocks, shape):
    return jnp.stack(unshuffle(blocks), 1).reshape(shape)


def unshuffle(blocks):
    me = lax.axis_index("tm")
    blocks = list(blocks)
    for b in range(bits_of(len(blocks))):
        odd = ((me >> b) & 1) == 1
        blocks = [jnp.where(odd, blocks[i ^ (1 << b)], blocks[i]) for i in range(len(blocks))]
    return blocks


def add_low(a, b):
    return (a.astype(F32) + b.astype(F32)).astype(BF16)


def split_share(value):
    count = bits_of(lax.axis_size("clips")) + bits_of(lax.axis_size("tm")) - 1
    return value.reshape((2,) * count + (value.shape[0] >> count, value.shape[1]))


def side_by_side(value, parts):
    return jnp.concatenate(jnp.split(value, parts, -2), -1)


class Sum:
    def __init__(self, folds):
        self.folds = folds
        clip_bits, self.time_bits = axis_bits("clips")[1:], axis_bits("tm")
        self.names = clip_bits[::-1] + self.time_bits[::-1]
        self.orders = (clip_bits, clip_bits[1:] + clip_bits[:1])
        self.rounds = len(clip_bits) + len(self.time_bits)

    def half(self, pair, names, name, other):
        at = names.index(name)
        mine = own_bit(*name)
        pick = lambda x: lax.dynamic_index_in_dim(x, 1 - mine if other else mine, at, keepdims=False)
        return add_low(*(pick(x) for x in pair))

    def half_of_all(self, index, state, other):
        sides = len(self.orders[0])
        if index < sides:
            names = [[n for n in self.names if n not in order[:index]] for order in self.orders]
            return [self.half(p, n, order[index], other) for p, n, order in zip(state, names, self.orders)]
        names = self.time_bits[index - sides :]
        parts = [self.half(pair, names[::-1], names[0], other) for pair in state]
        if len(parts) > 1:
            parts = [side_by_side(x, n) if n > 1 else x for x, n in zip(parts, self.folds)]
        return [jnp.concatenate(parts, -1) if len(parts) > 1 else parts[0]]

    def split(self, index, state):
        return [(away,) for away in self.half_of_all(index, state, True)] + state

    def send(self, index, state):
        sides = len(self.orders[0])
        names = [o[index] for o in self.orders] if index < sides else [self.time_bits[index - sides]]
        away, state = state[: len(names)], state[len(names) :]
        got = [hop(x, *name) for (x,), name in zip(away, names)]
        return list(zip(self.half_of_all(index, state, False), got))

    def scatter(self, index, state):
        return self.send(index, self.split(index, state))

    def share(self, state):
        return add_low(*state[0])

    def gather_orders(self):
        return [self.time_bits[::-1] + order[::-1] for order in self.orders]

    def gather(self, index, state, cut):
        if index < len(self.time_bits):
            return [(state[0], hop(state[0], *self.time_bits[::-1][index]))]
        names = [order[::-1][index - len(self.time_bits)] for order in self.orders]
        return [(value, hop(value, *name)) for value, name in zip(state, names)]

    def join(self, index, state, cut):
        out = [jnp.concatenate(pair, 0) for pair in state]
        if index == len(self.time_bits) - 1:
            return [out[0][..., :cut], out[0][..., cut:]]
        return out


def on_device(
    patches, mask_index, mask_count, w_qkv, q_bias, v_bias, w_out, out_bias, w_up, up_bias,
    w_down, down_bias, norm1_scale, norm1_shift, norm2_scale, norm2_shift, mask_embed, pos_embed,
    cotangent,
):
    clip_count, seg, width = patches.shape
    ff = w_up.shape[1]
    tm = lax.axis_size("tm")
    me = lax.axis_index("tm")
    length = seg * tm
    groups = clip_count // tm
    by_group = (groups, tm, seg, width)
    tile, chunk = 512, 512

    arrived, grouped = [], patches.reshape(by_group)
    for g in range(groups):
        arrived.append(take_clips(grouped[g : g + 1]))
        grouped, *arrived[g] = tie(grouped, *arrived[g])
    tied, *arrived[-1] = tie(cotangent, *arrived[-1])
    cot = take_clips(tied.reshape(by_group))
    arrived = [[b[0] for b in blocks] for blocks in arrived]

    row = lambda x: x.reshape(1, -1)
    joint_bias = row(jnp.concatenate([q_bias, jnp.zeros_like(q_bias), v_bias]))
    out_bias, up_bias, down_bias, gain1, shift1, gain2, shift2, embed = map(
        row, (out_bias, up_bias, down_bias, norm1_scale, norm1_shift, norm2_scale, norm2_shift, mask_embed)
    )
    starts = (me ^ jnp.arange(tm, dtype=jnp.int32)) * seg
    places = (starts[:, None] + jnp.arange(seg, dtype=jnp.int32)[None, :]).reshape(length)
    pos = jnp.concatenate([lax.dynamic_slice_in_dim(pos_embed, (me ^ d) * seg, seg, 0) for d in range(tm)], 0)
    slots = jnp.arange(mask_index.shape[1], dtype=jnp.int32)
    masks = []
    for g in range(groups):
        index_row = lax.dynamic_index_in_dim(mask_index, g * tm + me, 0, keepdims=False)
        count = lax.dynamic_index_in_dim(mask_count, g * tm + me, 0, keepdims=False)
        hit = (places[:, None] == index_row[None, :]) & (slots < count)[None, :]
        masks.append(jnp.any(hit, axis=1, keepdims=True).astype(F32))

    filled, normed_one, joints, attended, turned, logs = [], [], [], [], [], []
    for g in range(groups):
        f, n, j = project(arrived[g], masks[g], embed, pos, gain1, shift1, w_qkv, joint_bias)
        a, a_turned, log_sum = attend(j, width)
        if g < groups - 1:
            a, *arrived[g + 1] = tie(a, *arrived[g + 1])
        else:
            a, cot[1] = tie(a, cot[1])
        for kept, value in zip((filled, normed_one, joints, attended, turned, logs), (f, n, j, a, a_turned, log_sum)):
            kept.append(value)

    core = own_bit("clips", 1).astype(jnp.int32)
    kept_side = jnp.stack([core, me.astype(jnp.int32)])
    away_side = jnp.stack([1 - core, me.astype(jnp.int32)])
    shares = lax.axis_size("clips") // 2 * tm
    here = jnp.stack([(lax.axis_index("clips") // 2 * tm + me).astype(jnp.int32), core])
    hidden, normed_two, act, slope, block_out = forward(
        filled, attended, w_out, out_bias, gain2, shift2, down_bias, w_up, up_bias, w_down, 768, length * groups
    )
    block_out, *cot = tie(block_out, *cot)
    cot = jnp.concatenate(cot, 1).reshape(groups * length, width)
    norm_acc, down, up, up_sums_away = back_first(away_side, normed_two, cot, act, slope, w_up, w_down, tile, chunk)
    down_got, up_got = hop(down, "clips", 1), hop(up, "clips", 1)
    down, up, up_sums, grad_hidden, mix, grad_out, sums_two = back_last(
        kept_side, turned, normed_two, cot, act, slope, w_up, w_down, w_out, gain2, hidden, norm_acc, tile, chunk
    )
    one = Sum((2, 1))

    def after(values, *states):
        flat = [x for state in states for pair in state for x in pair]
        tied = list(tie(*values, *flat))
        values, flat = tied[: len(values)], tied[len(values) :]
        back = [[tuple(flat.pop(0) for _ in pair) for pair in state] for state in states]
        return (values, *back)

    state = [tuple(split_share(x) for x in pair) for pair in ((down, down_got), (up, up_got))]
    state = one.split(0, state)
    (mix, block_out), state = after((mix, block_out), state)
    state = one.send(0, state)
    block_out = send_clips(block_out.reshape(groups, length, width))
    grads = attend_back(away_side, joints, mix, logs)
    qkv, bias_sums, acc = joint_first(away_side, normed_one, grads, w_qkv)
    qkv_got = hop(qkv, "clips", 1)
    sent_out = block_out
    (acc, sent_out[1], sent_out[2]), state = after((acc, sent_out[1], sent_out[2]), state)
    state = one.split(1, state)
    (mix, acc), state = after((mix, acc), state)
    state = one.send(1, state)
    grads = attend_back(kept_side, joints, mix, logs)
    (grads, *rest_out), state = after((grads, *sent_out[3:]), state)
    sent_out[3:] = rest_out
    state = one.split(2, state)
    (grads,), state = after((grads,), state)
    state = one.send(2, state)
    qkv, input_grad, rest = joint_last(
        kept_side, normed_one, grads, w_qkv, acc, grad_hidden, gain1, filled, masks, bias_sums, sums_two,
        up_sums_away, up_sums, tm, chunk, shares
    )
    rest = rest.reshape(width, width)
    (qkv, input_grad, rest), state = after((qkv, input_grad, rest), state)
    rest_away = jnp.where(core == 1, grad_out, rest)
    rest_kept = jnp.where(core == 1, rest, grad_out)
    rest_got = hop(rest_away, "clips", 1)
    two = Sum((1, 1))
    pairs = [tuple(split_share(x) for x in pair) for pair in ((qkv, qkv_got), (rest_kept, rest_got))]
    cut_one, cut_two = ff // 2, 3 * width // 2
    share_rows = pairs[0][0].shape[-2]

    def scatter_steps(group, first):
        steps = [lambda s, i=i: group.split(i, s) for i in range(first, group.rounds)]
        return [(split, lambda s, i=i: group.send(i, s)) for i, split in zip(range(first, group.rounds), steps)]

    def gather_steps(group, cut):
        def prepare(i):
            if i == 0:
                return lambda s: [(group.share(s)[None],)]
            return lambda s: [(x,) for x in group.join(i - 1, s, cut)]

        return [
            (prepare(i), lambda s, i=i: group.gather(i, [x for (x,) in s], cut)) for i in range(group.rounds)
        ]

    def core_steps(group, cut):
        return [
            (
                lambda s: [(x,) for x in group.join(group.rounds - 1, s, cut)],
                lambda s: [(x, hop(x, "clips", 1)) for (x,) in s],
            )
        ]

    steps_one = scatter_steps(one, 3) + gather_steps(one, cut_one) + core_steps(one, cut_one)
    steps_two = scatter_steps(two, 0) + gather_steps(two, cut_two) + core_steps(two, cut_two)
    outputs = []
    for index in range(max(len(steps_one), len(steps_two))):
        if index == 2:
            block_out = all_clips(sent_out, patches.shape)
            (block_out,), state, pairs = after((block_out,), state, pairs)
        if index == len(steps_two) - 1:
            tied, pairs = after((*sent[3:], *outputs), pairs)
            sent[3:], outputs = tied[: len(sent) - 3], tied[len(sent) - 3 :]
        active = [steps[index] if index < len(steps) else None for steps in (steps_one, steps_two)]
        states = [step[0](x) if step else x for step, x in zip(active, (state, pairs))]
        live = [x for x, step in zip(states, active) if step]
        if index == 3:
            (input_grad,), *live = after((input_grad,), *live)
            sent = send_clips(input_grad.reshape(groups, length, width))
        elif index in (4, 5):
            sent[index - 3 : index - 2], *live = after(sent[index - 3 : index - 2], *live)
        else:
            _, *live = after((), *live)
        live = iter(live)
        state, pairs = (step[1](next(live)) if step else x for step, x in zip(active, states))
        if index == len(steps_one) - 1:
            one_all = [own for own, _ in state] + [other for _, other in state]
            if share_rows % 8 == 0:
                outputs = place(
                    place_one_kernel, here, one_all, one.gather_orders(), tm, ((2, ff // 2, width), (width, ff))
                )
    two_all = [own for own, _ in pairs] + [other for _, other in pairs]
    input_grad = all_clips(sent, patches.shape)

    orders_one, orders_two = one.gather_orders(), two.gather_orders()
    if share_rows % 8 == 0:
        down_sum, up_sum = outputs
        shapes = ((width, 3 * width), (width, width), (length, width), (width - length, width))
        qkv_sum, out_sum, pos_sum, small = place(place_two_kernel, here, two_all, orders_two, tm, shapes)
        down_sum = down_sum.reshape(ff, width)
    else:
        downs, ups = in_order(here, one_all, orders_one, tm)
        qkvs, rests = in_order(here, two_all, orders_two, tm)
        down_sum = jnp.stack(jnp.split(downs, 2, -1), 2).reshape(ff, width)
        up_sum = jnp.concatenate(list(ups.reshape(2, width, ff // 2)), 1)
        qkv_sum = jnp.stack(list(qkvs.reshape(2, width, 3, width // 2)), 2).reshape(width, 3 * width)
        out_sum, rest = rests[0].reshape(width, width), rests[1]
        pos_sum = rest[:, : length // shares].reshape(length, width)
        small = rest[:, length // shares :].reshape(width - length, width)
    v = []
    at = 0
    for n in (1, 1, 1, ff // width, 1, 1, 1, 1, 1, 1):
        v.append(small[at : at + n].reshape(-1))
        at += n
    return (block_out, input_grad, qkv_sum, v[0], v[1], out_sum, v[2], up_sum, v[3], down_sum, v[4],
            v[5], v[6], v[7], v[8], v[9], pos_sum)


def solution(mesh):
    rows = P("clips", "tm", None)
    in_specs = (rows, P("clips", None), P("clips")) + (P(),) * 15 + (rows,)
    out_specs = (rows, rows) + (P(),) * 15
    return jax.shard_map(on_device, mesh=mesh, in_specs=in_specs, out_specs=out_specs, check_vma=False)
```

```python
import functools

import jax
import jax.numpy as jnp
from jax import lax
from jax.experimental import pallas as pl
from jax.experimental.pallas import tpu as pltpu
from jax.sharding import PartitionSpec as P

HEADS = 12
LANES = 128
NORM_EPS = 1e-06
ROOT_HALF = 0.7071067811865476
ROOT_TWO_PI = 2.5066282746310002
LOG2_E = 1.4426950408889634
F32 = jnp.float32
BF16 = jnp.bfloat16
VMEM_LIMIT = 60 * 2**20


def contract(a, b, da, db):
    return lax.dot_general(a, b, (((da,), (db,)), ((), ())), preferred_element_type=F32)


def call(kernel, *, grid, in_specs, out_specs, out_shape, scratch=(), prefetch=0, flops=0, moved=0, exps=0, share=1):
    return pl.pallas_call(
        kernel,
        grid_spec=pltpu.PrefetchScalarGridSpec(
            num_scalar_prefetch=prefetch,
            grid=grid,
            in_specs=in_specs,
            out_specs=out_specs,
            scratch_shapes=scratch,
        ),
        out_shape=out_shape,
        cost_estimate=pl.CostEstimate(
            flops=int(flops) // share, bytes_accessed=int(moved) // share, transcendentals=int(exps) // share
        ),
        compiler_params=pltpu.CompilerParams(vmem_limit_bytes=VMEM_LIMIT),
    )


def fixed(shape):
    return pl.BlockSpec(shape, lambda *_: (0,) * len(shape), pipeline_mode=pl.Buffered(1))


def shaped(shape, dtype):
    return jax.ShapeDtypeStruct(shape, dtype)


def norm_parts(values):
    centred = values - jnp.mean(values, -1, keepdims=True)
    spread = jnp.mean(centred * centred, -1, keepdims=True)
    inverse = lax.rsqrt(spread + NORM_EPS)
    return centred * inverse, inverse


def norm_backward(grad_norm, unit, inverse, gains):
    scaled = grad_norm * gains
    return inverse * (
        scaled
        - jnp.mean(scaled, -1, keepdims=True)
        - unit * jnp.mean(scaled * unit, -1, keepdims=True)
    )


def project_kernel(*refs, tm):
    blocks = refs[:tm]
    mask_ref, embed_ref, pos_ref, gain_ref, shift_ref, w_ref, bias_ref, filled_ref, turned_ref, joint_ref, normed_s = refs[tm:]

    @pl.when(pl.program_id(0) == 0)
    def _():
        seg = blocks[0].shape[0]
        embed, gain, shift = (r[...].astype(F32) for r in (embed_ref, gain_ref, shift_ref))
        for d in range(tm):
            rows = slice(d * seg, (d + 1) * seg)
            filled = jnp.where(mask_ref[rows] > 0.5, embed, blocks[d][...].astype(F32)) + pos_ref[rows].astype(F32)
            unit, _ = norm_parts(filled)
            normed = (unit * gain + shift).astype(BF16)
            filled_ref[rows] = filled
            normed_s[rows] = normed
            turned_ref[:, rows] = normed.T

    joint_ref[...] = (contract(normed_s[...], w_ref[...], 1, 0) + bias_ref[...].astype(F32)).astype(BF16)


def project(blocks, mask, embed, pos, gain, shift, w_qkv, bias):
    tm = len(blocks)
    seg, width = blocks[0].shape
    rows = tm * seg
    return call(
        functools.partial(project_kernel, tm=tm),
        grid=(3,),
        in_specs=[fixed((seg, width))] * tm
        + [fixed((rows, 1)), fixed((1, width)), fixed((rows, width)), fixed((1, width)), fixed((1, width))]
        + [pl.BlockSpec((width, width), lambda j: (0, j)), pl.BlockSpec((1, width), lambda j: (0, j))],
        out_specs=[
            pl.BlockSpec((rows, width), lambda j: (0, 0)),
            pl.BlockSpec((width, rows), lambda j: (0, 0)),
            pl.BlockSpec((rows, width), lambda j: (0, j)),
        ],
        out_shape=[shaped((rows, width), F32), shaped((width, rows), BF16), shaped((rows, 3 * width), BF16)],
        scratch=[pltpu.VMEM((rows, width), BF16)],
        flops=6 * rows * width * width,
        moved=20 * rows * width,
    )(*blocks, mask, embed, pos, gain, shift, w_qkv, bias)


def own_lanes(value, i, head):
    lane = lax.broadcasted_iota(jnp.int32, value.shape, 1)
    return jnp.where((lane >= i * head) & (lane < (i + 1) * head), value, jnp.zeros_like(value))


def attend_kernel(q_ref, k_ref, v_ref, o_ref, turned_ref, log_ref, *, head):
    factor = head**-0.5 * LOG2_E
    per = LANES // head
    pairs = [slice(at, at + LANES) for at in range(0, q_ref.shape[1], LANES)]
    scores = [[contract(k_ref[:, n], own_lanes(q_ref[:, n], i, head), 1, 1) for i in range(per)] for n in pairs]
    for pair, lanes in enumerate(pairs):
        outs = []
        for i in range(per):
            peak = jnp.max(scores[pair][i], 0, keepdims=True)
            raised = jnp.exp2((scores[pair][i] - peak) * factor)
            total = jnp.sum(raised, 0, keepdims=True)
            mixed = contract(v_ref[:, lanes], raised.astype(BF16), 0, 0)
            outs.append(mixed[i * head : (i + 1) * head] * (1.0 / total))
            log_ref[pair, i : i + 1, :] = peak * factor + jnp.log2(total)
        turned = jnp.concatenate(outs, 0)
        turned_ref[lanes] = turned.astype(BF16)
        o_ref[:, lanes] = turned.T.astype(BF16)


def attend(joint, width):
    rows = joint.shape[0]
    head = width // HEADS
    pairs, per = width // LANES, LANES // head
    some = 2 if pairs % 2 == 0 else 1
    steps = pairs // some
    block = lambda off: pl.BlockSpec((rows, some * LANES), lambda h: (0, h + off))
    return call(
        functools.partial(attend_kernel, head=head),
        grid=(steps,),
        in_specs=[block(0), block(steps), block(2 * steps)],
        out_specs=[
            block(0),
            pl.BlockSpec((some * LANES, rows), lambda h: (h, 0)),
            pl.BlockSpec((some, per, rows), lambda h: (h, 0, 0)),
        ],
        out_shape=[shaped((rows, width), BF16), shaped((width, rows), BF16), shaped((pairs, per, rows), F32)],
        flops=16 * rows * rows * width,
        moved=8 * rows * width,
        exps=rows * rows * HEADS,
    )(joint, joint, joint)


def attend_back_kernel(side_ref, *refs, head, groups):
    per_clip = [refs[4 * c : 4 * c + 4] for c in range(groups)]
    g_ref, out_ref = refs[4 * groups :]
    scale = head**-0.5
    length = per_clip[0][0].shape[0]
    per = LANES // head
    ahead = []
    for c, (q_ref, k_ref, v_ref, log_ref) in enumerate(per_clip):
        rows = slice(c * length, (c + 1) * length)
        for i in range(per):
            q_own, g_own = own_lanes(q_ref[...], i, head), own_lanes(g_ref[rows], i, head)
            ahead.append((q_own, g_own, contract(k_ref[...], q_own, 1, 1), contract(v_ref[...], g_own, 1, 1)))
    for c, (q_ref, k_ref, v_ref, log_ref) in enumerate(per_clip):
        rows = slice(c * length, (c + 1) * length)
        grad_q, grad_k, grad_v = [], 0.0, 0.0
        for i in range(per):
            q_own, g_own, scores, grad_probs = ahead[c * per + i]
            probs = jnp.exp2(scores * (scale * LOG2_E) - log_ref[0, i : i + 1, :])
            delta = jnp.sum(probs * grad_probs, 0, keepdims=True)
            grad_scores = (probs * (grad_probs - delta)).astype(BF16)
            grad_v = grad_v + contract(probs.astype(BF16), g_own, 1, 0)
            grad_q.append(contract(k_ref[...], grad_scores, 0, 0)[i * head : (i + 1) * head])
            grad_k = grad_k + contract(grad_scores, q_own, 1, 0)
        out_ref[0, rows] = (jnp.concatenate(grad_q, 0) * scale).T.astype(BF16)
        out_ref[1, rows] = (grad_k * scale).astype(BF16)
        out_ref[2, rows] = grad_v.astype(BF16)


def attend_back(side, joints, mix, logs):
    rows, width = mix.shape
    groups = len(joints)
    length = rows // groups
    head = width // HEADS
    pairs, per = width // LANES, LANES // head
    half = pairs // 2

    def block(off):
        return pl.BlockSpec((length, LANES), lambda h, s: (0, off + s[0] * half + h))

    clip = [block(0), block(pairs), block(2 * pairs), pl.BlockSpec((1, per, length), lambda h, s: (s[0] * half + h, 0, 0))]
    operands = []
    for joint, log_sum in zip(joints, logs):
        operands += [joint, joint, joint, log_sum]
    return call(
        functools.partial(attend_back_kernel, head=head, groups=groups),
        prefetch=1,
        share=4096,
        grid=(half,),
        in_specs=clip * groups + [pl.BlockSpec((rows, LANES), lambda h, s: (0, s[0] * half + h))],
        out_specs=pl.BlockSpec((3, rows, LANES), lambda h, s: (0, 0, h)),
        out_shape=shaped((3, rows, width // 2), BF16),
        flops=20 * rows * length * width,
        moved=8 * rows * width,
        exps=rows * length * HEADS // 2,
    )(side, *operands, mix)


def gelu_parts(u):
    phi = 0.5 * (1.0 + lax.erf(u * ROOT_HALF))
    return u * phi, phi + u * jnp.exp(-0.5 * u * u) * (1.0 / ROOT_TWO_PI)


def by_segment(refs, values, clip=None):
    clips, seg, _ = refs[0].shape
    for c in range(clips) if clip is None else (clip,):
        for d, ref in enumerate(refs):
            at = ((0 if clip is not None else c) * len(refs) + d) * seg
            ref[c] = values[at : at + seg]


def forward_kernel(*refs, groups, chunk):
    filled, attended = refs[:groups], refs[groups : 2 * groups]
    (w_out_ref, out_bias_ref, gain_ref, shift_ref, down_bias_ref, w_up_ref, up_bias_ref, w_down_ref,
     hidden_ref, turned_ref, act_ref, slope_ref, *block_refs, out_s, normed_s) = refs[2 * groups :]
    rows_all = out_s.shape[0]
    step, last = pl.program_id(0), pl.num_programs(0) - 1

    @pl.when(step == 0)
    def _():
        gain, shift = gain_ref[...].astype(F32), shift_ref[...].astype(F32)
        out_bias, down_bias = out_bias_ref[...].astype(F32), down_bias_ref[...].astype(F32)
        length = filled[0].shape[0]
        for c in range(groups):
            rows = slice(c * length, (c + 1) * length)
            hidden = filled[c][...] + contract(attended[c][...], w_out_ref[...], 1, 0) + out_bias
            unit, _ = norm_parts(hidden)
            normed = (unit * gain + shift).astype(BF16)
            hidden_ref[rows] = hidden
            normed_s[rows] = normed
            turned_ref[:, rows] = normed.T
            out_s[rows] = hidden + down_bias

    w_up, w_down = w_up_ref[...], w_down_ref[...]
    bias = up_bias_ref[...].astype(F32)
    chunks = [slice(at, at + chunk) for at in range(0, rows_all, chunk)]
    ahead = [contract(normed_s[rows], w_up, 1, 0) for rows in chunks]
    for rows, up in zip(chunks, ahead):
        value, slope = gelu_parts(up + bias)
        act = value.astype(BF16)
        act_ref[:, rows] = act.T
        slope_ref[rows] = slope.astype(BF16)
        out_s[rows] += contract(act, w_down, 1, 0)

    @pl.when(step == last)
    def _():
        by_segment(block_refs, out_s[...].astype(BF16))


def forward(filled, attended, w_out, out_bias, gain, shift, down_bias, w_up, up_bias, w_down, tile, chunk, tm):
    groups, (length, width) = len(filled), filled[0].shape
    rows, ff = groups * length, w_up.shape[1]
    vec = fixed((1, width))
    whole = pl.BlockSpec((rows, width), lambda j: (0, 0), pipeline_mode=pl.Buffered(1))
    column = pl.BlockSpec((rows, tile), lambda j: (0, j))
    return call(
        functools.partial(forward_kernel, groups=groups, chunk=chunk),
        grid=(ff // tile,),
        in_specs=[fixed((length, width))] * (2 * groups)
        + [fixed((width, width)), vec, vec, vec, vec]
        + [
            pl.BlockSpec((width, tile), lambda j: (0, j)),
            pl.BlockSpec((1, tile), lambda j: (0, j)),
            pl.BlockSpec((tile, width), lambda j: (j, 0)),
        ],
        out_specs=[whole, fixed((width, rows)), pl.BlockSpec((tile, rows), lambda j: (j, 0)), column]
        + [fixed((groups, length // tm, width))] * tm,
        out_shape=[shaped((rows, width), F32), shaped((width, rows), BF16)]
        + [shaped((ff, rows), BF16), shaped((rows, ff), BF16)]
        + [shaped((groups, length // tm, width), BF16)] * tm,
        scratch=[pltpu.VMEM((rows, width), F32), pltpu.VMEM((rows, width), BF16)],
        flops=4 * rows * width * ff + 2 * rows * width * width,
        moved=14 * rows * width + 4 * rows * ff + 4 * width * ff,
        exps=rows * ff,
    )(*filled, *attended, w_out, out_bias, gain, shift, down_bias, w_up, up_bias, w_down)


def tile_back(turned_ref, cot_ref, act_ref, slope_ref, w_up_ref, w_down_ref, gup_s, norm_s, down_ref, up_ref, bias_ref, chunk):
    w_up, w_down = w_up_ref[...], w_down_ref[...]
    total = jnp.zeros(bias_ref.shape, F32)
    chunks = [slice(at, at + chunk) for at in range(0, cot_ref.shape[0], chunk)]
    ahead = [contract(cot_ref[rows], w_down, 1, 1) for rows in chunks]
    down_ref[...] = contract(act_ref[...], cot_ref[...], 1, 0).astype(BF16)
    for rows, grad_act in zip(chunks, ahead):
        gup = (grad_act * slope_ref[rows].astype(F32)).astype(BF16)
        gup_s[rows] = gup
        total = total + jnp.sum(gup.astype(F32), 0, keepdims=True)
        norm_s[rows] += contract(gup, w_up, 1, 1)
    bias_ref[...] = total
    up_ref[...] = contract(turned_ref[...], gup_s[...], 1, 0).astype(BF16)


def back_first_kernel(side_ref, turned_ref, cot_ref, act_ref, slope_ref, w_up_ref, w_down_ref, norm_ref, down_ref, up_ref, bias_ref, gup_s, *, chunk):
    @pl.when(pl.program_id(0) == 0)
    def _():
        norm_ref[...] = jnp.zeros_like(norm_ref)

    tile_back(turned_ref, cot_ref, act_ref, slope_ref, w_up_ref, w_down_ref, gup_s, norm_ref, down_ref, up_ref, bias_ref, chunk)


def back_last_kernel(side_ref, *refs, groups, chunk):
    attended = refs[:groups]
    (turned_ref, cot_ref, act_ref, slope_ref, w_up_ref, w_down_ref, w_out_ref, gain_ref, hidden_ref, norm_ref,
     down_ref, up_ref, bias_ref, grad_hidden_ref, mix_ref, grad_out_ref, sums_ref, gup_s, norm_s, branch_s) = refs[groups:]

    @pl.when(pl.program_id(0) == 0)
    def _():
        norm_s[...] = norm_ref[...]

    tile_back(turned_ref, cot_ref, act_ref, slope_ref, w_up_ref, w_down_ref, gup_s, norm_s, down_ref, up_ref, bias_ref, chunk)

    @pl.when(pl.program_id(0) == pl.num_programs(0) - 1)
    def _():
        gain = gain_ref[...].astype(F32)
        total = [jnp.zeros_like(gain) for _ in range(4)]
        w_out = w_out_ref[...]
        for r in range(norm_s.shape[0] // chunk):
            rows = slice(r * chunk, (r + 1) * chunk)
            unit, inverse = norm_parts(hidden_ref[rows])
            top, grad_norm = cot_ref[rows].astype(F32), norm_s[rows]
            grad_hidden = top + norm_backward(grad_norm, unit, inverse, gain)
            grad_hidden_ref[rows] = grad_hidden
            branch = grad_hidden.astype(BF16)
            branch_s[rows] = branch
            mix_ref[rows] = contract(branch, w_out, 1, 1).astype(BF16)
            parts = (branch.astype(F32), top, grad_norm * unit, grad_norm)
            total = [t + jnp.sum(p, 0, keepdims=True) for t, p in zip(total, parts)]
        sums_ref[...] = jnp.concatenate(total + [jnp.zeros_like(gain)] * 4, 0)
        length = attended[0].shape[1]
        grad_out = 0.0
        for c in range(groups):
            grad_out = grad_out + contract(attended[c][...], branch_s[c * length : (c + 1) * length], 1, 0)
        grad_out_ref[...] = grad_out.astype(BF16)


def back_specs(rows, width, half, tile):
    steps = half // tile
    column = lambda n: pl.BlockSpec((n, tile), lambda j, s: (0, s[0] * steps + j))
    ins = [fixed((width, rows)), fixed((rows, width))]
    ins += [pl.BlockSpec((tile, rows), lambda j, s: (s[0] * steps + j, 0)), column(rows), column(width)]
    ins.append(pl.BlockSpec((tile, width), lambda j, s: (s[0] * steps + j, 0)))
    outs = [
        pl.BlockSpec((tile, width), lambda j, s: (j, 0)),
        pl.BlockSpec((width, tile), lambda j, s: (0, j)),
        pl.BlockSpec((1, tile), lambda j, s: (0, j)),
    ]
    return ins, outs, [shaped((half, width), BF16), shaped((width, half), BF16), shaped((1, half), F32)]


def back_first(side, normed, cot, act, slope, w_up, w_down, tile, chunk):
    rows, width = cot.shape
    half = w_up.shape[1] // 2
    ins, outs, shapes = back_specs(rows, width, half, tile)
    return call(
        functools.partial(back_first_kernel, chunk=chunk),
        prefetch=1,
        grid=(half // tile,),
        in_specs=ins,
        out_specs=[fixed((rows, width))] + outs,
        out_shape=[shaped((rows, width), F32)] + shapes,
        scratch=[pltpu.VMEM((rows, tile), BF16)],
        flops=8 * rows * width * half,
        moved=8 * rows * width + 4 * rows * half + 8 * width * half,
    )(side, normed, cot, act, slope, w_up, w_down)


def back_last(side, attended, normed, cot, act, slope, w_up, w_down, w_out, gain, hidden, norm, tile, chunk):
    rows, width = cot.shape
    groups = len(attended)
    half = w_up.shape[1] // 2
    ins, outs, shapes = back_specs(rows, width, half, tile)
    whole = lambda n: fixed((n, width))
    return call(
        functools.partial(back_last_kernel, groups=groups, chunk=chunk),
        prefetch=1,
        grid=(half // tile,),
        in_specs=[fixed((width, rows // groups))] * groups + ins + [whole(width), whole(1), whole(rows), whole(rows)],
        out_specs=outs + [whole(rows), whole(rows), whole(width), whole(8)],
        out_shape=shapes
        + [shaped((rows, width), F32), shaped((rows, width), BF16), shaped((width, width), BF16), shaped((8, width), F32)],
        scratch=[pltpu.VMEM((rows, tile), BF16), pltpu.VMEM((rows, width), F32), pltpu.VMEM((rows, width), BF16)],
        flops=8 * rows * width * half + 4 * rows * width * width,
        moved=20 * rows * width + 4 * rows * half + 8 * width * half,
    )(side, *attended, normed, cot, act, slope, w_up, w_down, w_out, gain, hidden, norm)


def joint_part(normed, grad_ref, grad_w_ref, bias_ref):
    length = normed[0].shape[1]
    grad_w = 0.0
    for c, normed_ref in enumerate(normed):
        grad_w = grad_w + contract(normed_ref[...], grad_ref[0, c * length : (c + 1) * length], 1, 0)
    grad_w_ref[...] = grad_w.astype(BF16)
    bias_ref[0] = jnp.sum(grad_ref[0].astype(F32), 0, keepdims=True)


def joint_first_kernel(side_ref, *refs, groups):
    normed, (grad_ref, weight_ref, grad_w_ref, bias_ref, acc_ref) = refs[:groups], refs[groups:]
    joint_part(normed, grad_ref, grad_w_ref, bias_ref)
    part = contract(grad_ref[0], weight_ref[...], 1, 1)

    @pl.when(pl.program_id(0) == 0)
    def _():
        acc_ref[...] = part

    @pl.when(pl.program_id(0) > 0)
    def _():
        acc_ref[...] += part


def joint_last_kernel(side_ref, *refs, groups, tm):
    normed, (grad_ref, weight_ref, acc_ref, grad_hidden_ref, gain_ref) = refs[:groups], refs[groups : groups + 5]
    refs = refs[groups + 5 :]
    filled, masks = refs[:groups], refs[groups : 2 * groups]
    (other_bias_ref, sums_ref, up_other_ref, up_own_ref, grad_out_ref, grad_w_ref, away_ref, kept_ref, *input_refs,
     acc_s, pos_s, bias_s, rest_ref) = refs[2 * groups :]
    core, me = side_ref[0], side_ref[1]
    length, half = normed[0].shape[1], grad_w_ref.shape[1]
    step = pl.program_id(0)
    joint_part(normed, grad_ref, grad_w_ref, bias_s.at[pl.ds(step, 1)])

    @pl.when(step == 0)
    def _():
        acc_s[...] = acc_ref[...] + contract(grad_ref[0], weight_ref[...], 1, 1)

    @pl.when(step == 1)
    def _():
        acc_s[...] += contract(grad_ref[0], weight_ref[...], 1, 1)

    @pl.when(step == 2)
    def _():
        gain = gain_ref[...].astype(F32)
        weight = weight_ref[...]
        total = [jnp.zeros_like(gain) for _ in range(3)]
        clips = [slice(c * length, (c + 1) * length) for c in range(groups)]
        grad_norms = [acc_s[rows] + contract(grad_ref[0, rows], weight, 1, 1) for rows in clips]
        for c, rows in enumerate(clips):
            grad_norm = grad_norms[c]
            unit, inverse = norm_parts(filled[c][...])
            grad_filled = grad_hidden_ref[rows] + norm_backward(grad_norm, unit, inverse, gain)
            masked = masks[c][...] > 0.5
            by_segment(input_refs, jnp.where(masked, 0.0, grad_filled).astype(BF16), c)
            parts = (grad_norm * unit, grad_norm, jnp.where(masked, grad_filled, 0.0))
            total = [t + jnp.sum(p, 0, keepdims=True) for t, p in zip(total, parts)]
            pos_s[...] = grad_filled if c == 0 else pos_s[...] + grad_filled
        seg = length // tm
        shares, share_rows, _ = rest_ref.shape
        pos_rows, some = length // shares, shares // tm
        for d in range(tm):
            own = pos_s[d * seg : (d + 1) * seg].reshape(some, pos_rows, pos_s.shape[1])
            rest_ref[pl.ds((me ^ d) * some, some), :pos_rows] = own.astype(BF16)

        def both(other, mine):
            return jnp.where(core == 0, jnp.concatenate([mine, other], 1), jnp.concatenate([other, mine], 1))

        width = gain.shape[1]
        up = both(up_other_ref[...], up_own_ref[...])
        sums = sums_ref[...]
        lines = [both(other_bias_ref[i], bias_s[i]) for i in (0, 2)] + [sums[0:1]]
        lines += [up[:, i * width : (i + 1) * width] for i in range(up.shape[1] // width)]
        lines += [sums[1:2], total[0], total[1], sums[2:3], sums[3:4], total[2]]
        lines.append(jnp.zeros((shares * (share_rows - pos_rows) - len(lines), width), F32))
        small = jnp.concatenate(lines, 0).reshape(shares, share_rows - pos_rows, width)
        rest_ref[:, pos_rows:] = small.astype(BF16)
        rest, grad_out = rest_ref[...], grad_out_ref[...]
        away_ref[...] = jnp.where(core == 1, grad_out, rest)
        kept_ref[...] = jnp.where(core == 1, rest, grad_out)


def joint_specs(groups, rows, width):
    half = width // 2
    return [fixed((width, rows // groups))] * groups + [
        pl.BlockSpec((1, rows, half), lambda i, s: (i, 0, 0)),
        pl.BlockSpec((width, half), lambda i, s: (0, 2 * i + s[0])),
    ]


def joint_first(side, normed, grads, w_qkv):
    _, rows, half = grads.shape
    groups, width = len(normed), 2 * half
    return call(
        functools.partial(joint_first_kernel, groups=groups),
        prefetch=1,
        share=4096,
        grid=(3,),
        in_specs=joint_specs(groups, rows, width),
        out_specs=[
            pl.BlockSpec((width, half), lambda i, s: (0, i)),
            pl.BlockSpec((1, 1, half), lambda i, s: (i, 0, 0)),
            fixed((rows, width)),
        ],
        out_shape=[shaped((width, 3 * half), BF16), shaped((3, 1, half), F32), shaped((rows, width), F32)],
        flops=6 * rows * width * width,
        moved=12 * rows * width,
    )(side, *normed, grads, w_qkv)


def joint_last(side, normed, grads, w_qkv, acc, grad_hidden, gain, filled, masks, bias, sums, up_other, up_own, grad_out, tm):
    shares = grad_out.shape[0]
    _, rows, half = grads.shape
    groups, width = len(normed), 2 * half
    length = rows // groups
    return call(
        functools.partial(joint_last_kernel, groups=groups, tm=tm),
        prefetch=1,
        share=4096,
        grid=(3,),
        in_specs=joint_specs(groups, rows, width)
        + [fixed((rows, width))] * 2
        + [fixed((1, width))]
        + [fixed((length, width))] * groups
        + [fixed((length, 1))] * groups
        + [fixed((3, 1, half)), fixed((8, width)), fixed(up_other.shape), fixed(up_own.shape)]
        + [fixed(grad_out.shape)],
        out_specs=[
            pl.BlockSpec((width, half), lambda i, s: (0, i)),
            fixed(grad_out.shape),
            fixed(grad_out.shape),
        ]
        + [fixed((groups, length // tm, width))] * tm,
        out_shape=[
            shaped((width, 3 * half), BF16),
            shaped(grad_out.shape, BF16),
            shaped(grad_out.shape, BF16),
        ]
        + [shaped((groups, length // tm, width), BF16)] * tm,
        scratch=[
            pltpu.VMEM((rows, width), F32),
            pltpu.VMEM((length, width), F32),
            pltpu.VMEM((3, 1, half), F32),
            pltpu.VMEM(grad_out.shape, BF16),
        ],
        flops=6 * rows * width * width,
        moved=24 * rows * width,
    )(side, *normed, grads, w_qkv, acc, grad_hidden, gain, *filled, *masks, bias, sums, up_other, up_own, grad_out)


def spot_bits(order, tm):
    return [bits_of(bit) if axis == "tm" else bits_of(tm) + bits_of(bit) - 1 for axis, bit in order]


def shares_of(here_ref, refs, orders, tm, place):
    away = place ^ here_ref[0]
    low = here_ref[1] == 0
    half = len(refs) // 2
    out = []
    for own_ref, other_ref, order in zip(refs[:half], refs[half:], orders):
        index = sum(((away >> b) & 1) << k for k, b in enumerate(spot_bits(order, tm)))
        own, other = own_ref[index], other_ref[index]
        out.append((jnp.where(low, own, other).astype(F32), jnp.where(low, other, own).astype(F32)))
    return out


def place_one_kernel(here_ref, *refs, orders, tm, some):
    down_ref, up_ref = refs[4:]
    width = down_ref.shape[2]
    for u in range(some):
        downs, ups = shares_of(here_ref, refs[:4], orders, tm, pl.program_id(0) * some + u)
        rows = ups[0].shape[0]
        for core in range(2):
            parts = downs[core].shape[1] // width
            for part in range(parts):
                at = (u * parts + part) * rows
                down_ref[core, at : at + rows] = downs[core][:, part * width : (part + 1) * width]
            columns = ups[core].shape[1]
            up_ref[u * rows : (u + 1) * rows, core * columns : (core + 1) * columns] = ups[core]


def place_two_kernel(here_ref, *refs, orders, tm, some):
    qkv_ref, out_ref, pos_ref, small_ref = refs[4:]
    width = out_ref.shape[1]
    half = width // 2
    pos_rows, small_rows = pos_ref.shape[0] // some, small_ref.shape[0] // some
    for u in range(some):
        qkvs, (out, rest) = shares_of(here_ref, refs[:4], orders, tm, pl.program_id(0) * some + u)
        rows = slice(u * out.shape[0], (u + 1) * out.shape[0])
        for core in range(2):
            for i in range(3):
                at = i * width + core * half
                qkv_ref[rows, at : at + half] = qkvs[core][:, i * half : (i + 1) * half]
        out_ref[rows] = out
        pos_ref[u * pos_rows : (u + 1) * pos_rows] = rest[:pos_rows]
        small_ref[u * small_rows : (u + 1) * small_rows] = rest[pos_rows:]


def place(kernel, here, gathered, orders, tm, shapes):
    some = 4
    steps = gathered[0].shape[0] // some

    def cut(shape):
        block = shape[:-2] + (shape[-2] // steps, shape[-1])
        return pl.BlockSpec(block, lambda j, here: (0,) * (len(shape) - 2) + (j, 0))

    return call(
        functools.partial(kernel, orders=orders, tm=tm, some=some),
        prefetch=1,
        grid=(steps,),
        in_specs=[fixed(v.shape) for v in gathered],
        out_specs=[cut(s) for s in shapes],
        out_shape=[shaped(s, F32) for s in shapes],
        moved=sum(6 * v.size for v in gathered),
    )(here, *gathered)


def in_order(here, gathered, orders, tm):
    out = []
    half = len(gathered) // 2
    for own, other, order in zip(gathered[:half], gathered[half:], orders):
        bits = spot_bits(order, tm)
        away = jnp.arange(own.shape[0], dtype=jnp.int32) ^ here[0]
        index = sum(((away >> b) & 1) << k for k, b in enumerate(bits))
        own, other = (jnp.take(x, index, axis=0).astype(F32) for x in (own, other))
        low = here[1] == 0
        out.append(jnp.stack([jnp.where(low, own, other), jnp.where(low, other, own)]))
    return out


def bits_of(size):
    return size.bit_length() - 1


def axis_bits(axis):
    return [(axis, 1 << b) for b in range(bits_of(lax.axis_size(axis)))]


def own_bit(axis, bit):
    return (lax.axis_index(axis) // bit) % 2


def hop(value, axis, bit):
    size = lax.axis_size(axis)
    return lax.ppermute(value, axis, [(i, i ^ bit) for i in range(size)])


def tie(*values):
    return lax.optimization_barrier(values)


def take_clips(values):
    tm = lax.axis_size("tm")
    me = lax.axis_index("tm")
    out = []
    for d in range(tm):
        block = lax.dynamic_index_in_dim(values, me ^ d, 1, keepdims=False)
        out.append(hop(block, "tm", d) if d else block)
    return out


def send_clips(blocks):
    return [hop(block, "tm", d) if d else block for d, block in enumerate(blocks)]


def all_clips(blocks, shape):
    return jnp.stack(unshuffle(blocks), 1).reshape(shape)


def unshuffle(blocks):
    me = lax.axis_index("tm")
    blocks = list(blocks)
    for b in range(bits_of(len(blocks))):
        odd = ((me >> b) & 1) == 1
        blocks = [jnp.where(odd, blocks[i ^ (1 << b)], blocks[i]) for i in range(len(blocks))]
    return blocks


def add_low(a, b):
    return (a.astype(F32) + b.astype(F32)).astype(BF16)


def split_share(value):
    count = bits_of(lax.axis_size("clips")) + bits_of(lax.axis_size("tm")) - 1
    return value.reshape((2,) * count + (value.shape[0] >> count, value.shape[1]))


def side_by_side(value, parts):
    return jnp.concatenate(jnp.split(value, parts, -2), -1)


class Sum:
    def __init__(self, folds):
        self.folds = folds
        clip_bits, self.time_bits = axis_bits("clips")[1:], axis_bits("tm")
        self.names = clip_bits[::-1] + self.time_bits[::-1]
        self.orders = (clip_bits, clip_bits[1:] + clip_bits[:1])
        self.rounds = len(clip_bits) + len(self.time_bits)

    def half(self, pair, names, name, other):
        at = names.index(name)
        mine = own_bit(*name)
        pick = lambda x: lax.dynamic_index_in_dim(x, 1 - mine if other else mine, at, keepdims=False)
        return add_low(*(pick(x) for x in pair))

    def half_of_all(self, index, state, other):
        sides = len(self.orders[0])
        if index < sides:
            names = [[n for n in self.names if n not in order[:index]] for order in self.orders]
            return [self.half(p, n, order[index], other) for p, n, order in zip(state, names, self.orders)]
        names = self.time_bits[index - sides :]
        parts = [self.half(pair, names[::-1], names[0], other) for pair in state]
        if len(parts) > 1:
            parts = [side_by_side(x, n) if n > 1 else x for x, n in zip(parts, self.folds)]
        return [jnp.concatenate(parts, -1) if len(parts) > 1 else parts[0]]

    def split(self, index, state):
        return [(away,) for away in self.half_of_all(index, state, True)] + state

    def send(self, index, state):
        sides = len(self.orders[0])
        names = [o[index] for o in self.orders] if index < sides else [self.time_bits[index - sides]]
        away, state = state[: len(names)], state[len(names) :]
        got = [hop(x, *name) for (x,), name in zip(away, names)]
        return list(zip(self.half_of_all(index, state, False), got))

    def scatter(self, index, state):
        return self.send(index, self.split(index, state))

    def share(self, state):
        return add_low(*state[0])

    def gather_orders(self):
        return [self.time_bits[::-1] + order[::-1] for order in self.orders]

    def gather(self, index, state, cut):
        if index < len(self.time_bits):
            return [(state[0], hop(state[0], *self.time_bits[::-1][index]))]
        names = [order[::-1][index - len(self.time_bits)] for order in self.orders]
        return [(value, hop(value, *name)) for value, name in zip(state, names)]

    def join(self, index, state, cut):
        out = [jnp.concatenate(pair, 0) for pair in state]
        if index == len(self.time_bits) - 1:
            return [out[0][..., :cut], out[0][..., cut:]]
        return out


def on_device(
    patches, mask_index, mask_count, w_qkv, q_bias, v_bias, w_out, out_bias, w_up, up_bias,
    w_down, down_bias, norm1_scale, norm1_shift, norm2_scale, norm2_shift, mask_embed, pos_embed,
    cotangent,
):
    clip_count, seg, width = patches.shape
    ff = w_up.shape[1]
    tm = lax.axis_size("tm")
    me = lax.axis_index("tm")
    length = seg * tm
    groups = clip_count // tm
    by_group = (groups, tm, seg, width)
    tile, chunk = 512, 512

    arrived, grouped = [], patches.reshape(by_group)
    for g in range(groups):
        arrived.append(take_clips(grouped[g : g + 1]))
        grouped, *arrived[g] = tie(grouped, *arrived[g])
    tied, *arrived[-1] = tie(cotangent, *arrived[-1])
    cot = take_clips(tied.reshape(by_group))
    arrived = [[b[0] for b in blocks] for blocks in arrived]

    row = lambda x: x.reshape(1, -1)
    joint_bias = row(jnp.concatenate([q_bias, jnp.zeros_like(q_bias), v_bias]))
    out_bias, up_bias, down_bias, gain1, shift1, gain2, shift2, embed = map(
        row, (out_bias, up_bias, down_bias, norm1_scale, norm1_shift, norm2_scale, norm2_shift, mask_embed)
    )
    starts = (me ^ jnp.arange(tm, dtype=jnp.int32)) * seg
    places = (starts[:, None] + jnp.arange(seg, dtype=jnp.int32)[None, :]).reshape(length)
    pos = jnp.concatenate([lax.dynamic_slice_in_dim(pos_embed, (me ^ d) * seg, seg, 0) for d in range(tm)], 0)
    slots = jnp.arange(mask_index.shape[1], dtype=jnp.int32)
    masks = []
    for g in range(groups):
        index_row = lax.dynamic_index_in_dim(mask_index, g * tm + me, 0, keepdims=False)
        count = lax.dynamic_index_in_dim(mask_count, g * tm + me, 0, keepdims=False)
        hit = (places[:, None] == index_row[None, :]) & (slots < count)[None, :]
        masks.append(jnp.any(hit, axis=1, keepdims=True).astype(F32))

    filled, normed_one, joints, attended, turned, logs = [], [], [], [], [], []
    for g in range(groups):
        f, n, j = project(arrived[g], masks[g], embed, pos, gain1, shift1, w_qkv, joint_bias)
        a, a_turned, log_sum = attend(j, width)
        if g < groups - 1:
            a, *arrived[g + 1] = tie(a, *arrived[g + 1])
        else:
            a, cot[1] = tie(a, cot[1])
        for kept, value in zip((filled, normed_one, joints, attended, turned, logs), (f, n, j, a, a_turned, log_sum)):
            kept.append(value)

    core = own_bit("clips", 1).astype(jnp.int32)
    kept_side = jnp.stack([core, me.astype(jnp.int32)])
    away_side = jnp.stack([1 - core, me.astype(jnp.int32)])
    shares = lax.axis_size("clips") // 2 * tm
    here = jnp.stack([(lax.axis_index("clips") // 2 * tm + me).astype(jnp.int32), core])
    hidden, normed_two, act, slope, *block_out = forward(
        filled, attended, w_out, out_bias, gain2, shift2, down_bias, w_up, up_bias, w_down, 1024, 256, tm
    )
    block_out[0], *cot = tie(block_out[0], *cot)
    cot = jnp.concatenate(cot, 1).reshape(groups * length, width)
    norm_acc, down, up, up_sums_away = back_first(away_side, normed_two, cot, act, slope, w_up, w_down, tile, chunk)
    down_got, up_got = hop(down, "clips", 1), hop(up, "clips", 1)
    down, up, up_sums, grad_hidden, mix, grad_out, sums_two = back_last(
        kept_side, turned, normed_two, cot, act, slope, w_up, w_down, w_out, gain2, hidden, norm_acc, tile, chunk
    )
    one = Sum((2, 1))

    def after(values, *states):
        flat = [x for state in states for pair in state for x in pair]
        tied = list(tie(*values, *flat))
        values, flat = tied[: len(values)], tied[len(values) :]
        back = [[tuple(flat.pop(0) for _ in pair) for pair in state] for state in states]
        return (values, *back)

    state = [tuple(split_share(x) for x in pair) for pair in ((down, down_got), (up, up_got))]
    state = one.split(0, state)
    (mix, *block_out), state = after((mix, *block_out), state)
    state = one.send(0, state)
    block_out = send_clips(block_out)
    grads = attend_back(away_side, joints, mix, logs)
    qkv, bias_sums, acc = joint_first(away_side, normed_one, grads, w_qkv)
    qkv_got = hop(qkv, "clips", 1)
    sent_out = block_out
    (acc, sent_out[1], sent_out[2]), state = after((acc, sent_out[1], sent_out[2]), state)
    state = one.split(1, state)
    (mix, acc), state = after((mix, acc), state)
    state = one.send(1, state)
    grads = attend_back(kept_side, joints, mix, logs)
    (grads, *rest_out), state = after((grads, *sent_out[3:]), state)
    sent_out[3:] = rest_out
    state = one.split(2, state)
    (grads,), state = after((grads,), state)
    state = one.send(2, state)
    qkv, rest_away, rest_kept, *input_grad = joint_last(
        kept_side, normed_one, grads, w_qkv, acc, grad_hidden, gain1, filled, masks, bias_sums, sums_two,
        up_sums_away, up_sums, grad_out.reshape(shares, width // shares, width), tm
    )
    (qkv, rest_away, rest_kept, *input_grad), state = after((qkv, rest_away, rest_kept, *input_grad), state)
    rest_away, rest_kept = rest_away.reshape(width, width), rest_kept.reshape(width, width)
    rest_got = hop(rest_away, "clips", 1)
    two = Sum((1, 1))
    pairs = [tuple(split_share(x) for x in pair) for pair in ((qkv, qkv_got), (rest_kept, rest_got))]
    cut_one, cut_two = ff // 2, 3 * width // 2
    share_rows = pairs[0][0].shape[-2]

    def scatter_steps(group, first):
        steps = [lambda s, i=i: group.split(i, s) for i in range(first, group.rounds)]
        return [(split, lambda s, i=i: group.send(i, s)) for i, split in zip(range(first, group.rounds), steps)]

    def gather_steps(group, cut):
        def prepare(i):
            if i == 0:
                return lambda s: [(group.share(s)[None],)]
            return lambda s: [(x,) for x in group.join(i - 1, s, cut)]

        return [
            (prepare(i), lambda s, i=i: group.gather(i, [x for (x,) in s], cut)) for i in range(group.rounds)
        ]

    def core_steps(group, cut):
        return [
            (
                lambda s: [(x,) for x in group.join(group.rounds - 1, s, cut)],
                lambda s: [(x, hop(x, "clips", 1)) for (x,) in s],
            )
        ]

    steps_one = scatter_steps(one, 3) + gather_steps(one, cut_one) + [None] + core_steps(one, cut_one)
    steps_two = scatter_steps(two, 0) + gather_steps(two, cut_two) + core_steps(two, cut_two)
    outputs = []
    for index in range(max(len(steps_one), len(steps_two))):
        if index == 2:
            block_out = all_clips(sent_out, patches.shape)
            (block_out,), state, pairs = after((block_out,), state, pairs)
        if index == len(steps_two) - 1:
            tied, pairs = after((*sent[3:], *outputs), pairs)
            sent[3:], outputs = tied[: len(sent) - 3], tied[len(sent) - 3 :]
        active = [steps[index] if index < len(steps) else None for steps in (steps_one, steps_two)]
        states = [step[0](x) if step else x for step, x in zip(active, (state, pairs))]
        live = [x for x, step in zip(states, active) if step]
        if index == 3:
            input_grad, *live = after(input_grad, *live)
            sent = send_clips(input_grad)
        elif index in (6, 7):
            sent[8 - index : 9 - index], *live = after(sent[8 - index : 9 - index], *live)
        elif index:
            _, *live = after((), *live)
        live = iter(live)
        state, pairs = (step[1](next(live)) if step else x for step, x in zip(active, states))
        if index == len(steps_one) - 1:
            one_all = [own for own, _ in state] + [other for _, other in state]
            if share_rows % 8 == 0:
                outputs = place(
                    place_one_kernel, here, one_all, one.gather_orders(), tm, ((2, ff // 2, width), (width, ff))
                )
    two_all = [own for own, _ in pairs] + [other for _, other in pairs]
    input_grad = all_clips(sent, patches.shape)

    orders_one, orders_two = one.gather_orders(), two.gather_orders()
    if share_rows % 8 == 0:
        down_sum, up_sum = outputs
        shapes = ((width, 3 * width), (width, width), (length, width), (width - length, width))
        qkv_sum, out_sum, pos_sum, small = place(place_two_kernel, here, two_all, orders_two, tm, shapes)
        down_sum = down_sum.reshape(ff, width)
    else:
        downs, ups = in_order(here, one_all, orders_one, tm)
        qkvs, rests = in_order(here, two_all, orders_two, tm)
        down_sum = jnp.stack(jnp.split(downs, 2, -1), 2).reshape(ff, width)
        up_sum = jnp.concatenate(list(ups.reshape(2, width, ff // 2)), 1)
        qkv_sum = jnp.stack(list(qkvs.reshape(2, width, 3, width // 2)), 2).reshape(width, 3 * width)
        out_sum, rest = rests[0].reshape(width, width), rests[1]
        pos_sum = rest[:, : length // shares].reshape(length, width)
        small = rest[:, length // shares :].reshape(width - length, width)
    v = []
    at = 0
    for n in (1, 1, 1, ff // width, 1, 1, 1, 1, 1, 1):
        v.append(small[at : at + n].reshape(-1))
        at += n
    return (block_out, input_grad, qkv_sum, v[0], v[1], out_sum, v[2], up_sum, v[3], down_sum, v[4],
            v[5], v[6], v[7], v[8], v[9], pos_sum)


def solution(mesh):
    rows = P("clips", "tm", None)
    in_specs = (rows, P("clips", None), P("clips")) + (P(),) * 15 + (rows,)
    out_specs = (rows, rows) + (P(),) * 15
    return jax.shard_map(on_device, mesh=mesh, in_specs=in_specs, out_specs=out_specs, check_vma=False)
```

```python
import functools

import jax
import jax.numpy as jnp
from jax import lax
from jax.experimental import pallas as pl
from jax.experimental.pallas import tpu as pltpu
from jax.sharding import PartitionSpec as P

HEADS = 12
LANES = 128
NORM_EPS = 1e-06
ROOT_HALF = 0.7071067811865476
ROOT_TWO_PI = 2.5066282746310002
LOG2_E = 1.4426950408889634
F32 = jnp.float32
BF16 = jnp.bfloat16
VMEM_LIMIT = 60 * 2**20


def contract(a, b, da, db):
    return lax.dot_general(a, b, (((da,), (db,)), ((), ())), preferred_element_type=F32)


def call(kernel, *, grid, in_specs, out_specs, out_shape, scratch=(), prefetch=0, flops=0, moved=0, exps=0, share=1):
    return pl.pallas_call(
        kernel,
        grid_spec=pltpu.PrefetchScalarGridSpec(
            num_scalar_prefetch=prefetch,
            grid=grid,
            in_specs=in_specs,
            out_specs=out_specs,
            scratch_shapes=scratch,
        ),
        out_shape=out_shape,
        cost_estimate=pl.CostEstimate(
            flops=int(flops) // share, bytes_accessed=int(moved) // share, transcendentals=int(exps) // share
        ),
        compiler_params=pltpu.CompilerParams(vmem_limit_bytes=VMEM_LIMIT),
    )


def fixed(shape):
    return pl.BlockSpec(shape, lambda *_: (0,) * len(shape), pipeline_mode=pl.Buffered(1))


def shaped(shape, dtype):
    return jax.ShapeDtypeStruct(shape, dtype)


def norm_parts(values):
    centred = values - jnp.mean(values, -1, keepdims=True)
    spread = jnp.mean(centred * centred, -1, keepdims=True)
    inverse = lax.rsqrt(spread + NORM_EPS)
    return centred * inverse, inverse


def norm_backward(grad_norm, unit, inverse, gains):
    scaled = grad_norm * gains
    return inverse * (
        scaled
        - jnp.mean(scaled, -1, keepdims=True)
        - unit * jnp.mean(scaled * unit, -1, keepdims=True)
    )


def project_kernel(*refs, tm):
    blocks = refs[:tm]
    mask_ref, embed_ref, pos_ref, gain_ref, shift_ref, w_ref, bias_ref, filled_ref, turned_ref, joint_ref, normed_s = refs[tm:]

    @pl.when(pl.program_id(0) == 0)
    def _():
        seg = blocks[0].shape[0]
        embed, gain, shift = (r[...].astype(F32) for r in (embed_ref, gain_ref, shift_ref))
        for d in range(tm):
            rows = slice(d * seg, (d + 1) * seg)
            filled = jnp.where(mask_ref[rows] > 0.5, embed, blocks[d][...].astype(F32)) + pos_ref[rows].astype(F32)
            unit, _ = norm_parts(filled)
            normed = (unit * gain + shift).astype(BF16)
            filled_ref[rows] = filled
            normed_s[rows] = normed
            turned_ref[:, rows] = normed.T

    joint_ref[...] = (contract(normed_s[...], w_ref[...], 1, 0) + bias_ref[...].astype(F32)).astype(BF16)


def project(blocks, mask, embed, pos, gain, shift, w_qkv, bias):
    tm = len(blocks)
    seg, width = blocks[0].shape
    rows = tm * seg
    return call(
        functools.partial(project_kernel, tm=tm),
        grid=(3,),
        in_specs=[fixed((seg, width))] * tm
        + [fixed((rows, 1)), fixed((1, width)), fixed((rows, width)), fixed((1, width)), fixed((1, width))]
        + [pl.BlockSpec((width, width), lambda j: (0, j)), pl.BlockSpec((1, width), lambda j: (0, j))],
        out_specs=[
            pl.BlockSpec((rows, width), lambda j: (0, 0)),
            pl.BlockSpec((width, rows), lambda j: (0, 0)),
            pl.BlockSpec((rows, width), lambda j: (0, j)),
        ],
        out_shape=[shaped((rows, width), F32), shaped((width, rows), BF16), shaped((rows, 3 * width), BF16)],
        scratch=[pltpu.VMEM((rows, width), BF16)],
        flops=6 * rows * width * width,
        moved=20 * rows * width,
    )(*blocks, mask, embed, pos, gain, shift, w_qkv, bias)


def own_lanes(value, i, head):
    lane = lax.broadcasted_iota(jnp.int32, value.shape, 1)
    return jnp.where((lane >= i * head) & (lane < (i + 1) * head), value, jnp.zeros_like(value))


def attend_kernel(q_ref, k_ref, v_ref, o_ref, turned_ref, log_ref, *, head):
    factor = head**-0.5 * LOG2_E
    per = LANES // head
    pairs = [slice(at, at + LANES) for at in range(0, q_ref.shape[1], LANES)]
    scores = [[contract(k_ref[:, n], own_lanes(q_ref[:, n], i, head), 1, 1) for i in range(per)] for n in pairs]
    for pair, lanes in enumerate(pairs):
        outs = []
        for i in range(per):
            peak = jnp.max(scores[pair][i], 0, keepdims=True)
            raised = jnp.exp2((scores[pair][i] - peak) * factor)
            total = jnp.sum(raised, 0, keepdims=True)
            mixed = contract(v_ref[:, lanes], raised.astype(BF16), 0, 0)
            outs.append(mixed[i * head : (i + 1) * head] * (1.0 / total))
            log_ref[pair, i : i + 1, :] = peak * factor + jnp.log2(total)
        turned = jnp.concatenate(outs, 0)
        turned_ref[lanes] = turned.astype(BF16)
        o_ref[:, lanes] = turned.T.astype(BF16)


def attend(joint, width):
    rows = joint.shape[0]
    head = width // HEADS
    pairs, per = width // LANES, LANES // head
    some = 2 if pairs % 2 == 0 else 1
    steps = pairs // some
    block = lambda off: pl.BlockSpec((rows, some * LANES), lambda h: (0, h + off))
    return call(
        functools.partial(attend_kernel, head=head),
        grid=(steps,),
        in_specs=[block(0), block(steps), block(2 * steps)],
        out_specs=[
            block(0),
            pl.BlockSpec((some * LANES, rows), lambda h: (h, 0)),
            pl.BlockSpec((some, per, rows), lambda h: (h, 0, 0)),
        ],
        out_shape=[shaped((rows, width), BF16), shaped((width, rows), BF16), shaped((pairs, per, rows), F32)],
        flops=16 * rows * rows * width,
        moved=8 * rows * width,
        exps=rows * rows * HEADS,
    )(joint, joint, joint)


def attend_back_kernel(side_ref, *refs, head, groups):
    per_clip = [refs[4 * c : 4 * c + 4] for c in range(groups)]
    g_ref, out_ref = refs[4 * groups :]
    scale = head**-0.5
    length = per_clip[0][0].shape[0]
    per = LANES // head
    ahead = []
    for c, (q_ref, k_ref, v_ref, log_ref) in enumerate(per_clip):
        rows = slice(c * length, (c + 1) * length)
        for i in range(per):
            q_own, g_own = own_lanes(q_ref[...], i, head), own_lanes(g_ref[rows], i, head)
            ahead.append((q_own, g_own, contract(k_ref[...], q_own, 1, 1), contract(v_ref[...], g_own, 1, 1)))
    for c, (q_ref, k_ref, v_ref, log_ref) in enumerate(per_clip):
        rows = slice(c * length, (c + 1) * length)
        grad_q, grad_k, grad_v = [], 0.0, 0.0
        for i in range(per):
            q_own, g_own, scores, grad_probs = ahead[c * per + i]
            probs = jnp.exp2(scores * (scale * LOG2_E) - log_ref[0, i : i + 1, :])
            delta = jnp.sum(probs * grad_probs, 0, keepdims=True)
            grad_scores = (probs * (grad_probs - delta)).astype(BF16)
            grad_v = grad_v + contract(probs.astype(BF16), g_own, 1, 0)
            grad_q.append(contract(k_ref[...], grad_scores, 0, 0)[i * head : (i + 1) * head])
            grad_k = grad_k + contract(grad_scores, q_own, 1, 0)
        out_ref[0, rows] = (jnp.concatenate(grad_q, 0) * scale).T.astype(BF16)
        out_ref[1, rows] = (grad_k * scale).astype(BF16)
        out_ref[2, rows] = grad_v.astype(BF16)


def attend_back(side, joints, mix, logs):
    rows, width = mix.shape
    groups = len(joints)
    length = rows // groups
    head = width // HEADS
    pairs, per = width // LANES, LANES // head
    half = pairs // 2

    def block(off):
        return pl.BlockSpec((length, LANES), lambda h, s: (0, off + s[0] * half + h))

    clip = [block(0), block(pairs), block(2 * pairs), pl.BlockSpec((1, per, length), lambda h, s: (s[0] * half + h, 0, 0))]
    operands = []
    for joint, log_sum in zip(joints, logs):
        operands += [joint, joint, joint, log_sum]
    return call(
        functools.partial(attend_back_kernel, head=head, groups=groups),
        prefetch=1,
        share=4096,
        grid=(half,),
        in_specs=clip * groups + [pl.BlockSpec((rows, LANES), lambda h, s: (0, s[0] * half + h))],
        out_specs=pl.BlockSpec((3, rows, LANES), lambda h, s: (0, 0, h)),
        out_shape=shaped((3, rows, width // 2), BF16),
        flops=20 * rows * length * width,
        moved=8 * rows * width,
        exps=rows * length * HEADS // 2,
    )(side, *operands, mix)


def gelu_parts(u):
    phi = 0.5 * (1.0 + lax.erf(u * ROOT_HALF))
    return u * phi, phi + u * jnp.exp(-0.5 * u * u) * (1.0 / ROOT_TWO_PI)


def by_segment(refs, values, clip=None):
    clips, seg, _ = refs[0].shape
    for c in range(clips) if clip is None else (clip,):
        for d, ref in enumerate(refs):
            at = ((0 if clip is not None else c) * len(refs) + d) * seg
            ref[c] = values[at : at + seg]


def forward_kernel(*refs, groups, chunk):
    filled, attended = refs[:groups], refs[groups : 2 * groups]
    (w_out_ref, out_bias_ref, gain_ref, shift_ref, down_bias_ref, w_up_ref, up_bias_ref, w_down_ref,
     hidden_ref, turned_ref, act_ref, slope_ref, *block_refs, out_s, normed_s, hidden_s) = refs[2 * groups :]
    rows_all = out_s.shape[0]
    step, last = pl.program_id(0), pl.num_programs(0) - 1

    @pl.when(step == 0)
    def _():
        gain, shift = gain_ref[...].astype(F32), shift_ref[...].astype(F32)
        out_bias, down_bias = out_bias_ref[...].astype(F32), down_bias_ref[...].astype(F32)
        length = filled[0].shape[0]
        for c in range(groups):
            rows = slice(c * length, (c + 1) * length)
            hidden = filled[c][...] + contract(attended[c][...], w_out_ref[...], 1, 0) + out_bias
            unit, _ = norm_parts(hidden)
            normed = (unit * gain + shift).astype(BF16)
            hidden_s[rows] = hidden
            normed_s[rows] = normed
            turned_ref[:, rows] = normed.T
            out_s[rows] = hidden + down_bias

    w_up, w_down = w_up_ref[...], w_down_ref[...]
    bias = up_bias_ref[...].astype(F32)
    some = hidden_ref.shape[1]
    hidden_ref[...] = hidden_s[:, pl.ds(pl.multiple_of(step * some, some), some)]
    chunks = [slice(at, at + chunk) for at in range(0, rows_all, chunk)]
    ahead = [contract(normed_s[rows], w_up, 1, 0) for rows in chunks]
    for rows, up in zip(chunks, ahead):
        value, slope = gelu_parts(up + bias)
        act = value.astype(BF16)
        act_ref[:, rows] = act.T
        slope_ref[rows] = slope.astype(BF16)
        out_s[rows] += contract(act, w_down, 1, 0)

    @pl.when(step == last)
    def _():
        by_segment(block_refs, out_s[...].astype(BF16))


def forward(filled, attended, w_out, out_bias, gain, shift, down_bias, w_up, up_bias, w_down, tile, chunk, tm):
    groups, (length, width) = len(filled), filled[0].shape
    rows, ff = groups * length, w_up.shape[1]
    vec = fixed((1, width))
    column = pl.BlockSpec((rows, tile), lambda j: (0, j))
    return call(
        functools.partial(forward_kernel, groups=groups, chunk=chunk),
        grid=(ff // tile,),
        in_specs=[fixed((length, width))] * (2 * groups)
        + [fixed((width, width)), vec, vec, vec, vec]
        + [
            pl.BlockSpec((width, tile), lambda j: (0, j)),
            pl.BlockSpec((1, tile), lambda j: (0, j)),
            pl.BlockSpec((tile, width), lambda j: (j, 0)),
        ],
        out_specs=[cut_by_step(rows, width, ff // tile), fixed((width, rows)), pl.BlockSpec((tile, rows), lambda j: (j, 0)), column]
        + [fixed((groups, length // tm, width))] * tm,
        out_shape=[shaped((rows, width), F32), shaped((width, rows), BF16)]
        + [shaped((ff, rows), BF16), shaped((rows, ff), BF16)]
        + [shaped((groups, length // tm, width), BF16)] * tm,
        scratch=[pltpu.VMEM((rows, width), F32), pltpu.VMEM((rows, width), BF16), pltpu.VMEM((rows, width), F32)],
        flops=4 * rows * width * ff + 2 * rows * width * width,
        moved=14 * rows * width + 4 * rows * ff + 4 * width * ff,
        exps=rows * ff,
    )(*filled, *attended, w_out, out_bias, gain, shift, down_bias, w_up, up_bias, w_down)


def cut_by_step(rows, width, steps):
    return pl.BlockSpec((rows, width // steps), lambda j, *_: (0, j))


def tile_back(turned_ref, cot_ref, act_ref, slope_ref, w_up_ref, w_down_ref, gup_s, norm_s, down_ref, up_ref, bias_ref, chunk):
    w_up, w_down = w_up_ref[...], w_down_ref[...]
    total = jnp.zeros(bias_ref.shape, F32)
    chunks = [slice(at, at + chunk) for at in range(0, cot_ref.shape[0], chunk)]
    ahead = [contract(cot_ref[rows], w_down, 1, 1) for rows in chunks]
    down_ref[...] = contract(act_ref[...], cot_ref[...], 1, 0).astype(BF16)
    for rows, grad_act in zip(chunks, ahead):
        gup = (grad_act * slope_ref[rows].astype(F32)).astype(BF16)
        gup_s[rows] = gup
        total = total + jnp.sum(gup.astype(F32), 0, keepdims=True)
        norm_s[rows] += contract(gup, w_up, 1, 1)
    bias_ref[...] = total
    up_ref[...] = contract(turned_ref[...], gup_s[...], 1, 0).astype(BF16)


def back_first_kernel(side_ref, turned_ref, cot_ref, act_ref, slope_ref, w_up_ref, w_down_ref, norm_ref, down_ref, up_ref, bias_ref, gup_s, *, chunk):
    @pl.when(pl.program_id(0) == 0)
    def _():
        norm_ref[...] = jnp.zeros_like(norm_ref)

    tile_back(turned_ref, cot_ref, act_ref, slope_ref, w_up_ref, w_down_ref, gup_s, norm_ref, down_ref, up_ref, bias_ref, chunk)


def back_last_kernel(side_ref, *refs, groups, chunk):
    attended = refs[:groups]
    (turned_ref, cot_ref, act_ref, slope_ref, w_up_ref, w_down_ref, w_out_ref, gain_ref, hidden_ref, norm_ref,
     down_ref, up_ref, bias_ref, grad_hidden_ref, mix_ref, grad_out_ref, sums_ref, gup_s, norm_s, branch_s, hidden_s) = refs[groups:]

    @pl.when(pl.program_id(0) == 0)
    def _():
        norm_s[...] = jnp.zeros_like(norm_s)

    columns = pl.ds(pl.multiple_of(pl.program_id(0) * norm_ref.shape[1], norm_ref.shape[1]), norm_ref.shape[1])
    hidden_s[:, columns] = hidden_ref[...]
    norm_s[:, columns] += norm_ref[...]
    tile_back(turned_ref, cot_ref, act_ref, slope_ref, w_up_ref, w_down_ref, gup_s, norm_s, down_ref, up_ref, bias_ref, chunk)

    @pl.when(pl.program_id(0) == pl.num_programs(0) - 1)
    def _():
        gain = gain_ref[...].astype(F32)
        total = [jnp.zeros_like(gain) for _ in range(4)]
        w_out = w_out_ref[...]
        for r in range(norm_s.shape[0] // chunk):
            rows = slice(r * chunk, (r + 1) * chunk)
            unit, inverse = norm_parts(hidden_s[rows])
            top, grad_norm = cot_ref[rows].astype(F32), norm_s[rows]
            grad_hidden = top + norm_backward(grad_norm, unit, inverse, gain)
            grad_hidden_ref[rows] = grad_hidden
            branch = grad_hidden.astype(BF16)
            branch_s[rows] = branch
            mix_ref[rows] = contract(branch, w_out, 1, 1).astype(BF16)
            parts = (branch.astype(F32), top, grad_norm * unit, grad_norm)
            total = [t + jnp.sum(p, 0, keepdims=True) for t, p in zip(total, parts)]
        sums_ref[...] = jnp.concatenate(total + [jnp.zeros_like(gain)] * 4, 0)
        length = attended[0].shape[1]
        grad_out = 0.0
        for c in range(groups):
            grad_out = grad_out + contract(attended[c][...], branch_s[c * length : (c + 1) * length], 1, 0)
        grad_out_ref[...] = grad_out.astype(BF16)


def back_specs(rows, width, half, tile):
    steps = half // tile
    column = lambda n: pl.BlockSpec((n, tile), lambda j, s: (0, s[0] * steps + j))
    ins = [fixed((width, rows)), fixed((rows, width))]
    ins += [pl.BlockSpec((tile, rows), lambda j, s: (s[0] * steps + j, 0)), column(rows), column(width)]
    ins.append(pl.BlockSpec((tile, width), lambda j, s: (s[0] * steps + j, 0)))
    outs = [
        pl.BlockSpec((tile, width), lambda j, s: (j, 0)),
        pl.BlockSpec((width, tile), lambda j, s: (0, j)),
        pl.BlockSpec((1, tile), lambda j, s: (0, j)),
    ]
    return ins, outs, [shaped((half, width), BF16), shaped((width, half), BF16), shaped((1, half), F32)]


def back_first(side, normed, cot, act, slope, w_up, w_down, tile, chunk):
    rows, width = cot.shape
    half = w_up.shape[1] // 2
    ins, outs, shapes = back_specs(rows, width, half, tile)
    return call(
        functools.partial(back_first_kernel, chunk=chunk),
        prefetch=1,
        grid=(half // tile,),
        in_specs=ins,
        out_specs=[fixed((rows, width))] + outs,
        out_shape=[shaped((rows, width), F32)] + shapes,
        scratch=[pltpu.VMEM((rows, tile), BF16)],
        flops=8 * rows * width * half,
        moved=8 * rows * width + 4 * rows * half + 8 * width * half,
    )(side, normed, cot, act, slope, w_up, w_down)


def back_last(side, attended, normed, cot, act, slope, w_up, w_down, w_out, gain, hidden, norm, tile, chunk):
    rows, width = cot.shape
    groups = len(attended)
    half = w_up.shape[1] // 2
    ins, outs, shapes = back_specs(rows, width, half, tile)
    whole = lambda n: fixed((n, width))
    return call(
        functools.partial(back_last_kernel, groups=groups, chunk=chunk),
        prefetch=1,
        grid=(half // tile,),
        in_specs=[fixed((width, rows // groups))] * groups + ins + [whole(width), whole(1)] + [cut_by_step(rows, width, half // tile)] * 2,
        out_specs=outs + [whole(rows), whole(rows), whole(width), whole(8)],
        out_shape=shapes
        + [shaped((rows, width), F32), shaped((rows, width), BF16), shaped((width, width), BF16), shaped((8, width), F32)],
        scratch=[
            pltpu.VMEM((rows, tile), BF16),
            pltpu.VMEM((rows, width), F32),
            pltpu.VMEM((rows, width), BF16),
            pltpu.VMEM((rows, width), F32),
        ],
        flops=8 * rows * width * half + 4 * rows * width * width,
        moved=20 * rows * width + 4 * rows * half + 8 * width * half,
    )(side, *attended, normed, cot, act, slope, w_up, w_down, w_out, gain, hidden, norm)


def joint_part(normed, grad_ref, grad_w_ref, bias_ref):
    length = normed[0].shape[1]
    grad_w = 0.0
    for c, normed_ref in enumerate(normed):
        grad_w = grad_w + contract(normed_ref[...], grad_ref[0, c * length : (c + 1) * length], 1, 0)
    grad_w_ref[...] = grad_w.astype(BF16)
    bias_ref[0] = jnp.sum(grad_ref[0].astype(F32), 0, keepdims=True)


def joint_first_kernel(side_ref, *refs, groups):
    normed, (grad_ref, weight_ref, grad_w_ref, bias_ref, acc_ref) = refs[:groups], refs[groups:]
    joint_part(normed, grad_ref, grad_w_ref, bias_ref)
    part = contract(grad_ref[0], weight_ref[...], 1, 1)

    @pl.when(pl.program_id(0) == 0)
    def _():
        acc_ref[...] = part

    @pl.when(pl.program_id(0) > 0)
    def _():
        acc_ref[...] += part


def joint_last_kernel(side_ref, *refs, groups, tm):
    normed, (grad_ref, weight_ref, acc_ref, grad_hidden_ref, gain_ref) = refs[:groups], refs[groups : groups + 5]
    refs = refs[groups + 5 :]
    filled, masks = refs[:groups], refs[groups : 2 * groups]
    (other_bias_ref, sums_ref, up_other_ref, up_own_ref, grad_out_ref, grad_w_ref, away_ref, kept_ref, *input_refs,
     acc_s, pos_s, bias_s, rest_ref, hidden_s, filled_s) = refs[2 * groups :]
    core, me = side_ref[0], side_ref[1]
    length, half = normed[0].shape[1], grad_w_ref.shape[1]
    step = pl.program_id(0)
    joint_part(normed, grad_ref, grad_w_ref, bias_s.at[pl.ds(step, 1)])

    @pl.when(step == 0)
    def _():
        acc_s[...] = contract(grad_ref[0], weight_ref[...], 1, 1)

    some = acc_ref.shape[1]
    columns = pl.ds(pl.multiple_of(step * some, some), some)
    acc_s[:, columns] += acc_ref[...]
    hidden_s[:, columns] = grad_hidden_ref[...]
    for c in range(groups):
        filled_s[c, :, columns] = filled[c][...]

    @pl.when(step == 1)
    def _():
        acc_s[...] += contract(grad_ref[0], weight_ref[...], 1, 1)

    @pl.when(step == 2)
    def _():
        gain = gain_ref[...].astype(F32)
        weight = weight_ref[...]
        total = [jnp.zeros_like(gain) for _ in range(3)]
        clips = [slice(c * length, (c + 1) * length) for c in range(groups)]
        grad_norms = [acc_s[rows] + contract(grad_ref[0, rows], weight, 1, 1) for rows in clips]
        for c, rows in enumerate(clips):
            grad_norm = grad_norms[c]
            unit, inverse = norm_parts(filled_s[c])
            grad_filled = hidden_s[rows] + norm_backward(grad_norm, unit, inverse, gain)
            masked = masks[c][...] > 0.5
            by_segment(input_refs, jnp.where(masked, 0.0, grad_filled).astype(BF16), c)
            parts = (grad_norm * unit, grad_norm, jnp.where(masked, grad_filled, 0.0))
            total = [t + jnp.sum(p, 0, keepdims=True) for t, p in zip(total, parts)]
            pos_s[...] = grad_filled if c == 0 else pos_s[...] + grad_filled
        seg = length // tm
        shares, share_rows, _ = rest_ref.shape
        pos_rows, some = length // shares, shares // tm
        for d in range(tm):
            own = pos_s[d * seg : (d + 1) * seg].reshape(some, pos_rows, pos_s.shape[1])
            rest_ref[pl.ds((me ^ d) * some, some), :pos_rows] = own.astype(BF16)

        def both(other, mine):
            return jnp.where(core == 0, jnp.concatenate([mine, other], 1), jnp.concatenate([other, mine], 1))

        width = gain.shape[1]
        up = both(up_other_ref[...], up_own_ref[...])
        sums = sums_ref[...]
        lines = [both(other_bias_ref[i], bias_s[i]) for i in (0, 2)] + [sums[0:1]]
        lines += [up[:, i * width : (i + 1) * width] for i in range(up.shape[1] // width)]
        lines += [sums[1:2], total[0], total[1], sums[2:3], sums[3:4], total[2]]
        lines.append(jnp.zeros((shares * (share_rows - pos_rows) - len(lines), width), F32))
        small = jnp.concatenate(lines, 0).reshape(shares, share_rows - pos_rows, width)
        rest_ref[:, pos_rows:] = small.astype(BF16)
        rest, grad_out = rest_ref[...], grad_out_ref[...]
        away_ref[...] = jnp.where(core == 1, grad_out, rest)
        kept_ref[...] = jnp.where(core == 1, rest, grad_out)


def joint_specs(groups, rows, width):
    half = width // 2
    return [fixed((width, rows // groups))] * groups + [
        pl.BlockSpec((1, rows, half), lambda i, s: (i, 0, 0)),
        pl.BlockSpec((width, half), lambda i, s: (0, 2 * i + s[0])),
    ]


def joint_first(side, normed, grads, w_qkv):
    _, rows, half = grads.shape
    groups, width = len(normed), 2 * half
    return call(
        functools.partial(joint_first_kernel, groups=groups),
        prefetch=1,
        share=4096,
        grid=(3,),
        in_specs=joint_specs(groups, rows, width),
        out_specs=[
            pl.BlockSpec((width, half), lambda i, s: (0, i)),
            pl.BlockSpec((1, 1, half), lambda i, s: (i, 0, 0)),
            fixed((rows, width)),
        ],
        out_shape=[shaped((width, 3 * half), BF16), shaped((3, 1, half), F32), shaped((rows, width), F32)],
        flops=6 * rows * width * width,
        moved=12 * rows * width,
    )(side, *normed, grads, w_qkv)


def joint_last(side, normed, grads, w_qkv, acc, grad_hidden, gain, filled, masks, bias, sums, up_other, up_own, grad_out, tm):
    shares = grad_out.shape[0]
    _, rows, half = grads.shape
    groups, width = len(normed), 2 * half
    length = rows // groups
    return call(
        functools.partial(joint_last_kernel, groups=groups, tm=tm),
        prefetch=1,
        share=4096,
        grid=(3,),
        in_specs=joint_specs(groups, rows, width)
        + [cut_by_step(rows, width, 3)] * 2
        + [fixed((1, width))]
        + [cut_by_step(length, width, 3)] * groups
        + [fixed((length, 1))] * groups
        + [fixed((3, 1, half)), fixed((8, width)), fixed(up_other.shape), fixed(up_own.shape)]
        + [fixed(grad_out.shape)],
        out_specs=[
            pl.BlockSpec((width, half), lambda i, s: (0, i)),
            fixed(grad_out.shape),
            fixed(grad_out.shape),
        ]
        + [fixed((groups, length // tm, width))] * tm,
        out_shape=[
            shaped((width, 3 * half), BF16),
            shaped(grad_out.shape, BF16),
            shaped(grad_out.shape, BF16),
        ]
        + [shaped((groups, length // tm, width), BF16)] * tm,
        scratch=[
            pltpu.VMEM((rows, width), F32),
            pltpu.VMEM((length, width), F32),
            pltpu.VMEM((3, 1, half), F32),
            pltpu.VMEM(grad_out.shape, BF16),
            pltpu.VMEM((rows, width), F32),
            pltpu.VMEM((groups, length, width), F32),
        ],
        flops=6 * rows * width * width,
        moved=24 * rows * width,
    )(side, *normed, grads, w_qkv, acc, grad_hidden, gain, *filled, *masks, bias, sums, up_other, up_own, grad_out)


def spot_bits(order, tm):
    return [bits_of(bit) if axis == "tm" else bits_of(tm) + bits_of(bit) - 1 for axis, bit in order]


def shares_of(here_ref, refs, orders, tm, place):
    away = place ^ here_ref[0]
    low = here_ref[1] == 0
    half = len(refs) // 2
    out = []
    for own_ref, other_ref, order in zip(refs[:half], refs[half:], orders):
        index = sum(((away >> b) & 1) << k for k, b in enumerate(spot_bits(order, tm)))
        own, other = own_ref[index], other_ref[index]
        out.append((jnp.where(low, own, other).astype(F32), jnp.where(low, other, own).astype(F32)))
    return out


def place_one_kernel(here_ref, *refs, orders, tm, some):
    down_ref, up_ref = refs[4:]
    width = down_ref.shape[2]
    for u in range(some):
        downs, ups = shares_of(here_ref, refs[:4], orders, tm, pl.program_id(0) * some + u)
        rows = ups[0].shape[0]
        for core in range(2):
            parts = downs[core].shape[1] // width
            for part in range(parts):
                at = (u * parts + part) * rows
                down_ref[core, at : at + rows] = downs[core][:, part * width : (part + 1) * width]
            columns = ups[core].shape[1]
            up_ref[u * rows : (u + 1) * rows, core * columns : (core + 1) * columns] = ups[core]


def place_two_kernel(here_ref, *refs, orders, tm, some):
    qkv_ref, out_ref, pos_ref, small_ref = refs[4:]
    width = out_ref.shape[1]
    half = width // 2
    pos_rows, small_rows = pos_ref.shape[0] // some, small_ref.shape[0] // some
    for u in range(some):
        lefts, rights = shares_of(here_ref, refs[:4], orders, tm, pl.program_id(0) * some + u)
        shares = [jnp.concatenate(sides, 1) for sides in zip(lefts, rights)]
        qkvs = [share[:, : 3 * half] for share in shares]
        out, rest = [share[:, 3 * half :] for share in shares]
        rows = slice(u * out.shape[0], (u + 1) * out.shape[0])
        for core in range(2):
            for i in range(3):
                at = i * width + core * half
                qkv_ref[rows, at : at + half] = qkvs[core][:, i * half : (i + 1) * half]
        out_ref[rows] = out
        pos_ref[u * pos_rows : (u + 1) * pos_rows] = rest[:pos_rows]
        small_ref[u * small_rows : (u + 1) * small_rows] = rest[pos_rows:]


def place(kernel, here, gathered, orders, tm, shapes):
    some = 4
    steps = gathered[0].shape[0] // some

    def cut(shape):
        block = shape[:-2] + (shape[-2] // steps, shape[-1])
        return pl.BlockSpec(block, lambda j, here: (0,) * (len(shape) - 2) + (j, 0))

    return call(
        functools.partial(kernel, orders=orders, tm=tm, some=some),
        prefetch=1,
        grid=(steps,),
        in_specs=[fixed(v.shape) for v in gathered],
        out_specs=[cut(s) for s in shapes],
        out_shape=[shaped(s, F32) for s in shapes],
        moved=sum(6 * v.size for v in gathered),
    )(here, *gathered)


def in_order(here, gathered, orders, tm):
    out = []
    half = len(gathered) // 2
    for own, other, order in zip(gathered[:half], gathered[half:], orders):
        bits = spot_bits(order, tm)
        away = jnp.arange(own.shape[0], dtype=jnp.int32) ^ here[0]
        index = sum(((away >> b) & 1) << k for k, b in enumerate(bits))
        own, other = (jnp.take(x, index, axis=0).astype(F32) for x in (own, other))
        low = here[1] == 0
        out.append(jnp.stack([jnp.where(low, own, other), jnp.where(low, other, own)]))
    return out


def bits_of(size):
    return size.bit_length() - 1


def axis_bits(axis):
    return [(axis, 1 << b) for b in range(bits_of(lax.axis_size(axis)))]


def own_bit(axis, bit):
    return (lax.axis_index(axis) // bit) % 2


def hop(value, axis, bit):
    size = lax.axis_size(axis)
    return lax.ppermute(value, axis, [(i, i ^ bit) for i in range(size)])


def tie(*values):
    return lax.optimization_barrier(values)


def take_clips(values):
    tm = lax.axis_size("tm")
    me = lax.axis_index("tm")
    out = []
    for d in range(tm):
        block = lax.dynamic_index_in_dim(values, me ^ d, 1, keepdims=False)
        out.append(hop(block, "tm", d) if d else block)
    return out


def send_clips(blocks):
    return [hop(block, "tm", d) if d else block for d, block in enumerate(blocks)]


def all_clips(blocks, shape):
    return jnp.stack(unshuffle(blocks), 1).reshape(shape)


def unshuffle(blocks):
    me = lax.axis_index("tm")
    blocks = list(blocks)
    for b in range(bits_of(len(blocks))):
        odd = ((me >> b) & 1) == 1
        blocks = [jnp.where(odd, blocks[i ^ (1 << b)], blocks[i]) for i in range(len(blocks))]
    return blocks


def add_low(a, b):
    return (a.astype(F32) + b.astype(F32)).astype(BF16)


def split_share(value):
    count = bits_of(lax.axis_size("clips")) + bits_of(lax.axis_size("tm")) - 1
    return value.reshape((2,) * count + (value.shape[0] >> count, value.shape[1]))


def side_by_side(value, parts):
    return jnp.concatenate(jnp.split(value, parts, -2), -1)


class Sum:
    def __init__(self, folds):
        self.folds = folds
        clip_bits, self.time_bits = axis_bits("clips")[1:], axis_bits("tm")
        self.names = clip_bits[::-1] + self.time_bits[::-1]
        self.orders = (clip_bits, clip_bits[1:] + clip_bits[:1])
        self.rounds = len(clip_bits) + len(self.time_bits)

    def half(self, pair, names, name, other):
        at = names.index(name)
        mine = own_bit(*name)
        pick = lambda x: lax.dynamic_index_in_dim(x, 1 - mine if other else mine, at, keepdims=False)
        return add_low(*(pick(x) for x in pair))

    def half_of_all(self, index, state, other):
        sides = len(self.orders[0])
        if index < sides:
            names = [[n for n in self.names if n not in order[:index]] for order in self.orders]
            return [self.half(p, n, order[index], other) for p, n, order in zip(state, names, self.orders)]
        names = self.time_bits[index - sides :]
        parts = [self.half(pair, names[::-1], names[0], other) for pair in state]
        if len(parts) > 1:
            parts = [side_by_side(x, n) if n > 1 else x for x, n in zip(parts, self.folds)]
        return [jnp.concatenate(parts, -1) if len(parts) > 1 else parts[0]]

    def split(self, index, state):
        return [(away,) for away in self.half_of_all(index, state, True)] + state

    def send(self, index, state):
        sides = len(self.orders[0])
        names = [o[index] for o in self.orders] if index < sides else [self.time_bits[index - sides]]
        away, state = state[: len(names)], state[len(names) :]
        got = [hop(x, *name) for (x,), name in zip(away, names)]
        return list(zip(self.half_of_all(index, state, False), got))

    def scatter(self, index, state):
        return self.send(index, self.split(index, state))

    def share(self, state):
        return add_low(*state[0])

    def gather_orders(self):
        return [self.time_bits[::-1] + order[::-1] for order in self.orders]

    def gather(self, index, state, cut):
        if index < len(self.time_bits):
            return [(state[0], hop(state[0], *self.time_bits[::-1][index]))]
        names = [order[::-1][index - len(self.time_bits)] for order in self.orders]
        return [(value, hop(value, *name)) for value, name in zip(state, names)]

    def join(self, index, state, cut):
        out = [jnp.concatenate(pair, 0) for pair in state]
        if index == len(self.time_bits) - 1:
            return [out[0][..., :cut], out[0][..., cut:]]
        return out


def on_device(
    patches, mask_index, mask_count, w_qkv, q_bias, v_bias, w_out, out_bias, w_up, up_bias,
    w_down, down_bias, norm1_scale, norm1_shift, norm2_scale, norm2_shift, mask_embed, pos_embed,
    cotangent,
):
    clip_count, seg, width = patches.shape
    ff = w_up.shape[1]
    tm = lax.axis_size("tm")
    me = lax.axis_index("tm")
    length = seg * tm
    groups = clip_count // tm
    by_group = (groups, tm, seg, width)
    tile, chunk = 512, 512

    arrived, grouped = [], patches.reshape(by_group)
    for g in range(groups):
        arrived.append(take_clips(grouped[g : g + 1]))
        grouped, *arrived[g] = tie(grouped, *arrived[g])
    tied, *arrived[-1] = tie(cotangent, *arrived[-1])
    cot = take_clips(tied.reshape(by_group))
    arrived = [[b[0] for b in blocks] for blocks in arrived]

    row = lambda x: x.reshape(1, -1)
    joint_bias = row(jnp.concatenate([q_bias, jnp.zeros_like(q_bias), v_bias]))
    out_bias, up_bias, down_bias, gain1, shift1, gain2, shift2, embed = map(
        row, (out_bias, up_bias, down_bias, norm1_scale, norm1_shift, norm2_scale, norm2_shift, mask_embed)
    )
    starts = (me ^ jnp.arange(tm, dtype=jnp.int32)) * seg
    places = (starts[:, None] + jnp.arange(seg, dtype=jnp.int32)[None, :]).reshape(length)
    pos = jnp.concatenate([lax.dynamic_slice_in_dim(pos_embed, (me ^ d) * seg, seg, 0) for d in range(tm)], 0)
    slots = jnp.arange(mask_index.shape[1], dtype=jnp.int32)
    masks = []
    for g in range(groups):
        index_row = lax.dynamic_index_in_dim(mask_index, g * tm + me, 0, keepdims=False)
        count = lax.dynamic_index_in_dim(mask_count, g * tm + me, 0, keepdims=False)
        hit = (places[:, None] == index_row[None, :]) & (slots < count)[None, :]
        masks.append(jnp.any(hit, axis=1, keepdims=True).astype(F32))

    filled, normed_one, joints, attended, turned, logs = [], [], [], [], [], []
    for g in range(groups):
        f, n, j = project(arrived[g], masks[g], embed, pos, gain1, shift1, w_qkv, joint_bias)
        a, a_turned, log_sum = attend(j, width)
        if g < groups - 1:
            a, *arrived[g + 1] = tie(a, *arrived[g + 1])
        else:
            a, cot[1] = tie(a, cot[1])
        for kept, value in zip((filled, normed_one, joints, attended, turned, logs), (f, n, j, a, a_turned, log_sum)):
            kept.append(value)

    core = own_bit("clips", 1).astype(jnp.int32)
    kept_side = jnp.stack([core, me.astype(jnp.int32)])
    away_side = jnp.stack([1 - core, me.astype(jnp.int32)])
    shares = lax.axis_size("clips") // 2 * tm
    here = jnp.stack([(lax.axis_index("clips") // 2 * tm + me).astype(jnp.int32), core])
    hidden, normed_two, act, slope, *block_out = forward(
        filled, attended, w_out, out_bias, gain2, shift2, down_bias, w_up, up_bias, w_down, 1024, 256, tm
    )
    block_out[0], *cot = tie(block_out[0], *cot)
    cot = jnp.concatenate(cot, 1).reshape(groups * length, width)
    norm_acc, down, up, up_sums_away = back_first(away_side, normed_two, cot, act, slope, w_up, w_down, tile, chunk)
    down_got, up_got = hop(down, "clips", 1), hop(up, "clips", 1)
    down, up, up_sums, grad_hidden, mix, grad_out, sums_two = back_last(
        kept_side, turned, normed_two, cot, act, slope, w_up, w_down, w_out, gain2, hidden, norm_acc, tile, chunk
    )
    one = Sum((2, 1))

    def after(values, *states):
        flat = [x for state in states for pair in state for x in pair]
        tied = list(tie(*values, *flat))
        values, flat = tied[: len(values)], tied[len(values) :]
        back = [[tuple(flat.pop(0) for _ in pair) for pair in state] for state in states]
        return (values, *back)

    state = [tuple(split_share(x) for x in pair) for pair in ((down, down_got), (up, up_got))]
    state = one.split(0, state)
    (mix, *block_out), state = after((mix, *block_out), state)
    state = one.send(0, state)
    block_out = send_clips(block_out)
    grads = attend_back(away_side, joints, mix, logs)
    qkv, bias_sums, acc = joint_first(away_side, normed_one, grads, w_qkv)
    qkv_got = hop(qkv, "clips", 1)
    sent_out = block_out
    (acc, sent_out[1], sent_out[2]), state = after((acc, sent_out[1], sent_out[2]), state)
    state = one.split(1, state)
    (mix, acc), state = after((mix, acc), state)
    state = one.send(1, state)
    grads = attend_back(kept_side, joints, mix, logs)
    (grads, *rest_out), state = after((grads, *sent_out[3:]), state)
    sent_out[3:] = rest_out
    state = one.split(2, state)
    (grads,), state = after((grads,), state)
    state = one.send(2, state)
    qkv, rest_away, rest_kept, *input_grad = joint_last(
        kept_side, normed_one, grads, w_qkv, acc, grad_hidden, gain1, filled, masks, bias_sums, sums_two,
        up_sums_away, up_sums, grad_out.reshape(shares, width // shares, width), tm
    )
    (qkv, rest_away, rest_kept, *input_grad), state = after((qkv, rest_away, rest_kept, *input_grad), state)
    rest_away, rest_kept = rest_away.reshape(width, width), rest_kept.reshape(width, width)
    rest_got = hop(rest_away, "clips", 1)
    two = Sum((1, 1))
    pairs = [tuple(split_share(x) for x in pair) for pair in ((qkv, qkv_got), (rest_kept, rest_got))]
    cut_one, cut_two = ff // 2, -(-5 * width // 4 // LANES) * LANES
    share_rows = pairs[0][0].shape[-2]

    def scatter_steps(group, first):
        steps = [lambda s, i=i: group.split(i, s) for i in range(first, group.rounds)]
        return [(split, lambda s, i=i: group.send(i, s)) for i, split in zip(range(first, group.rounds), steps)]

    def gather_steps(group, cut):
        def prepare(i):
            if i == 0:
                return lambda s: [(group.share(s)[None],)]
            return lambda s: [(x,) for x in group.join(i - 1, s, cut)]

        return [
            (prepare(i), lambda s, i=i: group.gather(i, [x for (x,) in s], cut)) for i in range(group.rounds)
        ]

    def core_steps(group, cut):
        return [
            (
                lambda s: [(x,) for x in group.join(group.rounds - 1, s, cut)],
                lambda s: [(x, hop(x, "clips", 1)) for (x,) in s],
            )
        ]

    steps_one = scatter_steps(one, 3) + gather_steps(one, cut_one) + [None] + core_steps(one, cut_one)
    steps_two = scatter_steps(two, 0) + gather_steps(two, cut_two) + core_steps(two, cut_two)
    outputs = []
    for index in range(max(len(steps_one), len(steps_two))):
        if index == 2:
            block_out = all_clips(sent_out, patches.shape)
            (block_out,), state, pairs = after((block_out,), state, pairs)
        if index == len(steps_two) - 1:
            tied, pairs = after((*sent[3:], *outputs), pairs)
            sent[3:], outputs = tied[: len(sent) - 3], tied[len(sent) - 3 :]
        active = [steps[index] if index < len(steps) else None for steps in (steps_one, steps_two)]
        states = [step[0](x) if step else x for step, x in zip(active, (state, pairs))]
        live = [x for x, step in zip(states, active) if step]
        if index == 3:
            input_grad, *live = after(input_grad, *live)
            sent = send_clips(input_grad)
        elif index in (6, 7):
            sent[8 - index : 9 - index], *live = after(sent[8 - index : 9 - index], *live)
        elif index:
            _, *live = after((), *live)
        live = iter(live)
        state, pairs = (step[1](next(live)) if step else x for step, x in zip(active, states))
        if index == len(steps_one) - 1:
            one_all = [own for own, _ in state] + [other for _, other in state]
            if share_rows % 8 == 0:
                outputs = place(
                    place_one_kernel, here, one_all, one.gather_orders(), tm, ((2, ff // 2, width), (width, ff))
                )
    two_all = [own for own, _ in pairs] + [other for _, other in pairs]
    input_grad = all_clips(sent, patches.shape)

    orders_one, orders_two = one.gather_orders(), two.gather_orders()
    if share_rows % 8 == 0:
        down_sum, up_sum = outputs
        shapes = ((width, 3 * width), (width, width), (length, width), (width - length, width))
        qkv_sum, out_sum, pos_sum, small = place(place_two_kernel, here, two_all, orders_two, tm, shapes)
        down_sum = down_sum.reshape(ff, width)
    else:
        downs, ups = in_order(here, one_all, orders_one, tm)
        both = jnp.concatenate(in_order(here, two_all, orders_two, tm), -1)
        qkvs, rests = both[..., : 3 * width // 2], both[..., 3 * width // 2 :]
        down_sum = jnp.stack(jnp.split(downs, 2, -1), 2).reshape(ff, width)
        up_sum = jnp.concatenate(list(ups.reshape(2, width, ff // 2)), 1)
        qkv_sum = jnp.stack(list(qkvs.reshape(2, width, 3, width // 2)), 2).reshape(width, 3 * width)
        out_sum, rest = rests[0].reshape(width, width), rests[1]
        pos_sum = rest[:, : length // shares].reshape(length, width)
        small = rest[:, length // shares :].reshape(width - length, width)
    v = []
    at = 0
    for n in (1, 1, 1, ff // width, 1, 1, 1, 1, 1, 1):
        v.append(small[at : at + n].reshape(-1))
        at += n
    return (block_out, input_grad, qkv_sum, v[0], v[1], out_sum, v[2], up_sum, v[3], down_sum, v[4],
            v[5], v[6], v[7], v[8], v[9], pos_sum)


def solution(mesh):
    rows = P("clips", "tm", None)
    in_specs = (rows, P("clips", None), P("clips")) + (P(),) * 15 + (rows,)
    out_specs = (rows, rows) + (P(),) * 15
    return jax.shard_map(on_device, mesh=mesh, in_specs=in_specs, out_specs=out_specs, check_vma=False)
```

```python
import functools

import jax
import jax.numpy as jnp
from jax import lax
from jax.experimental import pallas as pl
from jax.experimental.pallas import tpu as pltpu
from jax.sharding import PartitionSpec as P

HEADS = 12
LANES = 128
NORM_EPS = 1e-06
ROOT_HALF = 0.7071067811865476
ROOT_TWO_PI = 2.5066282746310002
LOG2_E = 1.4426950408889634
F32 = jnp.float32
BF16 = jnp.bfloat16
VMEM_LIMIT = 60 * 2**20


def contract(a, b, da, db):
    return lax.dot_general(a, b, (((da,), (db,)), ((), ())), preferred_element_type=F32)


def call(kernel, *, grid, in_specs, out_specs, out_shape, scratch=(), prefetch=0, flops=0, moved=0, exps=0, share=1):
    return pl.pallas_call(
        kernel,
        grid_spec=pltpu.PrefetchScalarGridSpec(
            num_scalar_prefetch=prefetch,
            grid=grid,
            in_specs=in_specs,
            out_specs=out_specs,
            scratch_shapes=scratch,
        ),
        out_shape=out_shape,
        cost_estimate=pl.CostEstimate(
            flops=int(flops) // share, bytes_accessed=int(moved) // share, transcendentals=int(exps) // share
        ),
        compiler_params=pltpu.CompilerParams(vmem_limit_bytes=VMEM_LIMIT),
    )


def fixed(shape):
    return pl.BlockSpec(shape, lambda *_: (0,) * len(shape), pipeline_mode=pl.Buffered(1))


def shaped(shape, dtype):
    return jax.ShapeDtypeStruct(shape, dtype)


def norm_parts(values):
    centred = values - jnp.mean(values, -1, keepdims=True)
    spread = jnp.mean(centred * centred, -1, keepdims=True)
    inverse = lax.rsqrt(spread + NORM_EPS)
    return centred * inverse, inverse


def norm_backward(grad_norm, unit, inverse, gains):
    scaled = grad_norm * gains
    return inverse * (
        scaled
        - jnp.mean(scaled, -1, keepdims=True)
        - unit * jnp.mean(scaled * unit, -1, keepdims=True)
    )


def project_kernel(*refs, tm):
    blocks = refs[:tm]
    mask_ref, embed_ref, pos_ref, gain_ref, shift_ref, w_ref, bias_ref, filled_ref, turned_ref, joint_ref, normed_s = refs[tm:]

    @pl.when(pl.program_id(0) == 0)
    def _():
        seg = blocks[0].shape[0]
        embed, gain, shift = (r[...].astype(F32) for r in (embed_ref, gain_ref, shift_ref))
        for d in range(tm):
            rows = slice(d * seg, (d + 1) * seg)
            filled = jnp.where(mask_ref[rows] > 0.5, embed, blocks[d][...].astype(F32)) + pos_ref[rows].astype(F32)
            unit, _ = norm_parts(filled)
            normed = (unit * gain + shift).astype(BF16)
            filled_ref[rows] = filled
            normed_s[rows] = normed
            turned_ref[:, rows] = normed.T

    joint_ref[...] = (contract(normed_s[...], w_ref[...], 1, 0) + bias_ref[...].astype(F32)).astype(BF16)


def project(blocks, mask, embed, pos, gain, shift, w_qkv, bias):
    tm = len(blocks)
    seg, width = blocks[0].shape
    rows = tm * seg
    return call(
        functools.partial(project_kernel, tm=tm),
        grid=(3,),
        in_specs=[fixed((seg, width))] * tm
        + [fixed((rows, 1)), fixed((1, width)), fixed((rows, width)), fixed((1, width)), fixed((1, width))]
        + [pl.BlockSpec((width, width), lambda j: (0, j)), pl.BlockSpec((1, width), lambda j: (0, j))],
        out_specs=[
            pl.BlockSpec((rows, width), lambda j: (0, 0)),
            pl.BlockSpec((width, rows), lambda j: (0, 0)),
            pl.BlockSpec((rows, width), lambda j: (0, j)),
        ],
        out_shape=[shaped((rows, width), F32), shaped((width, rows), BF16), shaped((rows, 3 * width), BF16)],
        scratch=[pltpu.VMEM((rows, width), BF16)],
        flops=6 * rows * width * width,
        moved=20 * rows * width,
    )(*blocks, mask, embed, pos, gain, shift, w_qkv, bias)


def own_lanes(value, i, head):
    lane = lax.broadcasted_iota(jnp.int32, value.shape, 1)
    return jnp.where((lane >= i * head) & (lane < (i + 1) * head), value, jnp.zeros_like(value))


def attend_kernel(q_ref, k_ref, v_ref, o_ref, turned_ref, log_ref, *, head):
    factor = head**-0.5 * LOG2_E
    per = LANES // head
    pairs = [slice(at, at + LANES) for at in range(0, q_ref.shape[1], LANES)]
    scores = [[contract(k_ref[:, n], own_lanes(q_ref[:, n], i, head), 1, 1) for i in range(per)] for n in pairs]
    for pair, lanes in enumerate(pairs):
        outs = []
        for i in range(per):
            peak = jnp.max(scores[pair][i], 0, keepdims=True)
            raised = jnp.exp2((scores[pair][i] - peak) * factor)
            total = jnp.sum(raised, 0, keepdims=True)
            mixed = contract(v_ref[:, lanes], raised.astype(BF16), 0, 0)
            outs.append(mixed[i * head : (i + 1) * head] * (1.0 / total))
            log_ref[pair, i : i + 1, :] = peak * factor + jnp.log2(total)
        turned = jnp.concatenate(outs, 0)
        turned_ref[lanes] = turned.astype(BF16)
        o_ref[:, lanes] = turned.T.astype(BF16)


def attend(joint, width):
    rows = joint.shape[0]
    head = width // HEADS
    pairs, per = width // LANES, LANES // head
    some = 2 if pairs % 2 == 0 else 1
    steps = pairs // some
    block = lambda off: pl.BlockSpec((rows, some * LANES), lambda h: (0, h + off))
    return call(
        functools.partial(attend_kernel, head=head),
        grid=(steps,),
        in_specs=[block(0), block(steps), block(2 * steps)],
        out_specs=[
            block(0),
            pl.BlockSpec((some * LANES, rows), lambda h: (h, 0)),
            pl.BlockSpec((some, per, rows), lambda h: (h, 0, 0)),
        ],
        out_shape=[shaped((rows, width), BF16), shaped((width, rows), BF16), shaped((pairs, per, rows), F32)],
        flops=16 * rows * rows * width,
        moved=8 * rows * width,
        exps=rows * rows * HEADS,
    )(joint, joint, joint)


def attend_back_kernel(side_ref, *refs, head, groups):
    per_clip = [refs[4 * c : 4 * c + 4] for c in range(groups)]
    g_ref, out_ref = refs[4 * groups :]
    scale = head**-0.5
    length = per_clip[0][0].shape[0]
    per = LANES // head
    ahead = []
    for c, (q_ref, k_ref, v_ref, log_ref) in enumerate(per_clip):
        rows = slice(c * length, (c + 1) * length)
        for i in range(per):
            q_own, g_own = own_lanes(q_ref[...], i, head), own_lanes(g_ref[rows], i, head)
            ahead.append((q_own, g_own, contract(k_ref[...], q_own, 1, 1), contract(v_ref[...], g_own, 1, 1)))
    for c, (q_ref, k_ref, v_ref, log_ref) in enumerate(per_clip):
        rows = slice(c * length, (c + 1) * length)
        grad_q, grad_k, grad_v = [], 0.0, 0.0
        for i in range(per):
            q_own, g_own, scores, grad_probs = ahead[c * per + i]
            probs = jnp.exp2(scores * (scale * LOG2_E) - log_ref[0, i : i + 1, :])
            delta = jnp.sum(probs * grad_probs, 0, keepdims=True)
            grad_scores = (probs * (grad_probs - delta)).astype(BF16)
            grad_v = grad_v + contract(probs.astype(BF16), g_own, 1, 0)
            grad_q.append(contract(k_ref[...], grad_scores, 0, 0)[i * head : (i + 1) * head])
            grad_k = grad_k + contract(grad_scores, q_own, 1, 0)
        out_ref[0, rows] = (jnp.concatenate(grad_q, 0) * scale).T.astype(BF16)
        out_ref[1, rows] = (grad_k * scale).astype(BF16)
        out_ref[2, rows] = grad_v.astype(BF16)


def attend_back(side, joints, mix, logs):
    rows, width = mix.shape
    groups = len(joints)
    length = rows // groups
    head = width // HEADS
    pairs, per = width // LANES, LANES // head
    half = pairs // 2

    def block(off):
        return pl.BlockSpec((length, LANES), lambda h, s: (0, off + s[0] * half + h))

    clip = [block(0), block(pairs), block(2 * pairs), pl.BlockSpec((1, per, length), lambda h, s: (s[0] * half + h, 0, 0))]
    operands = []
    for joint, log_sum in zip(joints, logs):
        operands += [joint, joint, joint, log_sum]
    return call(
        functools.partial(attend_back_kernel, head=head, groups=groups),
        prefetch=1,
        share=4096,
        grid=(half,),
        in_specs=clip * groups + [pl.BlockSpec((rows, LANES), lambda h, s: (0, s[0] * half + h))],
        out_specs=pl.BlockSpec((3, rows, LANES), lambda h, s: (0, 0, h)),
        out_shape=shaped((3, rows, width // 2), BF16),
        flops=20 * rows * length * width,
        moved=8 * rows * width,
        exps=rows * length * HEADS // 2,
    )(side, *operands, mix)


def gelu_parts(u):
    phi = 0.5 * (1.0 + lax.erf(u * ROOT_HALF))
    return u * phi, phi + u * jnp.exp(-0.5 * u * u) * (1.0 / ROOT_TWO_PI)


def by_segment(refs, values, clip=None):
    clips, seg, _ = refs[0].shape
    for c in range(clips) if clip is None else (clip,):
        for d, ref in enumerate(refs):
            at = ((0 if clip is not None else c) * len(refs) + d) * seg
            ref[c] = values[at : at + seg]


def forward_kernel(*refs, groups, chunk):
    filled, attended = refs[:groups], refs[groups : 2 * groups]
    (w_out_ref, out_bias_ref, gain_ref, shift_ref, down_bias_ref, w_up_ref, up_bias_ref, w_down_ref,
     hidden_ref, turned_ref, act_ref, slope_ref, *block_refs, out_s, normed_s, hidden_s) = refs[2 * groups :]
    rows_all = out_s.shape[0]
    step, last = pl.program_id(0), pl.num_programs(0) - 1

    @pl.when(step == 0)
    def _():
        gain, shift = gain_ref[...].astype(F32), shift_ref[...].astype(F32)
        out_bias, down_bias = out_bias_ref[...].astype(F32), down_bias_ref[...].astype(F32)
        length = filled[0].shape[0]
        for c in range(groups):
            rows = slice(c * length, (c + 1) * length)
            hidden = filled[c][...] + contract(attended[c][...], w_out_ref[...], 1, 0) + out_bias
            unit, _ = norm_parts(hidden)
            normed = (unit * gain + shift).astype(BF16)
            hidden_s[rows] = hidden
            normed_s[rows] = normed
            turned_ref[:, rows] = normed.T
            out_s[rows] = hidden + down_bias

    w_up, w_down = w_up_ref[...], w_down_ref[...]
    bias = up_bias_ref[...].astype(F32)
    some = hidden_ref.shape[1]
    hidden_ref[...] = hidden_s[:, pl.ds(pl.multiple_of(step * some, some), some)]
    chunks = [slice(at, at + chunk) for at in range(0, rows_all, chunk)]
    ahead = [contract(normed_s[rows], w_up, 1, 0) for rows in chunks]
    for rows, up in zip(chunks, ahead):
        value, slope = gelu_parts(up + bias)
        act = value.astype(BF16)
        act_ref[:, rows] = act.T
        slope_ref[rows] = slope.astype(BF16)
        out_s[rows] += contract(act, w_down, 1, 0)

    @pl.when(step == last)
    def _():
        by_segment(block_refs, out_s[...].astype(BF16))


def forward(filled, attended, w_out, out_bias, gain, shift, down_bias, w_up, up_bias, w_down, tile, chunk, tm):
    groups, (length, width) = len(filled), filled[0].shape
    rows, ff = groups * length, w_up.shape[1]
    vec = fixed((1, width))
    column = pl.BlockSpec((rows, tile), lambda j: (0, j))
    return call(
        functools.partial(forward_kernel, groups=groups, chunk=chunk),
        grid=(ff // tile,),
        in_specs=[fixed((length, width))] * (2 * groups)
        + [fixed((width, width)), vec, vec, vec, vec]
        + [
            pl.BlockSpec((width, tile), lambda j: (0, j)),
            pl.BlockSpec((1, tile), lambda j: (0, j)),
            pl.BlockSpec((tile, width), lambda j: (j, 0)),
        ],
        out_specs=[cut_by_step(rows, width, ff // tile), fixed((width, rows)), pl.BlockSpec((tile, rows), lambda j: (j, 0)), column]
        + [fixed((groups, length // tm, width))] * tm,
        out_shape=[shaped((rows, width), F32), shaped((width, rows), BF16)]
        + [shaped((ff, rows), BF16), shaped((rows, ff), BF16)]
        + [shaped((groups, length // tm, width), BF16)] * tm,
        scratch=[pltpu.VMEM((rows, width), F32), pltpu.VMEM((rows, width), BF16), pltpu.VMEM((rows, width), F32)],
        flops=4 * rows * width * ff + 2 * rows * width * width,
        moved=14 * rows * width + 4 * rows * ff + 4 * width * ff,
        exps=rows * ff,
    )(*filled, *attended, w_out, out_bias, gain, shift, down_bias, w_up, up_bias, w_down)


def cut_by_step(rows, width, steps):
    return pl.BlockSpec((rows, width // steps), lambda j, *_: (0, j))


def tile_back(turned_ref, cot_ref, act_ref, slope_ref, w_up_ref, w_down_ref, gup_s, norm_s, down_ref, up_ref, bias_ref, chunk):
    w_up, w_down = w_up_ref[...], w_down_ref[...]
    total = jnp.zeros(bias_ref.shape, F32)
    chunks = [slice(at, at + chunk) for at in range(0, cot_ref.shape[0], chunk)]
    ahead = [contract(cot_ref[rows], w_down, 1, 1) for rows in chunks]
    down_ref[...] = contract(act_ref[...], cot_ref[...], 1, 0).astype(BF16)
    for rows, grad_act in zip(chunks, ahead):
        gup = (grad_act * slope_ref[rows].astype(F32)).astype(BF16)
        gup_s[rows] = gup
        total = total + jnp.sum(gup.astype(F32), 0, keepdims=True)
        norm_s[rows] += contract(gup, w_up, 1, 1)
    bias_ref[...] = total
    up_ref[...] = contract(turned_ref[...], gup_s[...], 1, 0).astype(BF16)


def back_first_kernel(side_ref, turned_ref, cot_ref, act_ref, slope_ref, w_up_ref, w_down_ref, norm_ref, down_ref, up_ref, bias_ref, gup_s, *, chunk):
    @pl.when(pl.program_id(0) == 0)
    def _():
        norm_ref[...] = jnp.zeros_like(norm_ref)

    tile_back(turned_ref, cot_ref, act_ref, slope_ref, w_up_ref, w_down_ref, gup_s, norm_ref, down_ref, up_ref, bias_ref, chunk)


def back_last_kernel(side_ref, *refs, groups, chunk):
    attended = refs[:groups]
    (turned_ref, cot_ref, act_ref, slope_ref, w_up_ref, w_down_ref, w_out_ref, gain_ref, hidden_ref, norm_ref,
     down_ref, up_ref, bias_ref, grad_hidden_ref, mix_ref, grad_out_ref, sums_ref, gup_s, norm_s, branch_s, hidden_s) = refs[groups:]

    @pl.when(pl.program_id(0) == 0)
    def _():
        norm_s[...] = jnp.zeros_like(norm_s)

    columns = pl.ds(pl.multiple_of(pl.program_id(0) * norm_ref.shape[1], norm_ref.shape[1]), norm_ref.shape[1])
    hidden_s[:, columns] = hidden_ref[...]
    norm_s[:, columns] += norm_ref[...]
    tile_back(turned_ref, cot_ref, act_ref, slope_ref, w_up_ref, w_down_ref, gup_s, norm_s, down_ref, up_ref, bias_ref, chunk)

    @pl.when(pl.program_id(0) == pl.num_programs(0) - 1)
    def _():
        gain = gain_ref[...].astype(F32)
        total = [jnp.zeros_like(gain) for _ in range(4)]
        w_out = w_out_ref[...]
        for r in range(norm_s.shape[0] // chunk):
            rows = slice(r * chunk, (r + 1) * chunk)
            unit, inverse = norm_parts(hidden_s[rows])
            top, grad_norm = cot_ref[rows].astype(F32), norm_s[rows]
            grad_hidden = top + norm_backward(grad_norm, unit, inverse, gain)
            grad_hidden_ref[rows] = grad_hidden
            branch = grad_hidden.astype(BF16)
            branch_s[rows] = branch
            mix_ref[rows] = contract(branch, w_out, 1, 1).astype(BF16)
            parts = (branch.astype(F32), top, grad_norm * unit, grad_norm)
            total = [t + jnp.sum(p, 0, keepdims=True) for t, p in zip(total, parts)]
        sums_ref[...] = jnp.concatenate(total + [jnp.zeros_like(gain)] * 4, 0)
        length = attended[0].shape[1]
        grad_out = 0.0
        for c in range(groups):
            grad_out = grad_out + contract(attended[c][...], branch_s[c * length : (c + 1) * length], 1, 0)
        grad_out_ref[...] = grad_out.astype(BF16)


def back_specs(rows, width, half, tile):
    steps = half // tile
    column = lambda n: pl.BlockSpec((n, tile), lambda j, s: (0, s[0] * steps + j))
    ins = [fixed((width, rows)), fixed((rows, width))]
    ins += [pl.BlockSpec((tile, rows), lambda j, s: (s[0] * steps + j, 0)), column(rows), column(width)]
    ins.append(pl.BlockSpec((tile, width), lambda j, s: (s[0] * steps + j, 0)))
    outs = [
        pl.BlockSpec((tile, width), lambda j, s: (j, 0)),
        pl.BlockSpec((width, tile), lambda j, s: (0, j)),
        pl.BlockSpec((1, tile), lambda j, s: (0, j)),
    ]
    return ins, outs, [shaped((half, width), BF16), shaped((width, half), BF16), shaped((1, half), F32)]


def back_first(side, normed, cot, act, slope, w_up, w_down, tile, chunk):
    rows, width = cot.shape
    half = w_up.shape[1] // 2
    ins, outs, shapes = back_specs(rows, width, half, tile)
    return call(
        functools.partial(back_first_kernel, chunk=chunk),
        prefetch=1,
        grid=(half // tile,),
        in_specs=ins,
        out_specs=[fixed((rows, width))] + outs,
        out_shape=[shaped((rows, width), F32)] + shapes,
        scratch=[pltpu.VMEM((rows, tile), BF16)],
        flops=8 * rows * width * half,
        moved=8 * rows * width + 4 * rows * half + 8 * width * half,
    )(side, normed, cot, act, slope, w_up, w_down)


def back_last(side, attended, normed, cot, act, slope, w_up, w_down, w_out, gain, hidden, norm, tile, chunk):
    rows, width = cot.shape
    groups = len(attended)
    half = w_up.shape[1] // 2
    ins, outs, shapes = back_specs(rows, width, half, tile)
    whole = lambda n: fixed((n, width))
    return call(
        functools.partial(back_last_kernel, groups=groups, chunk=chunk),
        prefetch=1,
        grid=(half // tile,),
        in_specs=[fixed((width, rows // groups))] * groups + ins + [whole(width), whole(1)] + [cut_by_step(rows, width, half // tile)] * 2,
        out_specs=outs + [whole(rows), whole(rows), whole(width), whole(8)],
        out_shape=shapes
        + [shaped((rows, width), F32), shaped((rows, width), BF16), shaped((width, width), BF16), shaped((8, width), F32)],
        scratch=[
            pltpu.VMEM((rows, tile), BF16),
            pltpu.VMEM((rows, width), F32),
            pltpu.VMEM((rows, width), BF16),
            pltpu.VMEM((rows, width), F32),
        ],
        flops=8 * rows * width * half + 4 * rows * width * width,
        moved=20 * rows * width + 4 * rows * half + 8 * width * half,
    )(side, *attended, normed, cot, act, slope, w_up, w_down, w_out, gain, hidden, norm)


def joint_part(normed, grad_ref, grad_w_ref, bias_ref):
    length = normed[0].shape[1]
    grad_w = 0.0
    for c, normed_ref in enumerate(normed):
        grad_w = grad_w + contract(normed_ref[...], grad_ref[0, c * length : (c + 1) * length], 1, 0)
    grad_w_ref[...] = grad_w.astype(BF16)
    bias_ref[0] = jnp.sum(grad_ref[0].astype(F32), 0, keepdims=True)


def joint_first_kernel(side_ref, *refs, groups):
    normed, (grad_ref, weight_ref, grad_w_ref, bias_ref, acc_ref) = refs[:groups], refs[groups:]
    joint_part(normed, grad_ref, grad_w_ref, bias_ref)
    part = contract(grad_ref[0], weight_ref[...], 1, 1)

    @pl.when(pl.program_id(0) == 0)
    def _():
        acc_ref[...] = part

    @pl.when(pl.program_id(0) > 0)
    def _():
        acc_ref[...] += part


def joint_last_kernel(side_ref, *refs, groups, tm):
    normed, (grad_ref, weight_ref, acc_ref, grad_hidden_ref, gain_ref) = refs[:groups], refs[groups : groups + 5]
    refs = refs[groups + 5 :]
    filled, masks = refs[:groups], refs[groups : 2 * groups]
    (other_bias_ref, sums_ref, up_other_ref, up_own_ref, grad_out_ref, grad_w_ref, away_ref, kept_ref, *input_refs,
     acc_s, pos_s, bias_s, rest_ref, hidden_s, filled_s) = refs[2 * groups :]
    core, me = side_ref[0], side_ref[1]
    length, half = normed[0].shape[1], grad_w_ref.shape[1]
    step = pl.program_id(0)
    joint_part(normed, grad_ref, grad_w_ref, bias_s.at[pl.ds(step, 1)])

    @pl.when(step == 0)
    def _():
        acc_s[...] = contract(grad_ref[0], weight_ref[...], 1, 1)

    some = acc_ref.shape[1]
    columns = pl.ds(pl.multiple_of(step * some, some), some)
    acc_s[:, columns] += acc_ref[...]
    hidden_s[:, columns] = grad_hidden_ref[...]
    for c in range(groups):
        filled_s[c, :, columns] = filled[c][...]

    @pl.when(step == 1)
    def _():
        acc_s[...] += contract(grad_ref[0], weight_ref[...], 1, 1)

    @pl.when(step == 2)
    def _():
        gain = gain_ref[...].astype(F32)
        weight = weight_ref[...]
        total = [jnp.zeros_like(gain) for _ in range(3)]
        clips = [slice(c * length, (c + 1) * length) for c in range(groups)]
        grad_norms = [acc_s[rows] + contract(grad_ref[0, rows], weight, 1, 1) for rows in clips]
        for c, rows in enumerate(clips):
            grad_norm = grad_norms[c]
            unit, inverse = norm_parts(filled_s[c])
            grad_filled = hidden_s[rows] + norm_backward(grad_norm, unit, inverse, gain)
            masked = masks[c][...] > 0.5
            by_segment(input_refs, jnp.where(masked, 0.0, grad_filled).astype(BF16), c)
            parts = (grad_norm * unit, grad_norm, jnp.where(masked, grad_filled, 0.0))
            total = [t + jnp.sum(p, 0, keepdims=True) for t, p in zip(total, parts)]
            pos_s[...] = grad_filled if c == 0 else pos_s[...] + grad_filled
        seg = length // tm
        shares, share_rows, _ = rest_ref.shape
        pos_rows, some = length // shares, shares // tm
        for d in range(tm):
            own = pos_s[d * seg : (d + 1) * seg].reshape(some, pos_rows, pos_s.shape[1])
            rest_ref[pl.ds((me ^ d) * some, some), :pos_rows] = own.astype(BF16)

        def both(other, mine):
            return jnp.where(core == 0, jnp.concatenate([mine, other], 1), jnp.concatenate([other, mine], 1))

        width = gain.shape[1]
        up = both(up_other_ref[...], up_own_ref[...])
        sums = sums_ref[...]
        lines = [both(other_bias_ref[i], bias_s[i]) for i in (0, 2)] + [sums[0:1]]
        lines += [up[:, i * width : (i + 1) * width] for i in range(up.shape[1] // width)]
        lines += [sums[1:2], total[0], total[1], sums[2:3], sums[3:4], total[2]]
        lines.append(jnp.zeros((shares * (share_rows - pos_rows) - len(lines), width), F32))
        small = jnp.concatenate(lines, 0).reshape(shares, share_rows - pos_rows, width)
        rest_ref[:, pos_rows:] = small.astype(BF16)
        rest, grad_out = rest_ref[...], grad_out_ref[...]
        away_ref[...] = jnp.where(core == 1, grad_out, rest)
        kept_ref[...] = jnp.where(core == 1, rest, grad_out)


def joint_specs(groups, rows, width):
    half = width // 2
    return [fixed((width, rows // groups))] * groups + [
        pl.BlockSpec((1, rows, half), lambda i, s: (i, 0, 0)),
        pl.BlockSpec((width, half), lambda i, s: (0, 2 * i + s[0])),
    ]


def joint_first(side, normed, grads, w_qkv):
    _, rows, half = grads.shape
    groups, width = len(normed), 2 * half
    return call(
        functools.partial(joint_first_kernel, groups=groups),
        prefetch=1,
        share=4096,
        grid=(3,),
        in_specs=joint_specs(groups, rows, width),
        out_specs=[
            pl.BlockSpec((width, half), lambda i, s: (0, i)),
            pl.BlockSpec((1, 1, half), lambda i, s: (i, 0, 0)),
            fixed((rows, width)),
        ],
        out_shape=[shaped((width, 3 * half), BF16), shaped((3, 1, half), F32), shaped((rows, width), F32)],
        flops=6 * rows * width * width,
        moved=12 * rows * width,
    )(side, *normed, grads, w_qkv)


def joint_last(side, normed, grads, w_qkv, acc, grad_hidden, gain, filled, masks, bias, sums, up_other, up_own, grad_out, tm):
    shares = grad_out.shape[0]
    _, rows, half = grads.shape
    groups, width = len(normed), 2 * half
    length = rows // groups
    return call(
        functools.partial(joint_last_kernel, groups=groups, tm=tm),
        prefetch=1,
        share=4096,
        grid=(3,),
        in_specs=joint_specs(groups, rows, width)
        + [cut_by_step(rows, width, 3)] * 2
        + [fixed((1, width))]
        + [cut_by_step(length, width, 3)] * groups
        + [fixed((length, 1))] * groups
        + [fixed((3, 1, half)), fixed((8, width)), fixed(up_other.shape), fixed(up_own.shape)]
        + [fixed(grad_out.shape)],
        out_specs=[
            pl.BlockSpec((width, half), lambda i, s: (0, i)),
            fixed(grad_out.shape),
            fixed(grad_out.shape),
        ]
        + [fixed((groups, length // tm, width))] * tm,
        out_shape=[
            shaped((width, 3 * half), BF16),
            shaped(grad_out.shape, BF16),
            shaped(grad_out.shape, BF16),
        ]
        + [shaped((groups, length // tm, width), BF16)] * tm,
        scratch=[
            pltpu.VMEM((rows, width), F32),
            pltpu.VMEM((length, width), F32),
            pltpu.VMEM((3, 1, half), F32),
            pltpu.VMEM(grad_out.shape, BF16),
            pltpu.VMEM((rows, width), F32),
            pltpu.VMEM((groups, length, width), F32),
        ],
        flops=6 * rows * width * width,
        moved=24 * rows * width,
    )(side, *normed, grads, w_qkv, acc, grad_hidden, gain, *filled, *masks, bias, sums, up_other, up_own, grad_out)


def spot_bits(order, tm):
    return [bits_of(bit) if axis == "tm" else bits_of(tm) + bits_of(bit) - 1 for axis, bit in order]


def shares_of(here_ref, refs, orders, tm, place):
    away = place ^ here_ref[0]
    low = here_ref[1] == 0
    half = len(refs) // 2
    out = []
    for own_ref, other_ref, order in zip(refs[:half], refs[half:], orders):
        index = sum(((away >> b) & 1) << k for k, b in enumerate(spot_bits(order, tm)))
        own, other = own_ref[index], other_ref[index]
        out.append((jnp.where(low, own, other).astype(F32), jnp.where(low, other, own).astype(F32)))
    return out


def place_one_kernel(here_ref, *refs, orders, tm, some):
    down_ref, up_ref = refs[4:]
    width = down_ref.shape[2]
    for u in range(some):
        downs, ups = shares_of(here_ref, refs[:4], orders, tm, pl.program_id(0) * some + u)
        rows = ups[0].shape[0]
        for core in range(2):
            parts = downs[core].shape[1] // width
            for part in range(parts):
                at = (u * parts + part) * rows
                down_ref[core, at : at + rows] = downs[core][:, part * width : (part + 1) * width]
            columns = ups[core].shape[1]
            up_ref[u * rows : (u + 1) * rows, core * columns : (core + 1) * columns] = ups[core]


def place_two_kernel(here_ref, *refs, orders, tm, some):
    qkv_ref, out_ref, pos_ref, small_ref = refs[4:]
    width = out_ref.shape[1]
    half = width // 2
    pos_rows, small_rows = pos_ref.shape[0] // some, small_ref.shape[0] // some
    for u in range(some):
        lefts, rights = shares_of(here_ref, refs[:4], orders, tm, pl.program_id(0) * some + u)
        shares = [jnp.concatenate(sides, 1) for sides in zip(lefts, rights)]
        qkvs = [share[:, : 3 * half] for share in shares]
        out, rest = [share[:, 3 * half :] for share in shares]
        rows = slice(u * out.shape[0], (u + 1) * out.shape[0])
        for core in range(2):
            for i in range(3):
                at = i * width + core * half
                qkv_ref[rows, at : at + half] = qkvs[core][:, i * half : (i + 1) * half]
        out_ref[rows] = out
        pos_ref[u * pos_rows : (u + 1) * pos_rows] = rest[:pos_rows]
        small_ref[u * small_rows : (u + 1) * small_rows] = rest[pos_rows:]


def place(kernel, here, gathered, orders, tm, shapes):
    some = 4
    steps = gathered[0].shape[0] // some

    def cut(shape):
        block = shape[:-2] + (shape[-2] // steps, shape[-1])
        return pl.BlockSpec(block, lambda j, here: (0,) * (len(shape) - 2) + (j, 0))

    return call(
        functools.partial(kernel, orders=orders, tm=tm, some=some),
        prefetch=1,
        grid=(steps,),
        in_specs=[fixed(v.shape) for v in gathered],
        out_specs=[cut(s) for s in shapes],
        out_shape=[shaped(s, F32) for s in shapes],
        moved=sum(6 * v.size for v in gathered),
    )(here, *gathered)


def in_order(here, gathered, orders, tm):
    out = []
    half = len(gathered) // 2
    for own, other, order in zip(gathered[:half], gathered[half:], orders):
        bits = spot_bits(order, tm)
        away = jnp.arange(own.shape[0], dtype=jnp.int32) ^ here[0]
        index = sum(((away >> b) & 1) << k for k, b in enumerate(bits))
        own, other = (jnp.take(x, index, axis=0).astype(F32) for x in (own, other))
        low = here[1] == 0
        out.append(jnp.stack([jnp.where(low, own, other), jnp.where(low, other, own)]))
    return out


def bits_of(size):
    return size.bit_length() - 1


def axis_bits(axis):
    return [(axis, 1 << b) for b in range(bits_of(lax.axis_size(axis)))]


def own_bit(axis, bit):
    return (lax.axis_index(axis) // bit) % 2


def hop(value, axis, bit):
    size = lax.axis_size(axis)
    return lax.ppermute(value, axis, [(i, i ^ bit) for i in range(size)])


def tie(*values):
    return lax.optimization_barrier(values)


def take_clips(values):
    tm = lax.axis_size("tm")
    me = lax.axis_index("tm")
    out = []
    for d in range(tm):
        block = lax.dynamic_index_in_dim(values, me ^ d, 1, keepdims=False)
        out.append(hop(block, "tm", d) if d else block)
    return out


def send_clips(blocks):
    return [hop(block, "tm", d) if d else block for d, block in enumerate(blocks)]


def all_clips(blocks, shape):
    return jnp.stack(unshuffle(blocks), 1).reshape(shape)


def unshuffle(blocks):
    me = lax.axis_index("tm")
    blocks = list(blocks)
    for b in range(bits_of(len(blocks))):
        odd = ((me >> b) & 1) == 1
        blocks = [jnp.where(odd, blocks[i ^ (1 << b)], blocks[i]) for i in range(len(blocks))]
    return blocks


def add_low(a, b):
    return (a.astype(F32) + b.astype(F32)).astype(BF16)


def split_share(value):
    count = bits_of(lax.axis_size("clips")) + bits_of(lax.axis_size("tm")) - 1
    return value.reshape((2,) * count + (value.shape[0] >> count, value.shape[1]))


def side_by_side(value, parts):
    return jnp.concatenate(jnp.split(value, parts, -2), -1)


class Sum:
    def __init__(self, folds):
        self.folds = folds
        clip_bits, self.time_bits = axis_bits("clips")[1:], axis_bits("tm")
        self.names = clip_bits[::-1] + self.time_bits[::-1]
        self.orders = (clip_bits, clip_bits[1:] + clip_bits[:1])
        self.rounds = len(clip_bits) + len(self.time_bits)

    def half(self, pair, names, name, other):
        at = names.index(name)
        mine = own_bit(*name)
        pick = lambda x: lax.dynamic_index_in_dim(x, 1 - mine if other else mine, at, keepdims=False)
        return add_low(*(pick(x) for x in pair))

    def half_of_all(self, index, state, other):
        sides = len(self.orders[0])
        if index < sides:
            names = [[n for n in self.names if n not in order[:index]] for order in self.orders]
            return [self.half(p, n, order[index], other) for p, n, order in zip(state, names, self.orders)]
        names = self.time_bits[index - sides :]
        parts = [self.half(pair, names[::-1], names[0], other) for pair in state]
        if len(parts) > 1:
            parts = [side_by_side(x, n) if n > 1 else x for x, n in zip(parts, self.folds)]
        return [jnp.concatenate(parts, -1) if len(parts) > 1 else parts[0]]

    def split(self, index, state):
        return [(away,) for away in self.half_of_all(index, state, True)] + state

    def send(self, index, state):
        sides = len(self.orders[0])
        names = [o[index] for o in self.orders] if index < sides else [self.time_bits[index - sides]]
        away, state = state[: len(names)], state[len(names) :]
        got = [hop(x, *name) for (x,), name in zip(away, names)]
        return list(zip(self.half_of_all(index, state, False), got))

    def scatter(self, index, state):
        return self.send(index, self.split(index, state))

    def share(self, state):
        return add_low(*state[0])

    def gather_orders(self, at_once=False):
        return [self.time_bits[:: 1 if at_once else -1] + order[::-1] for order in self.orders]


    def split_all(self, state):
        tm, me = lax.axis_size("tm"), lax.axis_index("tm")

        def pick(x, d):
            return lax.dynamic_index_in_dim(x.reshape((tm,) + x.shape[-2:]), me ^ d, 0, keepdims=False)

        def part(d):
            parts = [add_low(*(pick(x, d) for x in pair)) for pair in state]
            return jnp.concatenate([side_by_side(x, n) if n > 1 else x for x, n in zip(parts, self.folds)], -1)

        return [(part(d),) for d in range(tm)]

    def send_all(self, state):
        return [tuple(hop(x, "tm", d) if d else x for d, (x,) in enumerate(state))]

    def share_all(self, state):
        return sum(x.astype(F32) for x in state[0]).astype(BF16)

    def gather_all(self, state):
        return [tuple(hop(state[0][0], "tm", d) if d else state[0][0] for d in range(lax.axis_size("tm")))]

    def join_all(self, state, cut):
        whole = jnp.stack(state[0])
        return [whole[..., :cut], whole[..., cut:]]

    def gather(self, index, state, cut):
        if index < len(self.time_bits):
            return [(state[0], hop(state[0], *self.time_bits[::-1][index]))]
        names = [order[::-1][index - len(self.time_bits)] for order in self.orders]
        return [(value, hop(value, *name)) for value, name in zip(state, names)]

    def join(self, index, state, cut):
        out = [jnp.concatenate(pair, 0) for pair in state]
        if index == len(self.time_bits) - 1:
            return [out[0][..., :cut], out[0][..., cut:]]
        return out


def on_device(
    patches, mask_index, mask_count, w_qkv, q_bias, v_bias, w_out, out_bias, w_up, up_bias,
    w_down, down_bias, norm1_scale, norm1_shift, norm2_scale, norm2_shift, mask_embed, pos_embed,
    cotangent,
):
    clip_count, seg, width = patches.shape
    ff = w_up.shape[1]
    tm = lax.axis_size("tm")
    me = lax.axis_index("tm")
    length = seg * tm
    groups = clip_count // tm
    by_group = (groups, tm, seg, width)
    tile, chunk = 512, 512

    arrived, grouped = [], patches.reshape(by_group)
    for g in range(groups):
        arrived.append(take_clips(grouped[g : g + 1]))
        grouped, *arrived[g] = tie(grouped, *arrived[g])
    tied, *arrived[-1] = tie(cotangent, *arrived[-1])
    cot = take_clips(tied.reshape(by_group))
    arrived = [[b[0] for b in blocks] for blocks in arrived]

    row = lambda x: x.reshape(1, -1)
    joint_bias = row(jnp.concatenate([q_bias, jnp.zeros_like(q_bias), v_bias]))
    out_bias, up_bias, down_bias, gain1, shift1, gain2, shift2, embed = map(
        row, (out_bias, up_bias, down_bias, norm1_scale, norm1_shift, norm2_scale, norm2_shift, mask_embed)
    )
    starts = (me ^ jnp.arange(tm, dtype=jnp.int32)) * seg
    places = (starts[:, None] + jnp.arange(seg, dtype=jnp.int32)[None, :]).reshape(length)
    pos = jnp.concatenate([lax.dynamic_slice_in_dim(pos_embed, (me ^ d) * seg, seg, 0) for d in range(tm)], 0)
    slots = jnp.arange(mask_index.shape[1], dtype=jnp.int32)
    masks = []
    for g in range(groups):
        index_row = lax.dynamic_index_in_dim(mask_index, g * tm + me, 0, keepdims=False)
        count = lax.dynamic_index_in_dim(mask_count, g * tm + me, 0, keepdims=False)
        hit = (places[:, None] == index_row[None, :]) & (slots < count)[None, :]
        masks.append(jnp.any(hit, axis=1, keepdims=True).astype(F32))

    filled, normed_one, joints, attended, turned, logs = [], [], [], [], [], []
    for g in range(groups):
        f, n, j = project(arrived[g], masks[g], embed, pos, gain1, shift1, w_qkv, joint_bias)
        a, a_turned, log_sum = attend(j, width)
        if g < groups - 1:
            a, *arrived[g + 1] = tie(a, *arrived[g + 1])
        else:
            a, cot[1] = tie(a, cot[1])
        for kept, value in zip((filled, normed_one, joints, attended, turned, logs), (f, n, j, a, a_turned, log_sum)):
            kept.append(value)

    core = own_bit("clips", 1).astype(jnp.int32)
    kept_side = jnp.stack([core, me.astype(jnp.int32)])
    away_side = jnp.stack([1 - core, me.astype(jnp.int32)])
    shares = lax.axis_size("clips") // 2 * tm
    here = jnp.stack([(lax.axis_index("clips") // 2 * tm + me).astype(jnp.int32), core])
    hidden, normed_two, act, slope, *block_out = forward(
        filled, attended, w_out, out_bias, gain2, shift2, down_bias, w_up, up_bias, w_down, 1024, 256, tm
    )
    block_out[0], *cot = tie(block_out[0], *cot)
    cot = jnp.concatenate(cot, 1).reshape(groups * length, width)
    norm_acc, down, up, up_sums_away = back_first(away_side, normed_two, cot, act, slope, w_up, w_down, tile, chunk)
    down_got, up_got = hop(down, "clips", 1), hop(up, "clips", 1)
    down, up, up_sums, grad_hidden, mix, grad_out, sums_two = back_last(
        kept_side, turned, normed_two, cot, act, slope, w_up, w_down, w_out, gain2, hidden, norm_acc, tile, chunk
    )
    one = Sum((2, 1))

    def after(values, *states):
        flat = [x for state in states for pair in state for x in pair]
        tied = list(tie(*values, *flat))
        values, flat = tied[: len(values)], tied[len(values) :]
        back = [[tuple(flat.pop(0) for _ in pair) for pair in state] for state in states]
        return (values, *back)

    state = [tuple(split_share(x) for x in pair) for pair in ((down, down_got), (up, up_got))]
    state = one.split(0, state)
    (mix, *block_out), state = after((mix, *block_out), state)
    state = one.send(0, state)
    block_out = send_clips(block_out)
    grads = attend_back(away_side, joints, mix, logs)
    qkv, bias_sums, acc = joint_first(away_side, normed_one, grads, w_qkv)
    qkv_got = hop(qkv, "clips", 1)
    sent_out = block_out
    (acc, sent_out[1], sent_out[2]), state = after((acc, sent_out[1], sent_out[2]), state)
    state = one.split(1, state)
    (mix, acc), state = after((mix, acc), state)
    state = one.send(1, state)
    grads = attend_back(kept_side, joints, mix, logs)
    (grads, *rest_out), state = after((grads, *sent_out[3:]), state)
    sent_out[3:] = rest_out
    state = one.split(2, state)
    (grads,), state = after((grads,), state)
    state = one.send(2, state)
    qkv, rest_away, rest_kept, *input_grad = joint_last(
        kept_side, normed_one, grads, w_qkv, acc, grad_hidden, gain1, filled, masks, bias_sums, sums_two,
        up_sums_away, up_sums, grad_out.reshape(shares, width // shares, width), tm
    )
    (qkv, rest_away, rest_kept, *input_grad), state = after((qkv, rest_away, rest_kept, *input_grad), state)
    rest_away, rest_kept = rest_away.reshape(width, width), rest_kept.reshape(width, width)
    rest_got = hop(rest_away, "clips", 1)
    two = Sum((1, 1))
    pairs = [tuple(split_share(x) for x in pair) for pair in ((qkv, qkv_got), (rest_kept, rest_got))]
    cut_one, cut_two = ff // 2, -(-5 * width // 4 // LANES) * LANES
    share_rows = pairs[0][0].shape[-2]

    def scatter_steps(group, first):
        steps = [lambda s, i=i: group.split(i, s) for i in range(first, group.rounds)]
        return [(split, lambda s, i=i: group.send(i, s)) for i, split in zip(range(first, group.rounds), steps)]

    def gather_steps(group, cut):
        def prepare(i):
            if i == 0:
                return lambda s: [(group.share(s)[None],)]
            return lambda s: [(x,) for x in group.join(i - 1, s, cut)]

        return [
            (prepare(i), lambda s, i=i: group.gather(i, [x for (x,) in s], cut)) for i in range(group.rounds)
        ]

    def core_steps(group, cut):
        return [
            (
                lambda s: [(x,) for x in group.join(group.rounds - 1, s, cut)],
                lambda s: [(x, hop(x, "clips", 1)) for (x,) in s],
            )
        ]

    steps_one = scatter_steps(one, 3)
    turn = len(steps_one) - 1
    back_one = gather_steps(one, cut_one)
    steps_one += back_one[1:] + [None] + core_steps(one, cut_one)
    along = len(two.time_bits)
    steps_two = scatter_steps(two, 0)[:-along]
    steps_two.append((two.split_all, two.send_all))
    steps_two.append((lambda s: [(two.share_all(s),)], two.gather_all))
    back_two = gather_steps(two, cut_two)[along:]
    steps_two.append((lambda s: [(x,) for x in two.join_all(s, cut_two)], back_two[0][1]))
    steps_two += back_two[1:] + core_steps(two, cut_two)
    outputs = []
    for index in range(max(len(steps_one), len(steps_two))):
        if index == 2:
            block_out = all_clips(sent_out, patches.shape)
            (block_out,), state, pairs = after((block_out,), state, pairs)
        if index == len(steps_two) - 2:
            sent[1:3], state, pairs = after(sent[1:3], state, pairs)
        if index == len(steps_two) - 1:
            tied, pairs = after((*sent[3:], *outputs), pairs)
            sent[3:], outputs = tied[: len(sent) - 3], tied[len(sent) - 3 :]
        active = [steps[index] if index < len(steps) else None for steps in (steps_one, steps_two)]
        states = [step[0](x) if step else x for step, x in zip(active, (state, pairs))]
        live = [x for x, step in zip(states, active) if step]
        if index == 3:
            input_grad, *live = after(input_grad, *live)
            sent = send_clips(input_grad)
        elif index:
            _, *live = after((), *live)
        live = iter(live)
        state, pairs = (step[1](next(live)) if step else x for step, x in zip(active, states))
        if index == turn:
            state = back_one[0][1](back_one[0][0](state))
        if index == len(steps_one) - 1:
            one_all = [own for own, _ in state] + [other for _, other in state]
            if share_rows % 8 == 0:
                outputs = place(
                    place_one_kernel, here, one_all, one.gather_orders(), tm, ((2, ff // 2, width), (width, ff))
                )
    two_all = [own for own, _ in pairs] + [other for _, other in pairs]
    input_grad = all_clips(sent, patches.shape)

    orders_one, orders_two = one.gather_orders(), two.gather_orders(True)
    if share_rows % 8 == 0:
        down_sum, up_sum = outputs
        shapes = ((width, 3 * width), (width, width), (length, width), (width - length, width))
        qkv_sum, out_sum, pos_sum, small = place(place_two_kernel, here, two_all, orders_two, tm, shapes)
        down_sum = down_sum.reshape(ff, width)
    else:
        downs, ups = in_order(here, one_all, orders_one, tm)
        both = jnp.concatenate(in_order(here, two_all, orders_two, tm), -1)
        qkvs, rests = both[..., : 3 * width // 2], both[..., 3 * width // 2 :]
        down_sum = jnp.stack(jnp.split(downs, 2, -1), 2).reshape(ff, width)
        up_sum = jnp.concatenate(list(ups.reshape(2, width, ff // 2)), 1)
        qkv_sum = jnp.stack(list(qkvs.reshape(2, width, 3, width // 2)), 2).reshape(width, 3 * width)
        out_sum, rest = rests[0].reshape(width, width), rests[1]
        pos_sum = rest[:, : length // shares].reshape(length, width)
        small = rest[:, length // shares :].reshape(width - length, width)
    v = []
    at = 0
    for n in (1, 1, 1, ff // width, 1, 1, 1, 1, 1, 1):
        v.append(small[at : at + n].reshape(-1))
        at += n
    return (block_out, input_grad, qkv_sum, v[0], v[1], out_sum, v[2], up_sum, v[3], down_sum, v[4],
            v[5], v[6], v[7], v[8], v[9], pos_sum)


def solution(mesh):
    rows = P("clips", "tm", None)
    in_specs = (rows, P("clips", None), P("clips")) + (P(),) * 15 + (rows,)
    out_specs = (rows, rows) + (P(),) * 15
    return jax.shard_map(on_device, mesh=mesh, in_specs=in_specs, out_specs=out_specs, check_vma=False)
```

```python
import functools

import jax
import jax.numpy as jnp
from jax import lax
from jax.experimental import pallas as pl
from jax.experimental.pallas import tpu as pltpu
from jax.sharding import PartitionSpec as P

HEADS = 12
LANES = 128
NORM_EPS = 1e-06
ROOT_HALF = 0.7071067811865476
ROOT_TWO_PI = 2.5066282746310002
LOG2_E = 1.4426950408889634
F32 = jnp.float32
BF16 = jnp.bfloat16
VMEM_LIMIT = 60 * 2**20


def contract(a, b, da, db):
    return lax.dot_general(a, b, (((da,), (db,)), ((), ())), preferred_element_type=F32)


def call(kernel, *, grid, in_specs, out_specs, out_shape, scratch=(), prefetch=0, flops=0, moved=0, exps=0, share=1):
    return pl.pallas_call(
        kernel,
        grid_spec=pltpu.PrefetchScalarGridSpec(
            num_scalar_prefetch=prefetch,
            grid=grid,
            in_specs=in_specs,
            out_specs=out_specs,
            scratch_shapes=scratch,
        ),
        out_shape=out_shape,
        cost_estimate=pl.CostEstimate(
            flops=int(flops) // share, bytes_accessed=int(moved) // share, transcendentals=int(exps) // share
        ),
        compiler_params=pltpu.CompilerParams(vmem_limit_bytes=VMEM_LIMIT),
    )


def fixed(shape):
    return pl.BlockSpec(shape, lambda *_: (0,) * len(shape), pipeline_mode=pl.Buffered(1))


def shaped(shape, dtype):
    return jax.ShapeDtypeStruct(shape, dtype)


def norm_parts(values):
    centred = values - jnp.mean(values, -1, keepdims=True)
    spread = jnp.mean(centred * centred, -1, keepdims=True)
    inverse = lax.rsqrt(spread + NORM_EPS)
    return centred * inverse, inverse


def norm_backward(grad_norm, unit, inverse, gains):
    scaled = grad_norm * gains
    return inverse * (
        scaled
        - jnp.mean(scaled, -1, keepdims=True)
        - unit * jnp.mean(scaled * unit, -1, keepdims=True)
    )


def project_kernel(*refs, tm):
    blocks = refs[:tm]
    mask_ref, embed_ref, pos_ref, gain_ref, shift_ref, w_ref, bias_ref, filled_ref, turned_ref, joint_ref, normed_s = refs[tm:]

    @pl.when(pl.program_id(0) == 0)
    def _():
        seg = blocks[0].shape[0]
        embed, gain, shift = (r[...].astype(F32) for r in (embed_ref, gain_ref, shift_ref))
        for d in range(tm):
            rows = slice(d * seg, (d + 1) * seg)
            filled = jnp.where(mask_ref[rows] > 0.5, embed, blocks[d][...].astype(F32)) + pos_ref[rows].astype(F32)
            unit, _ = norm_parts(filled)
            normed = (unit * gain + shift).astype(BF16)
            filled_ref[rows] = filled
            normed_s[rows] = normed
            turned_ref[:, rows] = normed.T

    joint_ref[...] = (contract(normed_s[...], w_ref[...], 1, 0) + bias_ref[...].astype(F32)).astype(BF16)


def project(blocks, mask, embed, pos, gain, shift, w_qkv, bias):
    tm = len(blocks)
    seg, width = blocks[0].shape
    rows = tm * seg
    return call(
        functools.partial(project_kernel, tm=tm),
        grid=(3,),
        in_specs=[fixed((seg, width))] * tm
        + [fixed((rows, 1)), fixed((1, width)), fixed((rows, width)), fixed((1, width)), fixed((1, width))]
        + [pl.BlockSpec((width, width), lambda j: (0, j)), pl.BlockSpec((1, width), lambda j: (0, j))],
        out_specs=[
            pl.BlockSpec((rows, width), lambda j: (0, 0)),
            pl.BlockSpec((width, rows), lambda j: (0, 0)),
            pl.BlockSpec((rows, width), lambda j: (0, j)),
        ],
        out_shape=[shaped((rows, width), F32), shaped((width, rows), BF16), shaped((rows, 3 * width), BF16)],
        scratch=[pltpu.VMEM((rows, width), BF16)],
        flops=6 * rows * width * width,
        moved=20 * rows * width,
    )(*blocks, mask, embed, pos, gain, shift, w_qkv, bias)


def own_lanes(value, i, head):
    lane = lax.broadcasted_iota(jnp.int32, value.shape, 1)
    return jnp.where((lane >= i * head) & (lane < (i + 1) * head), value, jnp.zeros_like(value))


def attend_kernel(q_ref, k_ref, v_ref, o_ref, turned_ref, log_ref, *, head):
    factor = head**-0.5 * LOG2_E
    per = LANES // head
    pairs = [slice(at, at + LANES) for at in range(0, q_ref.shape[1], LANES)]
    scores = [[contract(k_ref[:, n], own_lanes(q_ref[:, n], i, head), 1, 1) for i in range(per)] for n in pairs]
    for pair, lanes in enumerate(pairs):
        outs = []
        for i in range(per):
            peak = jnp.max(scores[pair][i], 0, keepdims=True)
            raised = jnp.exp2((scores[pair][i] - peak) * factor)
            total = jnp.sum(raised, 0, keepdims=True)
            mixed = contract(v_ref[:, lanes], raised.astype(BF16), 0, 0)
            outs.append(mixed[i * head : (i + 1) * head] * (1.0 / total))
            log_ref[pair, i : i + 1, :] = peak * factor + jnp.log2(total)
        turned = jnp.concatenate(outs, 0)
        turned_ref[lanes] = turned.astype(BF16)
        o_ref[:, lanes] = turned.T.astype(BF16)


def attend(joint, width):
    rows = joint.shape[0]
    head = width // HEADS
    pairs, per = width // LANES, LANES // head
    some = 2 if pairs % 2 == 0 else 1
    steps = pairs // some
    block = lambda off: pl.BlockSpec((rows, some * LANES), lambda h: (0, h + off))
    return call(
        functools.partial(attend_kernel, head=head),
        grid=(steps,),
        in_specs=[block(0), block(steps), block(2 * steps)],
        out_specs=[
            block(0),
            pl.BlockSpec((some * LANES, rows), lambda h: (h, 0)),
            pl.BlockSpec((some, per, rows), lambda h: (h, 0, 0)),
        ],
        out_shape=[shaped((rows, width), BF16), shaped((width, rows), BF16), shaped((pairs, per, rows), F32)],
        flops=16 * rows * rows * width,
        moved=8 * rows * width,
        exps=rows * rows * HEADS,
    )(joint, joint, joint)


def attend_back_kernel(side_ref, *refs, head, groups):
    per_clip = [refs[4 * c : 4 * c + 4] for c in range(groups)]
    g_ref, out_ref = refs[4 * groups :]
    scale = head**-0.5
    length = per_clip[0][0].shape[0]
    per = LANES // head
    ahead = []
    for c, (q_ref, k_ref, v_ref, log_ref) in enumerate(per_clip):
        rows = slice(c * length, (c + 1) * length)
        for i in range(per):
            q_own, g_own = own_lanes(q_ref[...], i, head), own_lanes(g_ref[rows], i, head)
            ahead.append((q_own, g_own, contract(k_ref[...], q_own, 1, 1), contract(v_ref[...], g_own, 1, 1)))
    for c, (q_ref, k_ref, v_ref, log_ref) in enumerate(per_clip):
        rows = slice(c * length, (c + 1) * length)
        grad_q, grad_k, grad_v = [], 0.0, 0.0
        for i in range(per):
            q_own, g_own, scores, grad_probs = ahead[c * per + i]
            probs = jnp.exp2(scores * (scale * LOG2_E) - log_ref[0, i : i + 1, :])
            delta = jnp.sum(probs * grad_probs, 0, keepdims=True)
            grad_scores = (probs * (grad_probs - delta)).astype(BF16)
            grad_v = grad_v + contract(probs.astype(BF16), g_own, 1, 0)
            grad_q.append(contract(k_ref[...], grad_scores, 0, 0)[i * head : (i + 1) * head])
            grad_k = grad_k + contract(grad_scores, q_own, 1, 0)
        out_ref[0, rows] = (jnp.concatenate(grad_q, 0) * scale).T.astype(BF16)
        out_ref[1, rows] = (grad_k * scale).astype(BF16)
        out_ref[2, rows] = grad_v.astype(BF16)


def attend_back(side, joints, mix, logs):
    rows, width = mix.shape
    groups = len(joints)
    length = rows // groups
    head = width // HEADS
    pairs, per = width // LANES, LANES // head
    half = pairs // 2

    def block(off):
        return pl.BlockSpec((length, LANES), lambda h, s: (0, off + s[0] * half + h))

    clip = [block(0), block(pairs), block(2 * pairs), pl.BlockSpec((1, per, length), lambda h, s: (s[0] * half + h, 0, 0))]
    operands = []
    for joint, log_sum in zip(joints, logs):
        operands += [joint, joint, joint, log_sum]
    return call(
        functools.partial(attend_back_kernel, head=head, groups=groups),
        prefetch=1,
        share=4096,
        grid=(half,),
        in_specs=clip * groups + [pl.BlockSpec((rows, LANES), lambda h, s: (0, s[0] * half + h))],
        out_specs=pl.BlockSpec((3, rows, LANES), lambda h, s: (0, 0, h)),
        out_shape=shaped((3, rows, width // 2), BF16),
        flops=20 * rows * length * width,
        moved=8 * rows * width,
        exps=rows * length * HEADS // 2,
    )(side, *operands, mix)


def gelu_parts(u):
    phi = 0.5 * (1.0 + lax.erf(u * ROOT_HALF))
    return u * phi, phi + u * jnp.exp(-0.5 * u * u) * (1.0 / ROOT_TWO_PI)


def by_segment(refs, values, clip=None):
    clips, seg, _ = refs[0].shape
    for c in range(clips) if clip is None else (clip,):
        for d, ref in enumerate(refs):
            at = ((0 if clip is not None else c) * len(refs) + d) * seg
            ref[c] = values[at : at + seg]


def forward_kernel(*refs, groups, chunk):
    filled, attended = refs[:groups], refs[groups : 2 * groups]
    (w_out_ref, out_bias_ref, gain_ref, shift_ref, down_bias_ref, w_up_ref, up_bias_ref, w_down_ref,
     hidden_ref, turned_ref, act_ref, slope_ref, *block_refs, out_s, normed_s, hidden_s) = refs[2 * groups :]
    rows_all = out_s.shape[0]
    step, last = pl.program_id(0), pl.num_programs(0) - 1

    @pl.when(step == 0)
    def _():
        gain, shift = gain_ref[...].astype(F32), shift_ref[...].astype(F32)
        out_bias, down_bias = out_bias_ref[...].astype(F32), down_bias_ref[...].astype(F32)
        length = filled[0].shape[0]
        for c in range(groups):
            rows = slice(c * length, (c + 1) * length)
            hidden = filled[c][...] + contract(attended[c][...], w_out_ref[...], 1, 0) + out_bias
            unit, _ = norm_parts(hidden)
            normed = (unit * gain + shift).astype(BF16)
            hidden_s[rows] = hidden
            normed_s[rows] = normed
            turned_ref[:, rows] = normed.T
            out_s[rows] = hidden + down_bias

    w_up, w_down = w_up_ref[...], w_down_ref[...]
    bias = up_bias_ref[...].astype(F32)
    some = hidden_ref.shape[1]
    hidden_ref[...] = hidden_s[:, pl.ds(pl.multiple_of(step * some, some), some)]
    chunks = [slice(at, at + chunk) for at in range(0, rows_all, chunk)]
    ahead = [contract(normed_s[rows], w_up, 1, 0) for rows in chunks]
    for rows, up in zip(chunks, ahead):
        value, slope = gelu_parts(up + bias)
        act = value.astype(BF16)
        act_ref[:, rows] = act.T
        slope_ref[rows] = slope.astype(BF16)
        out_s[rows] += contract(act, w_down, 1, 0)

    @pl.when(step == last)
    def _():
        by_segment(block_refs, out_s[...].astype(BF16))


def forward(filled, attended, w_out, out_bias, gain, shift, down_bias, w_up, up_bias, w_down, tile, chunk, tm):
    groups, (length, width) = len(filled), filled[0].shape
    rows, ff = groups * length, w_up.shape[1]
    vec = fixed((1, width))
    column = pl.BlockSpec((rows, tile), lambda j: (0, j))
    return call(
        functools.partial(forward_kernel, groups=groups, chunk=chunk),
        grid=(ff // tile,),
        in_specs=[fixed((length, width))] * (2 * groups)
        + [fixed((width, width)), vec, vec, vec, vec]
        + [
            pl.BlockSpec((width, tile), lambda j: (0, j)),
            pl.BlockSpec((1, tile), lambda j: (0, j)),
            pl.BlockSpec((tile, width), lambda j: (j, 0)),
        ],
        out_specs=[cut_by_step(rows, width, ff // tile), fixed((width, rows)), pl.BlockSpec((tile, rows), lambda j: (j, 0)), column]
        + [fixed((groups, length // tm, width))] * tm,
        out_shape=[shaped((rows, width), F32), shaped((width, rows), BF16)]
        + [shaped((ff, rows), BF16), shaped((rows, ff), BF16)]
        + [shaped((groups, length // tm, width), BF16)] * tm,
        scratch=[pltpu.VMEM((rows, width), F32), pltpu.VMEM((rows, width), BF16), pltpu.VMEM((rows, width), F32)],
        flops=4 * rows * width * ff + 2 * rows * width * width,
        moved=14 * rows * width + 4 * rows * ff + 4 * width * ff,
        exps=rows * ff,
    )(*filled, *attended, w_out, out_bias, gain, shift, down_bias, w_up, up_bias, w_down)


def cut_by_step(rows, width, steps):
    return pl.BlockSpec((rows, width // steps), lambda j, *_: (0, j))


def tile_back(turned_ref, cot_ref, act_ref, slope_ref, w_up_ref, w_down_ref, gup_s, norm_s, down_ref, up_ref, bias_ref, chunk):
    w_up, w_down = w_up_ref[...], w_down_ref[...]
    total = jnp.zeros(bias_ref.shape, F32)
    chunks = [slice(at, at + chunk) for at in range(0, cot_ref.shape[0], chunk)]
    ahead = [contract(cot_ref[rows], w_down, 1, 1) for rows in chunks]
    down_ref[...] = contract(act_ref[...], cot_ref[...], 1, 0).astype(BF16)
    for rows, grad_act in zip(chunks, ahead):
        gup = (grad_act * slope_ref[rows].astype(F32)).astype(BF16)
        gup_s[rows] = gup
        total = total + jnp.sum(gup.astype(F32), 0, keepdims=True)
        norm_s[rows] += contract(gup, w_up, 1, 1)
    bias_ref[...] = total
    up_ref[...] = contract(turned_ref[...], gup_s[...], 1, 0).astype(BF16)


def back_first_kernel(side_ref, turned_ref, cot_ref, act_ref, slope_ref, w_up_ref, w_down_ref, norm_ref, down_ref, up_ref, bias_ref, gup_s, *, chunk):
    @pl.when(pl.program_id(0) == 0)
    def _():
        norm_ref[...] = jnp.zeros_like(norm_ref)

    tile_back(turned_ref, cot_ref, act_ref, slope_ref, w_up_ref, w_down_ref, gup_s, norm_ref, down_ref, up_ref, bias_ref, chunk)


def back_last_kernel(side_ref, *refs, groups, chunk):
    attended = refs[:groups]
    (turned_ref, cot_ref, act_ref, slope_ref, w_up_ref, w_down_ref, w_out_ref, gain_ref, hidden_ref, norm_ref,
     down_ref, up_ref, bias_ref, grad_hidden_ref, mix_ref, grad_out_ref, sums_ref, gup_s, norm_s, branch_s, hidden_s) = refs[groups:]

    @pl.when(pl.program_id(0) == 0)
    def _():
        norm_s[...] = jnp.zeros_like(norm_s)

    columns = pl.ds(pl.multiple_of(pl.program_id(0) * norm_ref.shape[1], norm_ref.shape[1]), norm_ref.shape[1])
    hidden_s[:, columns] = hidden_ref[...]
    norm_s[:, columns] += norm_ref[...]
    tile_back(turned_ref, cot_ref, act_ref, slope_ref, w_up_ref, w_down_ref, gup_s, norm_s, down_ref, up_ref, bias_ref, chunk)

    @pl.when(pl.program_id(0) == pl.num_programs(0) - 1)
    def _():
        gain = gain_ref[...].astype(F32)
        total = [jnp.zeros_like(gain) for _ in range(4)]
        w_out = w_out_ref[...]
        for r in range(norm_s.shape[0] // chunk):
            rows = slice(r * chunk, (r + 1) * chunk)
            unit, inverse = norm_parts(hidden_s[rows])
            top, grad_norm = cot_ref[rows].astype(F32), norm_s[rows]
            grad_hidden = top + norm_backward(grad_norm, unit, inverse, gain)
            grad_hidden_ref[rows] = grad_hidden
            branch = grad_hidden.astype(BF16)
            branch_s[rows] = branch
            mix_ref[rows] = contract(branch, w_out, 1, 1).astype(BF16)
            parts = (branch.astype(F32), top, grad_norm * unit, grad_norm)
            total = [t + jnp.sum(p, 0, keepdims=True) for t, p in zip(total, parts)]
        sums_ref[...] = jnp.concatenate(total + [jnp.zeros_like(gain)] * 4, 0)
        length = attended[0].shape[1]
        grad_out = 0.0
        for c in range(groups):
            grad_out = grad_out + contract(attended[c][...], branch_s[c * length : (c + 1) * length], 1, 0)
        grad_out_ref[...] = grad_out.astype(BF16)


def back_specs(rows, width, half, tile):
    steps = half // tile
    column = lambda n: pl.BlockSpec((n, tile), lambda j, s: (0, s[0] * steps + j))
    ins = [fixed((width, rows)), fixed((rows, width))]
    ins += [pl.BlockSpec((tile, rows), lambda j, s: (s[0] * steps + j, 0)), column(rows), column(width)]
    ins.append(pl.BlockSpec((tile, width), lambda j, s: (s[0] * steps + j, 0)))
    outs = [
        pl.BlockSpec((tile, width), lambda j, s: (j, 0)),
        pl.BlockSpec((width, tile), lambda j, s: (0, j)),
        pl.BlockSpec((1, tile), lambda j, s: (0, j)),
    ]
    return ins, outs, [shaped((half, width), BF16), shaped((width, half), BF16), shaped((1, half), F32)]


def back_first(side, normed, cot, act, slope, w_up, w_down, tile, chunk):
    rows, width = cot.shape
    half = w_up.shape[1] // 2
    ins, outs, shapes = back_specs(rows, width, half, tile)
    return call(
        functools.partial(back_first_kernel, chunk=chunk),
        prefetch=1,
        grid=(half // tile,),
        in_specs=ins,
        out_specs=[fixed((rows, width))] + outs,
        out_shape=[shaped((rows, width), F32)] + shapes,
        scratch=[pltpu.VMEM((rows, tile), BF16)],
        flops=8 * rows * width * half,
        moved=8 * rows * width + 4 * rows * half + 8 * width * half,
    )(side, normed, cot, act, slope, w_up, w_down)


def back_last(side, attended, normed, cot, act, slope, w_up, w_down, w_out, gain, hidden, norm, tile, chunk):
    rows, width = cot.shape
    groups = len(attended)
    half = w_up.shape[1] // 2
    ins, outs, shapes = back_specs(rows, width, half, tile)
    whole = lambda n: fixed((n, width))
    return call(
        functools.partial(back_last_kernel, groups=groups, chunk=chunk),
        prefetch=1,
        grid=(half // tile,),
        in_specs=[fixed((width, rows // groups))] * groups + ins + [whole(width), whole(1)] + [cut_by_step(rows, width, half // tile)] * 2,
        out_specs=outs + [whole(rows), whole(rows), whole(width), whole(8)],
        out_shape=shapes
        + [shaped((rows, width), F32), shaped((rows, width), BF16), shaped((width, width), BF16), shaped((8, width), F32)],
        scratch=[
            pltpu.VMEM((rows, tile), BF16),
            pltpu.VMEM((rows, width), F32),
            pltpu.VMEM((rows, width), BF16),
            pltpu.VMEM((rows, width), F32),
        ],
        flops=8 * rows * width * half + 4 * rows * width * width,
        moved=20 * rows * width + 4 * rows * half + 8 * width * half,
    )(side, *attended, normed, cot, act, slope, w_up, w_down, w_out, gain, hidden, norm)


def joint_part(normed, grad_ref, grad_w_ref, bias_ref):
    length = normed[0].shape[1]
    grad_w = 0.0
    for c, normed_ref in enumerate(normed):
        grad_w = grad_w + contract(normed_ref[...], grad_ref[0, c * length : (c + 1) * length], 1, 0)
    grad_w_ref[...] = grad_w.astype(BF16)
    bias_ref[0] = jnp.sum(grad_ref[0].astype(F32), 0, keepdims=True)


def joint_first_kernel(side_ref, *refs, groups):
    normed, (grad_ref, weight_ref, grad_w_ref, bias_ref, acc_ref) = refs[:groups], refs[groups:]
    joint_part(normed, grad_ref, grad_w_ref, bias_ref)
    part = contract(grad_ref[0], weight_ref[...], 1, 1)

    @pl.when(pl.program_id(0) == 0)
    def _():
        acc_ref[...] = part

    @pl.when(pl.program_id(0) > 0)
    def _():
        acc_ref[...] += part


def joint_last_kernel(side_ref, *refs, groups, tm):
    normed, (grad_ref, weight_ref, acc_ref, grad_hidden_ref, gain_ref) = refs[:groups], refs[groups : groups + 5]
    refs = refs[groups + 5 :]
    filled, masks = refs[:groups], refs[groups : 2 * groups]
    (other_bias_ref, sums_ref, up_other_ref, up_own_ref, grad_out_ref, grad_w_ref, away_ref, kept_ref, *input_refs,
     acc_s, pos_s, bias_s, rest_ref, hidden_s, filled_s) = refs[2 * groups :]
    core, me = side_ref[0], side_ref[1]
    length, half = normed[0].shape[1], grad_w_ref.shape[1]
    step = pl.program_id(0)
    joint_part(normed, grad_ref, grad_w_ref, bias_s.at[pl.ds(step, 1)])

    @pl.when(step == 0)
    def _():
        acc_s[...] = contract(grad_ref[0], weight_ref[...], 1, 1)

    some = acc_ref.shape[1]
    columns = pl.ds(pl.multiple_of(step * some, some), some)
    acc_s[:, columns] += acc_ref[...]
    hidden_s[:, columns] = grad_hidden_ref[...]
    for c in range(groups):
        filled_s[c, :, columns] = filled[c][...]

    @pl.when(step == 1)
    def _():
        acc_s[...] += contract(grad_ref[0], weight_ref[...], 1, 1)

    @pl.when(step == 2)
    def _():
        gain = gain_ref[...].astype(F32)
        weight = weight_ref[...]
        total = [jnp.zeros_like(gain) for _ in range(3)]
        clips = [slice(c * length, (c + 1) * length) for c in range(groups)]
        grad_norms = [acc_s[rows] + contract(grad_ref[0, rows], weight, 1, 1) for rows in clips]
        for c, rows in enumerate(clips):
            grad_norm = grad_norms[c]
            unit, inverse = norm_parts(filled_s[c])
            grad_filled = hidden_s[rows] + norm_backward(grad_norm, unit, inverse, gain)
            masked = masks[c][...] > 0.5
            by_segment(input_refs, jnp.where(masked, 0.0, grad_filled).astype(BF16), c)
            parts = (grad_norm * unit, grad_norm, jnp.where(masked, grad_filled, 0.0))
            total = [t + jnp.sum(p, 0, keepdims=True) for t, p in zip(total, parts)]
            pos_s[...] = grad_filled if c == 0 else pos_s[...] + grad_filled
        seg = length // tm
        shares, share_rows, _ = rest_ref.shape
        pos_rows, some = length // shares, shares // tm
        for d in range(tm):
            own = pos_s[d * seg : (d + 1) * seg].reshape(some, pos_rows, pos_s.shape[1])
            rest_ref[pl.ds((me ^ d) * some, some), :pos_rows] = own.astype(BF16)

        def both(other, mine):
            return jnp.where(core == 0, jnp.concatenate([mine, other], 1), jnp.concatenate([other, mine], 1))

        width = gain.shape[1]
        up = both(up_other_ref[...], up_own_ref[...])
        sums = sums_ref[...]
        lines = [both(other_bias_ref[i], bias_s[i]) for i in (0, 2)] + [sums[0:1]]
        lines += [up[:, i * width : (i + 1) * width] for i in range(up.shape[1] // width)]
        lines += [sums[1:2], total[0], total[1], sums[2:3], sums[3:4], total[2]]
        lines.append(jnp.zeros((shares * (share_rows - pos_rows) - len(lines), width), F32))
        small = jnp.concatenate(lines, 0).reshape(shares, share_rows - pos_rows, width)
        rest_ref[:, pos_rows:] = small.astype(BF16)
        rest, grad_out = rest_ref[...], grad_out_ref[...]
        away_ref[...] = jnp.where(core == 1, grad_out, rest)
        kept_ref[...] = jnp.where(core == 1, rest, grad_out)


def joint_specs(groups, rows, width):
    half = width // 2
    return [fixed((width, rows // groups))] * groups + [
        pl.BlockSpec((1, rows, half), lambda i, s: (i, 0, 0)),
        pl.BlockSpec((width, half), lambda i, s: (0, 2 * i + s[0])),
    ]


def joint_first(side, normed, grads, w_qkv):
    _, rows, half = grads.shape
    groups, width = len(normed), 2 * half
    return call(
        functools.partial(joint_first_kernel, groups=groups),
        prefetch=1,
        share=4096,
        grid=(3,),
        in_specs=joint_specs(groups, rows, width),
        out_specs=[
            pl.BlockSpec((width, half), lambda i, s: (0, i)),
            pl.BlockSpec((1, 1, half), lambda i, s: (i, 0, 0)),
            fixed((rows, width)),
        ],
        out_shape=[shaped((width, 3 * half), BF16), shaped((3, 1, half), F32), shaped((rows, width), F32)],
        flops=6 * rows * width * width,
        moved=12 * rows * width,
    )(side, *normed, grads, w_qkv)


def joint_last(side, normed, grads, w_qkv, acc, grad_hidden, gain, filled, masks, bias, sums, up_other, up_own, grad_out, tm):
    shares = grad_out.shape[0]
    _, rows, half = grads.shape
    groups, width = len(normed), 2 * half
    length = rows // groups
    return call(
        functools.partial(joint_last_kernel, groups=groups, tm=tm),
        prefetch=1,
        share=4096,
        grid=(3,),
        in_specs=joint_specs(groups, rows, width)
        + [cut_by_step(rows, width, 3)] * 2
        + [fixed((1, width))]
        + [cut_by_step(length, width, 3)] * groups
        + [fixed((length, 1))] * groups
        + [fixed((3, 1, half)), fixed((8, width)), fixed(up_other.shape), fixed(up_own.shape)]
        + [fixed(grad_out.shape)],
        out_specs=[
            pl.BlockSpec((width, half), lambda i, s: (0, i)),
            fixed(grad_out.shape),
            fixed(grad_out.shape),
        ]
        + [fixed((groups, length // tm, width))] * tm,
        out_shape=[
            shaped((width, 3 * half), BF16),
            shaped(grad_out.shape, BF16),
            shaped(grad_out.shape, BF16),
        ]
        + [shaped((groups, length // tm, width), BF16)] * tm,
        scratch=[
            pltpu.VMEM((rows, width), F32),
            pltpu.VMEM((length, width), F32),
            pltpu.VMEM((3, 1, half), F32),
            pltpu.VMEM(grad_out.shape, BF16),
            pltpu.VMEM((rows, width), F32),
            pltpu.VMEM((groups, length, width), F32),
        ],
        flops=6 * rows * width * width,
        moved=24 * rows * width,
    )(side, *normed, grads, w_qkv, acc, grad_hidden, gain, *filled, *masks, bias, sums, up_other, up_own, grad_out)


def spot_bits(order, tm):
    return [bits_of(bit) if axis == "tm" else bits_of(tm) + bits_of(bit) - 1 for axis, bit in order]


def shares_of(here_ref, refs, orders, tm, place):
    away = place ^ here_ref[0]
    low = here_ref[1] == 0
    half = len(refs) // 2
    out = []
    for own_ref, other_ref, order in zip(refs[:half], refs[half:], orders):
        index = sum(((away >> b) & 1) << k for k, b in enumerate(spot_bits(order, tm)))
        own, other = own_ref[index], other_ref[index]
        out.append((jnp.where(low, own, other).astype(F32), jnp.where(low, other, own).astype(F32)))
    return out


def place_one_kernel(here_ref, *refs, orders, tm, some):
    down_ref, up_ref = refs[4:]
    width = down_ref.shape[2]
    for u in range(some):
        downs, ups = shares_of(here_ref, refs[:4], orders, tm, pl.program_id(0) * some + u)
        rows = ups[0].shape[0]
        for core in range(2):
            parts = downs[core].shape[1] // width
            for part in range(parts):
                at = (u * parts + part) * rows
                down_ref[core, at : at + rows] = downs[core][:, part * width : (part + 1) * width]
            columns = ups[core].shape[1]
            up_ref[u * rows : (u + 1) * rows, core * columns : (core + 1) * columns] = ups[core]


def place_two_kernel(here_ref, *refs, orders, tm, some):
    qkv_ref, out_ref, pos_ref, small_ref = refs[4:]
    width = out_ref.shape[1]
    half = width // 2
    pos_rows, small_rows = pos_ref.shape[0] // some, small_ref.shape[0] // some
    for u in range(some):
        lefts, rights = shares_of(here_ref, refs[:4], orders, tm, pl.program_id(0) * some + u)
        shares = [jnp.concatenate(sides, 1) for sides in zip(lefts, rights)]
        qkvs = [share[:, : 3 * half] for share in shares]
        out, rest = [share[:, 3 * half :] for share in shares]
        rows = slice(u * out.shape[0], (u + 1) * out.shape[0])
        for core in range(2):
            for i in range(3):
                at = i * width + core * half
                qkv_ref[rows, at : at + half] = qkvs[core][:, i * half : (i + 1) * half]
        out_ref[rows] = out
        pos_ref[u * pos_rows : (u + 1) * pos_rows] = rest[:pos_rows]
        small_ref[u * small_rows : (u + 1) * small_rows] = rest[pos_rows:]


def place(kernel, here, gathered, orders, tm, shapes):
    some = 4
    steps = gathered[0].shape[0] // some

    def cut(shape):
        block = shape[:-2] + (shape[-2] // steps, shape[-1])
        return pl.BlockSpec(block, lambda j, here: (0,) * (len(shape) - 2) + (j, 0))

    return call(
        functools.partial(kernel, orders=orders, tm=tm, some=some),
        prefetch=1,
        grid=(steps,),
        in_specs=[fixed(v.shape) for v in gathered],
        out_specs=[cut(s) for s in shapes],
        out_shape=[shaped(s, F32) for s in shapes],
        moved=sum(6 * v.size for v in gathered),
    )(here, *gathered)


def in_order(here, gathered, orders, tm):
    out = []
    half = len(gathered) // 2
    for own, other, order in zip(gathered[:half], gathered[half:], orders):
        bits = spot_bits(order, tm)
        away = jnp.arange(own.shape[0], dtype=jnp.int32) ^ here[0]
        index = sum(((away >> b) & 1) << k for k, b in enumerate(bits))
        own, other = (jnp.take(x, index, axis=0).astype(F32) for x in (own, other))
        low = here[1] == 0
        out.append(jnp.stack([jnp.where(low, own, other), jnp.where(low, other, own)]))
    return out


def bits_of(size):
    return size.bit_length() - 1


def axis_bits(axis):
    return [(axis, 1 << b) for b in range(bits_of(lax.axis_size(axis)))]


def own_bit(axis, bit):
    return (lax.axis_index(axis) // bit) % 2


def hop(value, axis, bit):
    size = lax.axis_size(axis)
    return lax.ppermute(value, axis, [(i, i ^ bit) for i in range(size)])


def tie(*values):
    return lax.optimization_barrier(values)


def take_clips(values):
    tm = lax.axis_size("tm")
    me = lax.axis_index("tm")
    out = []
    for d in range(tm):
        block = lax.dynamic_index_in_dim(values, me ^ d, 1, keepdims=False)
        out.append(hop(block, "tm", d) if d else block)
    return out


def send_clips(blocks):
    return [hop(block, "tm", d) if d else block for d, block in enumerate(blocks)]


def all_clips(blocks, shape):
    return jnp.stack(unshuffle(blocks), 1).reshape(shape)


def unshuffle(blocks):
    me = lax.axis_index("tm")
    blocks = list(blocks)
    for b in range(bits_of(len(blocks))):
        odd = ((me >> b) & 1) == 1
        blocks = [jnp.where(odd, blocks[i ^ (1 << b)], blocks[i]) for i in range(len(blocks))]
    return blocks


def add_low(a, b):
    return (a.astype(F32) + b.astype(F32)).astype(BF16)


def split_share(value):
    count = bits_of(lax.axis_size("clips")) + bits_of(lax.axis_size("tm")) - 1
    return value.reshape((2,) * count + (value.shape[0] >> count, value.shape[1]))


def side_by_side(value, parts):
    return jnp.concatenate(jnp.split(value, parts, -2), -1)


class Sum:
    def __init__(self, folds):
        self.folds = folds
        clip_bits, self.time_bits = axis_bits("clips")[1:], axis_bits("tm")
        self.names = clip_bits[::-1] + self.time_bits[::-1]
        self.orders = (clip_bits, clip_bits[1:] + clip_bits[:1])
        self.rounds = len(clip_bits) + len(self.time_bits)

    def half(self, pair, names, name, other):
        at = names.index(name)
        mine = own_bit(*name)
        pick = lambda x: lax.dynamic_index_in_dim(x, 1 - mine if other else mine, at, keepdims=False)
        return add_low(*(pick(x) for x in pair))

    def half_of_all(self, index, state, other):
        sides = len(self.orders[0])
        if index < sides:
            names = [[n for n in self.names if n not in order[:index]] for order in self.orders]
            return [self.half(p, n, order[index], other) for p, n, order in zip(state, names, self.orders)]
        names = self.time_bits[index - sides :]
        parts = [self.half(pair, names[::-1], names[0], other) for pair in state]
        if len(parts) > 1:
            parts = [side_by_side(x, n) if n > 1 else x for x, n in zip(parts, self.folds)]
        return [jnp.concatenate(parts, -1) if len(parts) > 1 else parts[0]]

    def split(self, index, state):
        return [(away,) for away in self.half_of_all(index, state, True)] + state

    def send(self, index, state):
        sides = len(self.orders[0])
        names = [o[index] for o in self.orders] if index < sides else [self.time_bits[index - sides]]
        away, state = state[: len(names)], state[len(names) :]
        got = [hop(x, *name) for (x,), name in zip(away, names)]
        return list(zip(self.half_of_all(index, state, False), got))

    def scatter(self, index, state):
        return self.send(index, self.split(index, state))

    def share(self, state):
        return add_low(*state[0])

    def gather_orders(self, at_once=False):
        return [self.time_bits[:: 1 if at_once else -1] + order[::-1] for order in self.orders]


    def split_all(self, state):
        tm, me = lax.axis_size("tm"), lax.axis_index("tm")

        def pick(x, d):
            return lax.dynamic_index_in_dim(x.reshape((tm,) + x.shape[-2:]), me ^ d, 0, keepdims=False)

        def part(d):
            parts = [add_low(*(pick(x, d) for x in pair)) for pair in state]
            return jnp.concatenate([side_by_side(x, n) if n > 1 else x for x, n in zip(parts, self.folds)], -1)

        return [(part(d),) for d in range(tm)]

    def send_all(self, state):
        return [tuple(hop(x, "tm", d) if d else x for d, (x,) in enumerate(state))]

    def share_all(self, state):
        return sum(x.astype(F32) for x in state[0]).astype(BF16)

    def gather_all(self, state):
        return [tuple(hop(state[0][0], "tm", d) if d else state[0][0] for d in range(lax.axis_size("tm")))]

    def join_all(self, state, cut):
        whole = jnp.stack(state[0])
        return [whole[..., :cut], whole[..., cut:]]

    def gather(self, index, state, cut):
        if index < len(self.time_bits):
            return [(state[0], hop(state[0], *self.time_bits[::-1][index]))]
        names = [order[::-1][index - len(self.time_bits)] for order in self.orders]
        return [(value, hop(value, *name)) for value, name in zip(state, names)]

    def join(self, index, state, cut):
        out = [jnp.concatenate(pair, 0) for pair in state]
        if index == len(self.time_bits) - 1:
            return [out[0][..., :cut], out[0][..., cut:]]
        return out


def on_device(
    patches, mask_index, mask_count, w_qkv, q_bias, v_bias, w_out, out_bias, w_up, up_bias,
    w_down, down_bias, norm1_scale, norm1_shift, norm2_scale, norm2_shift, mask_embed, pos_embed,
    cotangent,
):
    clip_count, seg, width = patches.shape
    ff = w_up.shape[1]
    tm = lax.axis_size("tm")
    me = lax.axis_index("tm")
    length = seg * tm
    groups = clip_count // tm
    by_group = (groups, tm, seg, width)
    tile, chunk = 512, 512

    arrived, grouped = [], patches.reshape(by_group)
    for g in range(groups):
        arrived.append(take_clips(grouped[g : g + 1]))
        grouped, *arrived[g] = tie(grouped, *arrived[g])
    tied, *arrived[-1] = tie(cotangent, *arrived[-1])
    cot = take_clips(tied.reshape(by_group))
    arrived = [[b[0] for b in blocks] for blocks in arrived]

    row = lambda x: x.reshape(1, -1)
    joint_bias = row(jnp.concatenate([q_bias, jnp.zeros_like(q_bias), v_bias]))
    out_bias, up_bias, down_bias, gain1, shift1, gain2, shift2, embed = map(
        row, (out_bias, up_bias, down_bias, norm1_scale, norm1_shift, norm2_scale, norm2_shift, mask_embed)
    )
    starts = (me ^ jnp.arange(tm, dtype=jnp.int32)) * seg
    places = (starts[:, None] + jnp.arange(seg, dtype=jnp.int32)[None, :]).reshape(length)
    pos = jnp.concatenate([lax.dynamic_slice_in_dim(pos_embed, (me ^ d) * seg, seg, 0) for d in range(tm)], 0)
    slots = jnp.arange(mask_index.shape[1], dtype=jnp.int32)
    masks = []
    for g in range(groups):
        index_row = lax.dynamic_index_in_dim(mask_index, g * tm + me, 0, keepdims=False)
        count = lax.dynamic_index_in_dim(mask_count, g * tm + me, 0, keepdims=False)
        hit = (places[:, None] == index_row[None, :]) & (slots < count)[None, :]
        masks.append(jnp.any(hit, axis=1, keepdims=True).astype(F32))

    filled, normed_one, joints, attended, turned, logs = [], [], [], [], [], []
    for g in range(groups):
        f, n, j = project(arrived[g], masks[g], embed, pos, gain1, shift1, w_qkv, joint_bias)
        a, a_turned, log_sum = attend(j, width)
        if g < groups - 1:
            a, *arrived[g + 1] = tie(a, *arrived[g + 1])
        else:
            a, cot[1] = tie(a, cot[1])
        for kept, value in zip((filled, normed_one, joints, attended, turned, logs), (f, n, j, a, a_turned, log_sum)):
            kept.append(value)

    core = own_bit("clips", 1).astype(jnp.int32)
    kept_side = jnp.stack([core, me.astype(jnp.int32)])
    away_side = jnp.stack([1 - core, me.astype(jnp.int32)])
    shares = lax.axis_size("clips") // 2 * tm
    here = jnp.stack([(lax.axis_index("clips") // 2 * tm + me).astype(jnp.int32), core])
    hidden, normed_two, act, slope, *block_out = forward(
        filled, attended, w_out, out_bias, gain2, shift2, down_bias, w_up, up_bias, w_down, 1024, 256, tm
    )
    block_out[0], *cot = tie(block_out[0], *cot)
    cot = jnp.concatenate(cot, 1).reshape(groups * length, width)
    norm_acc, down, up, up_sums_away = back_first(away_side, normed_two, cot, act, slope, w_up, w_down, tile, chunk)
    down_got, up_got = hop(down, "clips", 1), hop(up, "clips", 1)
    down, up, up_sums, grad_hidden, mix, grad_out, sums_two = back_last(
        kept_side, turned, normed_two, cot, act, slope, w_up, w_down, w_out, gain2, hidden, norm_acc, tile, chunk
    )
    one = Sum((2, 1))

    def after(values, *states):
        flat = [x for state in states for pair in state for x in pair]
        tied = list(tie(*values, *flat))
        values, flat = tied[: len(values)], tied[len(values) :]
        back = [[tuple(flat.pop(0) for _ in pair) for pair in state] for state in states]
        return (values, *back)

    state = [tuple(split_share(x) for x in pair) for pair in ((down, down_got), (up, up_got))]
    state = one.split(0, state)
    (mix, *block_out), state = after((mix, *block_out), state)
    state = one.send(0, state)
    block_out = send_clips(block_out)
    grads = attend_back(away_side, joints, mix, logs)
    qkv, bias_sums, acc = joint_first(away_side, normed_one, grads, w_qkv)
    qkv_got = hop(qkv, "clips", 1)
    sent_out = block_out
    (acc, sent_out[1], sent_out[2]), state = after((acc, sent_out[1], sent_out[2]), state)
    state = one.split(1, state)
    (mix, acc), state = after((mix, acc), state)
    state = one.send(1, state)
    grads = attend_back(kept_side, joints, mix, logs)
    (grads, *rest_out), state = after((grads, *sent_out[3:]), state)
    sent_out[3:] = rest_out
    third = (one.split_all, one.send_all)
    if len(one.orders[0]) > 2:
        third = (lambda s: one.split(2, s), lambda s: one.send(2, s))
    state = third[0](state)
    (grads,), state = after((grads,), state)
    state = third[1](state)
    qkv, rest_away, rest_kept, *input_grad = joint_last(
        kept_side, normed_one, grads, w_qkv, acc, grad_hidden, gain1, filled, masks, bias_sums, sums_two,
        up_sums_away, up_sums, grad_out.reshape(shares, width // shares, width), tm
    )
    (qkv, rest_away, rest_kept, *input_grad), state = after((qkv, rest_away, rest_kept, *input_grad), state)
    rest_away, rest_kept = rest_away.reshape(width, width), rest_kept.reshape(width, width)
    rest_got = hop(rest_away, "clips", 1)
    two = Sum((1, 1))
    pairs = [tuple(split_share(x) for x in pair) for pair in ((qkv, qkv_got), (rest_kept, rest_got))]
    cut_one, cut_two = ff // 2, -(-5 * width // 4 // LANES) * LANES
    share_rows = pairs[0][0].shape[-2]

    def scatter_steps(group, first):
        steps = [lambda s, i=i: group.split(i, s) for i in range(first, group.rounds)]
        return [(split, lambda s, i=i: group.send(i, s)) for i, split in zip(range(first, group.rounds), steps)]

    def gather_steps(group, cut):
        def prepare(i):
            if i == 0:
                return lambda s: [(group.share(s)[None],)]
            return lambda s: [(x,) for x in group.join(i - 1, s, cut)]

        return [
            (prepare(i), lambda s, i=i: group.gather(i, [x for (x,) in s], cut)) for i in range(group.rounds)
        ]

    def core_steps(group, cut):
        return [
            (
                lambda s: [(x,) for x in group.join(group.rounds - 1, s, cut)],
                lambda s: [(x, hop(x, "clips", 1)) for (x,) in s],
            )
        ]

    along = len(two.time_bits)
    steps_one = [None]
    if len(one.orders[0]) > 2:
        steps_one = scatter_steps(one, 3)[:-along] + [(one.split_all, one.send_all)]
    turn = len(steps_one) - 1
    back_one = gather_steps(one, cut_one)
    back_one[0] = (lambda s: [(one.share_all(s)[None],)], back_one[0][1])
    steps_one += back_one[1:] + [None] + core_steps(one, cut_one)
    steps_two = scatter_steps(two, 0)[:-along]
    steps_two.append((two.split_all, two.send_all))
    steps_two.append((lambda s: [(two.share_all(s),)], two.gather_all))
    back_two = gather_steps(two, cut_two)[along:]
    steps_two.append((lambda s: [(x,) for x in two.join_all(s, cut_two)], back_two[0][1]))
    steps_two += back_two[1:] + core_steps(two, cut_two)
    outputs = []
    for index in range(max(len(steps_one), len(steps_two))):
        if index == 2:
            block_out = all_clips(sent_out, patches.shape)
            (block_out,), state, pairs = after((block_out,), state, pairs)
        if index == len(steps_two) - 2:
            sent[1:3], state, pairs = after(sent[1:3], state, pairs)
        if index == len(steps_two) - 1:
            tied, pairs = after((*sent[3:], *outputs), pairs)
            sent[3:], outputs = tied[: len(sent) - 3], tied[len(sent) - 3 :]
        active = [steps[index] if index < len(steps) else None for steps in (steps_one, steps_two)]
        states = [step[0](x) if step else x for step, x in zip(active, (state, pairs))]
        live = [x for x, step in zip(states, active) if step]
        if index == 3:
            input_grad, *live = after(input_grad, *live)
            sent = send_clips(input_grad)
        elif index:
            _, *live = after((), *live)
        live = iter(live)
        state, pairs = (step[1](next(live)) if step else x for step, x in zip(active, states))
        if index == turn:
            state = back_one[0][1](back_one[0][0](state))
        if index == len(steps_one) - 1:
            one_all = [own for own, _ in state] + [other for _, other in state]
            if share_rows % 8 == 0:
                outputs = place(
                    place_one_kernel, here, one_all, one.gather_orders(), tm, ((2, ff // 2, width), (width, ff))
                )
    two_all = [own for own, _ in pairs] + [other for _, other in pairs]
    input_grad = all_clips(sent, patches.shape)

    orders_one, orders_two = one.gather_orders(), two.gather_orders(True)
    if share_rows % 8 == 0:
        down_sum, up_sum = outputs
        shapes = ((width, 3 * width), (width, width), (length, width), (width - length, width))
        qkv_sum, out_sum, pos_sum, small = place(place_two_kernel, here, two_all, orders_two, tm, shapes)
        down_sum = down_sum.reshape(ff, width)
    else:
        downs, ups = in_order(here, one_all, orders_one, tm)
        both = jnp.concatenate(in_order(here, two_all, orders_two, tm), -1)
        qkvs, rests = both[..., : 3 * width // 2], both[..., 3 * width // 2 :]
        down_sum = jnp.stack(jnp.split(downs, 2, -1), 2).reshape(ff, width)
        up_sum = jnp.concatenate(list(ups.reshape(2, width, ff // 2)), 1)
        qkv_sum = jnp.stack(list(qkvs.reshape(2, width, 3, width // 2)), 2).reshape(width, 3 * width)
        out_sum, rest = rests[0].reshape(width, width), rests[1]
        pos_sum = rest[:, : length // shares].reshape(length, width)
        small = rest[:, length // shares :].reshape(width - length, width)
    v = []
    at = 0
    for n in (1, 1, 1, ff // width, 1, 1, 1, 1, 1, 1):
        v.append(small[at : at + n].reshape(-1))
        at += n
    return (block_out, input_grad, qkv_sum, v[0], v[1], out_sum, v[2], up_sum, v[3], down_sum, v[4],
            v[5], v[6], v[7], v[8], v[9], pos_sum)


def solution(mesh):
    rows = P("clips", "tm", None)
    in_specs = (rows, P("clips", None), P("clips")) + (P(),) * 15 + (rows,)
    out_specs = (rows, rows) + (P(),) * 15
    return jax.shard_map(on_device, mesh=mesh, in_specs=in_specs, out_specs=out_specs, check_vma=False)
```

```python
import functools

import jax
import jax.numpy as jnp
from jax import lax
from jax.experimental import pallas as pl
from jax.experimental.pallas import tpu as pltpu
from jax.sharding import PartitionSpec as P

HEADS = 12
LANES = 128
NORM_EPS = 1e-06
ROOT_HALF = 0.7071067811865476
ROOT_TWO_PI = 2.5066282746310002
LOG2_E = 1.4426950408889634
F32 = jnp.float32
BF16 = jnp.bfloat16
VMEM_LIMIT = 60 * 2**20


def contract(a, b, da, db):
    return lax.dot_general(a, b, (((da,), (db,)), ((), ())), preferred_element_type=F32)


def call(kernel, *, grid, in_specs, out_specs, out_shape, scratch=(), prefetch=0, flops=0, moved=0, exps=0, share=1):
    return pl.pallas_call(
        kernel,
        grid_spec=pltpu.PrefetchScalarGridSpec(
            num_scalar_prefetch=prefetch,
            grid=grid,
            in_specs=in_specs,
            out_specs=out_specs,
            scratch_shapes=scratch,
        ),
        out_shape=out_shape,
        cost_estimate=pl.CostEstimate(
            flops=int(flops) // share, bytes_accessed=int(moved) // share, transcendentals=int(exps) // share
        ),
        compiler_params=pltpu.CompilerParams(vmem_limit_bytes=VMEM_LIMIT),
    )


def fixed(shape):
    return pl.BlockSpec(shape, lambda *_: (0,) * len(shape), pipeline_mode=pl.Buffered(1))


def shaped(shape, dtype):
    return jax.ShapeDtypeStruct(shape, dtype)


def norm_parts(values):
    centred = values - jnp.mean(values, -1, keepdims=True)
    spread = jnp.mean(centred * centred, -1, keepdims=True)
    inverse = lax.rsqrt(spread + NORM_EPS)
    return centred * inverse, inverse


def norm_backward(grad_norm, unit, inverse, gains):
    scaled = grad_norm * gains
    return inverse * (
        scaled
        - jnp.mean(scaled, -1, keepdims=True)
        - unit * jnp.mean(scaled * unit, -1, keepdims=True)
    )


def project_kernel(*refs, tm):
    blocks = refs[:tm]
    mask_ref, embed_ref, pos_ref, gain_ref, shift_ref, w_ref, bias_ref, filled_ref, turned_ref, joint_ref, normed_s = refs[tm:]

    @pl.when(pl.program_id(0) == 0)
    def _():
        seg = blocks[0].shape[0]
        embed, gain, shift = (r[...].astype(F32) for r in (embed_ref, gain_ref, shift_ref))
        for d in range(tm):
            rows = slice(d * seg, (d + 1) * seg)
            filled = jnp.where(mask_ref[rows] > 0.5, embed, blocks[d][...].astype(F32)) + pos_ref[rows].astype(F32)
            unit, _ = norm_parts(filled)
            normed = (unit * gain + shift).astype(BF16)
            filled_ref[rows] = filled
            normed_s[rows] = normed
            turned_ref[:, rows] = normed.T

    joint_ref[...] = (contract(normed_s[...], w_ref[...], 1, 0) + bias_ref[...].astype(F32)).astype(BF16)


def project(blocks, mask, embed, pos, gain, shift, w_qkv, bias):
    tm = len(blocks)
    seg, width = blocks[0].shape
    rows = tm * seg
    return call(
        functools.partial(project_kernel, tm=tm),
        grid=(3,),
        in_specs=[fixed((seg, width))] * tm
        + [fixed((rows, 1)), fixed((1, width)), fixed((rows, width)), fixed((1, width)), fixed((1, width))]
        + [pl.BlockSpec((width, width), lambda j: (0, j)), pl.BlockSpec((1, width), lambda j: (0, j))],
        out_specs=[
            pl.BlockSpec((rows, width), lambda j: (0, 0)),
            pl.BlockSpec((width, rows), lambda j: (0, 0)),
            pl.BlockSpec((rows, width), lambda j: (0, j)),
        ],
        out_shape=[shaped((rows, width), F32), shaped((width, rows), BF16), shaped((rows, 3 * width), BF16)],
        scratch=[pltpu.VMEM((rows, width), BF16)],
        flops=6 * rows * width * width,
        moved=20 * rows * width,
    )(*blocks, mask, embed, pos, gain, shift, w_qkv, bias)


def own_lanes(value, i, head):
    lane = lax.broadcasted_iota(jnp.int32, value.shape, 1)
    return jnp.where((lane >= i * head) & (lane < (i + 1) * head), value, jnp.zeros_like(value))


def attend_kernel(q_ref, k_ref, v_ref, o_ref, turned_ref, log_ref, *, head):
    factor = head**-0.5 * LOG2_E
    per = LANES // head
    pairs = [slice(at, at + LANES) for at in range(0, q_ref.shape[1], LANES)]
    scores = [[contract(k_ref[:, n], own_lanes(q_ref[:, n], i, head), 1, 1) for i in range(per)] for n in pairs]
    for pair, lanes in enumerate(pairs):
        outs = []
        for i in range(per):
            peak = jnp.max(scores[pair][i], 0, keepdims=True)
            raised = jnp.exp2((scores[pair][i] - peak) * factor)
            total = jnp.sum(raised, 0, keepdims=True)
            mixed = contract(v_ref[:, lanes], raised.astype(BF16), 0, 0)
            outs.append(mixed[i * head : (i + 1) * head] * (1.0 / total))
            log_ref[pair, i : i + 1, :] = peak * factor + jnp.log2(total)
        turned = jnp.concatenate(outs, 0)
        turned_ref[lanes] = turned.astype(BF16)
        o_ref[:, lanes] = turned.T.astype(BF16)


def attend(joint, width):
    rows = joint.shape[0]
    head = width // HEADS
    pairs, per = width // LANES, LANES // head
    some = 2 if pairs % 2 == 0 else 1
    steps = pairs // some
    block = lambda off: pl.BlockSpec((rows, some * LANES), lambda h: (0, h + off))
    return call(
        functools.partial(attend_kernel, head=head),
        grid=(steps,),
        in_specs=[block(0), block(steps), block(2 * steps)],
        out_specs=[
            block(0),
            pl.BlockSpec((some * LANES, rows), lambda h: (h, 0)),
            pl.BlockSpec((some, per, rows), lambda h: (h, 0, 0)),
        ],
        out_shape=[shaped((rows, width), BF16), shaped((width, rows), BF16), shaped((pairs, per, rows), F32)],
        flops=16 * rows * rows * width,
        moved=8 * rows * width,
        exps=rows * rows * HEADS,
    )(joint, joint, joint)


def attend_back_kernel(side_ref, *refs, head, groups):
    per_clip = [refs[4 * c : 4 * c + 4] for c in range(groups)]
    g_ref, out_ref = refs[4 * groups :]
    scale = head**-0.5
    length = per_clip[0][0].shape[0]
    per = LANES // head
    ahead = []
    for c, (q_ref, k_ref, v_ref, log_ref) in enumerate(per_clip):
        rows = slice(c * length, (c + 1) * length)
        for i in range(per):
            q_own, g_own = own_lanes(q_ref[...], i, head), own_lanes(g_ref[rows], i, head)
            ahead.append((q_own, g_own, contract(k_ref[...], q_own, 1, 1), contract(v_ref[...], g_own, 1, 1)))
    for c, (q_ref, k_ref, v_ref, log_ref) in enumerate(per_clip):
        rows = slice(c * length, (c + 1) * length)
        grad_q, grad_k, grad_v = [], 0.0, 0.0
        for i in range(per):
            q_own, g_own, scores, grad_probs = ahead[c * per + i]
            probs = jnp.exp2(scores * (scale * LOG2_E) - log_ref[0, i : i + 1, :])
            delta = jnp.sum(probs * grad_probs, 0, keepdims=True)
            grad_scores = (probs * (grad_probs - delta)).astype(BF16)
            grad_v = grad_v + contract(probs.astype(BF16), g_own, 1, 0)
            grad_q.append(contract(k_ref[...], grad_scores, 0, 0)[i * head : (i + 1) * head])
            grad_k = grad_k + contract(grad_scores, q_own, 1, 0)
        out_ref[0, rows] = (jnp.concatenate(grad_q, 0) * scale).T.astype(BF16)
        out_ref[1, rows] = (grad_k * scale).astype(BF16)
        out_ref[2, rows] = grad_v.astype(BF16)


def attend_back(side, joints, mix, logs):
    rows, width = mix.shape
    groups = len(joints)
    length = rows // groups
    head = width // HEADS
    pairs, per = width // LANES, LANES // head
    half = pairs // 2

    def block(off):
        return pl.BlockSpec((length, LANES), lambda h, s: (0, off + s[0] * half + h))

    clip = [block(0), block(pairs), block(2 * pairs), pl.BlockSpec((1, per, length), lambda h, s: (s[0] * half + h, 0, 0))]
    operands = []
    for joint, log_sum in zip(joints, logs):
        operands += [joint, joint, joint, log_sum]
    return call(
        functools.partial(attend_back_kernel, head=head, groups=groups),
        prefetch=1,
        share=4096,
        grid=(half,),
        in_specs=clip * groups + [pl.BlockSpec((rows, LANES), lambda h, s: (0, s[0] * half + h))],
        out_specs=pl.BlockSpec((3, rows, LANES), lambda h, s: (0, 0, h)),
        out_shape=shaped((3, rows, width // 2), BF16),
        flops=20 * rows * length * width,
        moved=8 * rows * width,
        exps=rows * length * HEADS // 2,
    )(side, *operands, mix)


def gelu_parts(u):
    phi = 0.5 * (1.0 + lax.erf(u * ROOT_HALF))
    return u * phi, phi + u * jnp.exp(-0.5 * u * u) * (1.0 / ROOT_TWO_PI)


def by_segment(refs, values, clip=None):
    clips, seg, _ = refs[0].shape
    for c in range(clips) if clip is None else (clip,):
        for d, ref in enumerate(refs):
            at = ((0 if clip is not None else c) * len(refs) + d) * seg
            ref[c] = values[at : at + seg]


def forward_kernel(*refs, groups, chunk):
    filled, attended = refs[:groups], refs[groups : 2 * groups]
    (w_out_ref, out_bias_ref, gain_ref, shift_ref, down_bias_ref, w_up_ref, up_bias_ref, w_down_ref,
     hidden_ref, turned_ref, act_ref, slope_ref, *block_refs, out_s, normed_s, hidden_s) = refs[2 * groups :]
    rows_all = out_s.shape[0]
    step, last = pl.program_id(0), pl.num_programs(0) - 1

    @pl.when(step == 0)
    def _():
        gain, shift = gain_ref[...].astype(F32), shift_ref[...].astype(F32)
        out_bias, down_bias = out_bias_ref[...].astype(F32), down_bias_ref[...].astype(F32)
        length = filled[0].shape[0]
        for c in range(groups):
            rows = slice(c * length, (c + 1) * length)
            hidden = filled[c][...] + contract(attended[c][...], w_out_ref[...], 1, 0) + out_bias
            unit, _ = norm_parts(hidden)
            normed = (unit * gain + shift).astype(BF16)
            hidden_s[rows] = hidden
            normed_s[rows] = normed
            turned_ref[:, rows] = normed.T
            out_s[rows] = hidden + down_bias

    w_up, w_down = w_up_ref[...], w_down_ref[...]
    bias = up_bias_ref[...].astype(F32)
    some = hidden_ref.shape[1]
    hidden_ref[...] = hidden_s[:, pl.ds(pl.multiple_of(step * some, some), some)]
    chunks = [slice(at, at + chunk) for at in range(0, rows_all, chunk)]
    ahead = [contract(normed_s[rows], w_up, 1, 0) for rows in chunks]
    for rows, up in zip(chunks, ahead):
        value, slope = gelu_parts(up + bias)
        act = value.astype(BF16)
        act_ref[:, rows] = act.T
        slope_ref[rows] = slope.astype(BF16)
        out_s[rows] += contract(act, w_down, 1, 0)

    @pl.when(step == last)
    def _():
        by_segment(block_refs, out_s[...].astype(BF16))


def forward(filled, attended, w_out, out_bias, gain, shift, down_bias, w_up, up_bias, w_down, tile, chunk, tm):
    groups, (length, width) = len(filled), filled[0].shape
    rows, ff = groups * length, w_up.shape[1]
    vec = fixed((1, width))
    column = pl.BlockSpec((rows, tile), lambda j: (0, j))
    return call(
        functools.partial(forward_kernel, groups=groups, chunk=chunk),
        grid=(ff // tile,),
        in_specs=[fixed((length, width))] * (2 * groups)
        + [fixed((width, width)), vec, vec, vec, vec]
        + [
            pl.BlockSpec((width, tile), lambda j: (0, j)),
            pl.BlockSpec((1, tile), lambda j: (0, j)),
            pl.BlockSpec((tile, width), lambda j: (j, 0)),
        ],
        out_specs=[cut_by_step(rows, width, ff // tile), fixed((width, rows)), pl.BlockSpec((tile, rows), lambda j: (j, 0)), column]
        + [fixed((groups, length // tm, width))] * tm,
        out_shape=[shaped((rows, width), F32), shaped((width, rows), BF16)]
        + [shaped((ff, rows), BF16), shaped((rows, ff), BF16)]
        + [shaped((groups, length // tm, width), BF16)] * tm,
        scratch=[pltpu.VMEM((rows, width), F32), pltpu.VMEM((rows, width), BF16), pltpu.VMEM((rows, width), F32)],
        flops=4 * rows * width * ff + 2 * rows * width * width,
        moved=14 * rows * width + 4 * rows * ff + 4 * width * ff,
        exps=rows * ff,
    )(*filled, *attended, w_out, out_bias, gain, shift, down_bias, w_up, up_bias, w_down)


def cut_by_step(rows, width, steps):
    return pl.BlockSpec((rows, width // steps), lambda j, *_: (0, j))


def tile_back(turned_ref, cot_ref, act_ref, slope_ref, w_up_ref, w_down_ref, gup_s, norm_s, down_ref, up_ref, bias_ref, chunk):
    w_up, w_down = w_up_ref[...], w_down_ref[...]
    total = jnp.zeros(bias_ref.shape, F32)
    chunks = [slice(at, at + chunk) for at in range(0, cot_ref.shape[0], chunk)]
    ahead = [contract(cot_ref[rows], w_down, 1, 1) for rows in chunks]
    down_ref[...] = contract(act_ref[...], cot_ref[...], 1, 0).astype(BF16)
    for rows, grad_act in zip(chunks, ahead):
        gup = (grad_act * slope_ref[rows].astype(F32)).astype(BF16)
        gup_s[rows] = gup
        total = total + jnp.sum(gup.astype(F32), 0, keepdims=True)
        norm_s[rows] += contract(gup, w_up, 1, 1)
    bias_ref[...] = total
    up_ref[...] = contract(turned_ref[...], gup_s[...], 1, 0).astype(BF16)


def back_first_kernel(side_ref, turned_ref, cot_ref, act_ref, slope_ref, w_up_ref, w_down_ref, norm_ref, down_ref, up_ref, bias_ref, gup_s, *, chunk):
    @pl.when(pl.program_id(0) == 0)
    def _():
        norm_ref[...] = jnp.zeros_like(norm_ref)

    tile_back(turned_ref, cot_ref, act_ref, slope_ref, w_up_ref, w_down_ref, gup_s, norm_ref, down_ref, up_ref, bias_ref, chunk)


def back_last_kernel(side_ref, *refs, groups, chunk):
    attended = refs[:groups]
    (turned_ref, cot_ref, act_ref, slope_ref, w_up_ref, w_down_ref, w_out_ref, gain_ref, hidden_ref, norm_ref,
     down_ref, up_ref, bias_ref, grad_hidden_ref, mix_ref, grad_out_ref, sums_ref, gup_s, norm_s, branch_s, hidden_s) = refs[groups:]

    @pl.when(pl.program_id(0) == 0)
    def _():
        norm_s[...] = jnp.zeros_like(norm_s)

    columns = pl.ds(pl.multiple_of(pl.program_id(0) * norm_ref.shape[1], norm_ref.shape[1]), norm_ref.shape[1])
    hidden_s[:, columns] = hidden_ref[...]
    norm_s[:, columns] += norm_ref[...]
    tile_back(turned_ref, cot_ref, act_ref, slope_ref, w_up_ref, w_down_ref, gup_s, norm_s, down_ref, up_ref, bias_ref, chunk)

    @pl.when(pl.program_id(0) == pl.num_programs(0) - 1)
    def _():
        gain = gain_ref[...].astype(F32)
        total = [jnp.zeros_like(gain) for _ in range(4)]
        w_out = w_out_ref[...]
        for r in range(norm_s.shape[0] // chunk):
            rows = slice(r * chunk, (r + 1) * chunk)
            unit, inverse = norm_parts(hidden_s[rows])
            top, grad_norm = cot_ref[rows].astype(F32), norm_s[rows]
            grad_hidden = top + norm_backward(grad_norm, unit, inverse, gain)
            grad_hidden_ref[rows] = grad_hidden
            branch = grad_hidden.astype(BF16)
            branch_s[rows] = branch
            mix_ref[rows] = contract(branch, w_out, 1, 1).astype(BF16)
            parts = (branch.astype(F32), top, grad_norm * unit, grad_norm)
            total = [t + jnp.sum(p, 0, keepdims=True) for t, p in zip(total, parts)]
        sums_ref[...] = jnp.concatenate(total + [jnp.zeros_like(gain)] * 4, 0)
        length = attended[0].shape[1]
        grad_out = 0.0
        for c in range(groups):
            grad_out = grad_out + contract(attended[c][...], branch_s[c * length : (c + 1) * length], 1, 0)
        grad_out_ref[...] = grad_out.astype(BF16)


def back_specs(rows, width, half, tile):
    steps = half // tile
    column = lambda n: pl.BlockSpec((n, tile), lambda j, s: (0, s[0] * steps + j))
    ins = [fixed((width, rows)), fixed((rows, width))]
    ins += [pl.BlockSpec((tile, rows), lambda j, s: (s[0] * steps + j, 0)), column(rows), column(width)]
    ins.append(pl.BlockSpec((tile, width), lambda j, s: (s[0] * steps + j, 0)))
    outs = [
        pl.BlockSpec((tile, width), lambda j, s: (j, 0)),
        pl.BlockSpec((width, tile), lambda j, s: (0, j)),
        pl.BlockSpec((1, tile), lambda j, s: (0, j)),
    ]
    return ins, outs, [shaped((half, width), BF16), shaped((width, half), BF16), shaped((1, half), F32)]


def back_first(side, normed, cot, act, slope, w_up, w_down, tile, chunk):
    rows, width = cot.shape
    half = w_up.shape[1] // 2
    ins, outs, shapes = back_specs(rows, width, half, tile)
    return call(
        functools.partial(back_first_kernel, chunk=chunk),
        prefetch=1,
        grid=(half // tile,),
        in_specs=ins,
        out_specs=[fixed((rows, width))] + outs,
        out_shape=[shaped((rows, width), F32)] + shapes,
        scratch=[pltpu.VMEM((rows, tile), BF16)],
        flops=8 * rows * width * half,
        moved=8 * rows * width + 4 * rows * half + 8 * width * half,
    )(side, normed, cot, act, slope, w_up, w_down)


def back_last(side, attended, normed, cot, act, slope, w_up, w_down, w_out, gain, hidden, norm, tile, chunk):
    rows, width = cot.shape
    groups = len(attended)
    half = w_up.shape[1] // 2
    ins, outs, shapes = back_specs(rows, width, half, tile)
    whole = lambda n: fixed((n, width))
    return call(
        functools.partial(back_last_kernel, groups=groups, chunk=chunk),
        prefetch=1,
        grid=(half // tile,),
        in_specs=[fixed((width, rows // groups))] * groups + ins + [whole(width), whole(1)] + [cut_by_step(rows, width, half // tile)] * 2,
        out_specs=outs + [whole(rows), whole(rows), whole(width), whole(8)],
        out_shape=shapes
        + [shaped((rows, width), F32), shaped((rows, width), BF16), shaped((width, width), BF16), shaped((8, width), F32)],
        scratch=[
            pltpu.VMEM((rows, tile), BF16),
            pltpu.VMEM((rows, width), F32),
            pltpu.VMEM((rows, width), BF16),
            pltpu.VMEM((rows, width), F32),
        ],
        flops=8 * rows * width * half + 4 * rows * width * width,
        moved=20 * rows * width + 4 * rows * half + 8 * width * half,
    )(side, *attended, normed, cot, act, slope, w_up, w_down, w_out, gain, hidden, norm)


def joint_part(normed, grad_ref, grad_w_ref, bias_ref):
    length = normed[0].shape[1]
    grad_w = 0.0
    for c, normed_ref in enumerate(normed):
        grad_w = grad_w + contract(normed_ref[...], grad_ref[0, c * length : (c + 1) * length], 1, 0)
    grad_w_ref[...] = grad_w.astype(BF16)
    bias_ref[0] = jnp.sum(grad_ref[0].astype(F32), 0, keepdims=True)


def joint_first_kernel(side_ref, *refs, groups):
    normed, (grad_ref, weight_ref, grad_w_ref, bias_ref, acc_ref) = refs[:groups], refs[groups:]
    joint_part(normed, grad_ref, grad_w_ref, bias_ref)
    part = contract(grad_ref[0], weight_ref[...], 1, 1)

    @pl.when(pl.program_id(0) == 0)
    def _():
        acc_ref[...] = part

    @pl.when(pl.program_id(0) > 0)
    def _():
        acc_ref[...] += part


def joint_last_kernel(side_ref, *refs, groups, tm):
    normed, (grad_ref, weight_ref, acc_ref, grad_hidden_ref, gain_ref) = refs[:groups], refs[groups : groups + 5]
    refs = refs[groups + 5 :]
    filled, masks = refs[:groups], refs[groups : 2 * groups]
    (other_bias_ref, sums_ref, up_other_ref, up_own_ref, grad_out_ref, grad_w_ref, away_ref, kept_ref, *input_refs,
     acc_s, pos_s, bias_s, rest_ref, hidden_s, filled_s) = refs[2 * groups :]
    core, me = side_ref[0], side_ref[1]
    length, half = normed[0].shape[1], grad_w_ref.shape[1]
    step = pl.program_id(0)
    joint_part(normed, grad_ref, grad_w_ref, bias_s.at[pl.ds(step, 1)])

    @pl.when(step == 0)
    def _():
        acc_s[...] = contract(grad_ref[0], weight_ref[...], 1, 1)

    some = acc_ref.shape[1]
    columns = pl.ds(pl.multiple_of(step * some, some), some)
    acc_s[:, columns] += acc_ref[...]
    hidden_s[:, columns] = grad_hidden_ref[...]
    for c in range(groups):
        filled_s[c, :, columns] = filled[c][...]

    @pl.when(step == 1)
    def _():
        acc_s[...] += contract(grad_ref[0], weight_ref[...], 1, 1)

    @pl.when(step == 2)
    def _():
        gain = gain_ref[...].astype(F32)
        weight = weight_ref[...]
        total = [jnp.zeros_like(gain) for _ in range(3)]
        clips = [slice(c * length, (c + 1) * length) for c in range(groups)]
        grad_norms = [acc_s[rows] + contract(grad_ref[0, rows], weight, 1, 1) for rows in clips]
        for c, rows in enumerate(clips):
            grad_norm = grad_norms[c]
            unit, inverse = norm_parts(filled_s[c])
            grad_filled = hidden_s[rows] + norm_backward(grad_norm, unit, inverse, gain)
            masked = masks[c][...] > 0.5
            by_segment(input_refs, jnp.where(masked, 0.0, grad_filled).astype(BF16), c)
            parts = (grad_norm * unit, grad_norm, jnp.where(masked, grad_filled, 0.0))
            total = [t + jnp.sum(p, 0, keepdims=True) for t, p in zip(total, parts)]
            pos_s[...] = grad_filled if c == 0 else pos_s[...] + grad_filled
        seg = length // tm
        shares, share_rows, _ = rest_ref.shape
        pos_rows, some = length // shares, shares // tm
        for d in range(tm):
            own = pos_s[d * seg : (d + 1) * seg].reshape(some, pos_rows, pos_s.shape[1])
            rest_ref[pl.ds((me ^ d) * some, some), :pos_rows] = own.astype(BF16)

        def both(other, mine):
            return jnp.where(core == 0, jnp.concatenate([mine, other], 1), jnp.concatenate([other, mine], 1))

        width = gain.shape[1]
        up = both(up_other_ref[...], up_own_ref[...])
        sums = sums_ref[...]
        lines = [both(other_bias_ref[i], bias_s[i]) for i in (0, 2)] + [sums[0:1]]
        lines += [up[:, i * width : (i + 1) * width] for i in range(up.shape[1] // width)]
        lines += [sums[1:2], total[0], total[1], sums[2:3], sums[3:4], total[2]]
        lines.append(jnp.zeros((shares * (share_rows - pos_rows) - len(lines), width), F32))
        small = jnp.concatenate(lines, 0).reshape(shares, share_rows - pos_rows, width)
        rest_ref[:, pos_rows:] = small.astype(BF16)
        rest, grad_out = rest_ref[...], grad_out_ref[...]
        away_ref[...] = jnp.where(core == 1, grad_out, rest)
        kept_ref[...] = jnp.where(core == 1, rest, grad_out)


def joint_specs(groups, rows, width):
    half = width // 2
    return [fixed((width, rows // groups))] * groups + [
        pl.BlockSpec((1, rows, half), lambda i, s: (i, 0, 0)),
        pl.BlockSpec((width, half), lambda i, s: (0, 2 * i + s[0])),
    ]


def joint_first(side, normed, grads, w_qkv):
    _, rows, half = grads.shape
    groups, width = len(normed), 2 * half
    return call(
        functools.partial(joint_first_kernel, groups=groups),
        prefetch=1,
        share=4096,
        grid=(3,),
        in_specs=joint_specs(groups, rows, width),
        out_specs=[
            pl.BlockSpec((width, half), lambda i, s: (0, i)),
            pl.BlockSpec((1, 1, half), lambda i, s: (i, 0, 0)),
            fixed((rows, width)),
        ],
        out_shape=[shaped((width, 3 * half), BF16), shaped((3, 1, half), F32), shaped((rows, width), F32)],
        flops=6 * rows * width * width,
        moved=12 * rows * width,
    )(side, *normed, grads, w_qkv)


def joint_last(side, normed, grads, w_qkv, acc, grad_hidden, gain, filled, masks, bias, sums, up_other, up_own, grad_out, tm):
    shares = grad_out.shape[0]
    _, rows, half = grads.shape
    groups, width = len(normed), 2 * half
    length = rows // groups
    return call(
        functools.partial(joint_last_kernel, groups=groups, tm=tm),
        prefetch=1,
        share=4096,
        grid=(3,),
        in_specs=joint_specs(groups, rows, width)
        + [cut_by_step(rows, width, 3)] * 2
        + [fixed((1, width))]
        + [cut_by_step(length, width, 3)] * groups
        + [fixed((length, 1))] * groups
        + [fixed((3, 1, half)), fixed((8, width)), fixed(up_other.shape), fixed(up_own.shape)]
        + [fixed(grad_out.shape)],
        out_specs=[
            pl.BlockSpec((width, half), lambda i, s: (0, i)),
            fixed(grad_out.shape),
            fixed(grad_out.shape),
        ]
        + [fixed((groups, length // tm, width))] * tm,
        out_shape=[
            shaped((width, 3 * half), BF16),
            shaped(grad_out.shape, BF16),
            shaped(grad_out.shape, BF16),
        ]
        + [shaped((groups, length // tm, width), BF16)] * tm,
        scratch=[
            pltpu.VMEM((rows, width), F32),
            pltpu.VMEM((length, width), F32),
            pltpu.VMEM((3, 1, half), F32),
            pltpu.VMEM(grad_out.shape, BF16),
            pltpu.VMEM((rows, width), F32),
            pltpu.VMEM((groups, length, width), F32),
        ],
        flops=6 * rows * width * width,
        moved=24 * rows * width,
    )(side, *normed, grads, w_qkv, acc, grad_hidden, gain, *filled, *masks, bias, sums, up_other, up_own, grad_out)


def spot_bits(order, tm):
    return [bits_of(bit) if axis == "tm" else bits_of(tm) + bits_of(bit) - 1 for axis, bit in order]


def shares_of(here_ref, refs, orders, tm, place):
    away = place ^ here_ref[0]
    low = here_ref[1] == 0
    half = len(refs) // 2
    out = []
    for own_ref, other_ref, order in zip(refs[:half], refs[half:], orders):
        index = sum(((away >> b) & 1) << k for k, b in enumerate(spot_bits(order, tm)))
        own, other = own_ref[index], other_ref[index]
        out.append((jnp.where(low, own, other).astype(F32), jnp.where(low, other, own).astype(F32)))
    return out


def place_one_kernel(here_ref, *refs, orders, tm, some):
    down_ref, up_ref = refs[4:]
    width = down_ref.shape[2]
    for u in range(some):
        downs, ups = shares_of(here_ref, refs[:4], orders, tm, pl.program_id(0) * some + u)
        rows = ups[0].shape[0]
        for core in range(2):
            parts = downs[core].shape[1] // width
            for part in range(parts):
                at = (u * parts + part) * rows
                down_ref[core, at : at + rows] = downs[core][:, part * width : (part + 1) * width]
            columns = ups[core].shape[1]
            up_ref[u * rows : (u + 1) * rows, core * columns : (core + 1) * columns] = ups[core]


def place_two_kernel(here_ref, *refs, orders, tm, some):
    qkv_ref, out_ref, pos_ref, small_ref = refs[4:]
    width = out_ref.shape[1]
    half = width // 2
    pos_rows, small_rows = pos_ref.shape[0] // some, small_ref.shape[0] // some
    for u in range(some):
        lefts, rights = shares_of(here_ref, refs[:4], orders, tm, pl.program_id(0) * some + u)
        shares = [jnp.concatenate(sides, 1) for sides in zip(lefts, rights)]
        qkvs = [share[:, : 3 * half] for share in shares]
        out, rest = [share[:, 3 * half :] for share in shares]
        rows = slice(u * out.shape[0], (u + 1) * out.shape[0])
        for core in range(2):
            for i in range(3):
                at = i * width + core * half
                qkv_ref[rows, at : at + half] = qkvs[core][:, i * half : (i + 1) * half]
        out_ref[rows] = out
        pos_ref[u * pos_rows : (u + 1) * pos_rows] = rest[:pos_rows]
        small_ref[u * small_rows : (u + 1) * small_rows] = rest[pos_rows:]


def place(kernel, here, gathered, orders, tm, shapes):
    some = 4
    steps = gathered[0].shape[0] // some

    def cut(shape):
        block = shape[:-2] + (shape[-2] // steps, shape[-1])
        return pl.BlockSpec(block, lambda j, here: (0,) * (len(shape) - 2) + (j, 0))

    return call(
        functools.partial(kernel, orders=orders, tm=tm, some=some),
        prefetch=1,
        grid=(steps,),
        in_specs=[fixed(v.shape) for v in gathered],
        out_specs=[cut(s) for s in shapes],
        out_shape=[shaped(s, F32) for s in shapes],
        moved=sum(6 * v.size for v in gathered),
    )(here, *gathered)


def in_order(here, gathered, orders, tm):
    out = []
    half = len(gathered) // 2
    for own, other, order in zip(gathered[:half], gathered[half:], orders):
        bits = spot_bits(order, tm)
        away = jnp.arange(own.shape[0], dtype=jnp.int32) ^ here[0]
        index = sum(((away >> b) & 1) << k for k, b in enumerate(bits))
        own, other = (jnp.take(x, index, axis=0).astype(F32) for x in (own, other))
        low = here[1] == 0
        out.append(jnp.stack([jnp.where(low, own, other), jnp.where(low, other, own)]))
    return out


def bits_of(size):
    return size.bit_length() - 1


def axis_bits(axis):
    return [(axis, 1 << b) for b in range(bits_of(lax.axis_size(axis)))]


def own_bit(axis, bit):
    return (lax.axis_index(axis) // bit) % 2


def hop(value, axis, bit):
    size = lax.axis_size(axis)
    return lax.ppermute(value, axis, [(i, i ^ bit) for i in range(size)])


def tie(*values):
    return lax.optimization_barrier(values)


def take_clips(values):
    tm = lax.axis_size("tm")
    me = lax.axis_index("tm")
    out = []
    for d in range(tm):
        block = lax.dynamic_index_in_dim(values, me ^ d, 1, keepdims=False)
        out.append(hop(block, "tm", d) if d else block)
    return out


def send_clips(blocks):
    return [hop(block, "tm", d) if d else block for d, block in enumerate(blocks)]


def all_clips(blocks, shape):
    return jnp.stack(unshuffle(blocks), 1).reshape(shape)


def unshuffle(blocks):
    me = lax.axis_index("tm")
    blocks = list(blocks)
    for b in range(bits_of(len(blocks))):
        odd = ((me >> b) & 1) == 1
        blocks = [jnp.where(odd, blocks[i ^ (1 << b)], blocks[i]) for i in range(len(blocks))]
    return blocks


def add_low(a, b):
    return (a.astype(F32) + b.astype(F32)).astype(BF16)


def split_share(value):
    count = bits_of(lax.axis_size("clips")) + bits_of(lax.axis_size("tm")) - 1
    return value.reshape((2,) * count + (value.shape[0] >> count, value.shape[1]))


def side_by_side(value, parts):
    return jnp.concatenate(jnp.split(value, parts, -2), -1)


class Sum:
    def __init__(self, folds):
        self.folds = folds
        clip_bits, self.time_bits = axis_bits("clips")[1:], axis_bits("tm")
        self.names = clip_bits[::-1] + self.time_bits[::-1]
        self.orders = (clip_bits, clip_bits[1:] + clip_bits[:1])
        self.rounds = len(clip_bits) + len(self.time_bits)

    def half(self, pair, names, name, other):
        at = names.index(name)
        mine = own_bit(*name)
        pick = lambda x: lax.dynamic_index_in_dim(x, 1 - mine if other else mine, at, keepdims=False)
        return add_low(*(pick(x) for x in pair))

    def half_of_all(self, index, state, other):
        sides = len(self.orders[0])
        if index < sides:
            names = [[n for n in self.names if n not in order[:index]] for order in self.orders]
            return [self.half(p, n, order[index], other) for p, n, order in zip(state, names, self.orders)]
        names = self.time_bits[index - sides :]
        parts = [self.half(pair, names[::-1], names[0], other) for pair in state]
        if len(parts) > 1:
            parts = [side_by_side(x, n) if n > 1 else x for x, n in zip(parts, self.folds)]
        return [jnp.concatenate(parts, -1) if len(parts) > 1 else parts[0]]

    def split(self, index, state):
        return [(away,) for away in self.half_of_all(index, state, True)] + state

    def send(self, index, state):
        sides = len(self.orders[0])
        names = [o[index] for o in self.orders] if index < sides else [self.time_bits[index - sides]]
        away, state = state[: len(names)], state[len(names) :]
        got = [hop(x, *name) for (x,), name in zip(away, names)]
        return list(zip(self.half_of_all(index, state, False), got))

    def scatter(self, index, state):
        return self.send(index, self.split(index, state))

    def share(self, state):
        return add_low(*state[0])

    def gather_orders(self, at_once=False):
        return [self.time_bits[:: 1 if at_once else -1] + order[::-1] for order in self.orders]


    def split_all(self, state):
        tm, me = lax.axis_size("tm"), lax.axis_index("tm")

        def pick(x, d):
            return lax.dynamic_index_in_dim(x.reshape((tm,) + x.shape[-2:]), me ^ d, 0, keepdims=False)

        def part(d):
            parts = [add_low(*(pick(x, d) for x in pair)) for pair in state]
            return jnp.concatenate([side_by_side(x, n) if n > 1 else x for x, n in zip(parts, self.folds)], -1)

        return [(part(d),) for d in range(tm)]

    def send_all(self, state):
        return [tuple(hop(x, "tm", d) if d else x for d, (x,) in enumerate(state))]

    def share_all(self, state):
        return sum(x.astype(F32) for x in state[0]).astype(BF16)

    def gather_all(self, state):
        return [tuple(hop(state[0][0], "tm", d) if d else state[0][0] for d in range(lax.axis_size("tm")))]

    def join_all(self, state, cut):
        whole = jnp.stack(state[0])
        return [whole[..., :cut], whole[..., cut:]]

    def gather(self, index, state, cut):
        if index < len(self.time_bits):
            return [(state[0], hop(state[0], *self.time_bits[::-1][index]))]
        names = [order[::-1][index - len(self.time_bits)] for order in self.orders]
        return [(value, hop(value, *name)) for value, name in zip(state, names)]

    def join(self, index, state, cut):
        out = [jnp.concatenate(pair, 0) for pair in state]
        if index == len(self.time_bits) - 1:
            return [out[0][..., :cut], out[0][..., cut:]]
        return out


def on_device(
    patches, mask_index, mask_count, w_qkv, q_bias, v_bias, w_out, out_bias, w_up, up_bias,
    w_down, down_bias, norm1_scale, norm1_shift, norm2_scale, norm2_shift, mask_embed, pos_embed,
    cotangent,
):
    clip_count, seg, width = patches.shape
    ff = w_up.shape[1]
    tm = lax.axis_size("tm")
    me = lax.axis_index("tm")
    length = seg * tm
    groups = clip_count // tm
    by_group = (groups, tm, seg, width)
    tile, chunk = 512, 512

    arrived, grouped = [], patches.reshape(by_group)
    for g in range(groups):
        arrived.append(take_clips(grouped[g : g + 1]))
        grouped, *arrived[g] = tie(grouped, *arrived[g])
    tied, *arrived[-1] = tie(cotangent, *arrived[-1])
    cot = take_clips(tied.reshape(by_group))
    arrived = [[b[0] for b in blocks] for blocks in arrived]

    row = lambda x: x.reshape(1, -1)
    joint_bias = row(jnp.concatenate([q_bias, jnp.zeros_like(q_bias), v_bias]))
    out_bias, up_bias, down_bias, gain1, shift1, gain2, shift2, embed = map(
        row, (out_bias, up_bias, down_bias, norm1_scale, norm1_shift, norm2_scale, norm2_shift, mask_embed)
    )
    starts = (me ^ jnp.arange(tm, dtype=jnp.int32)) * seg
    places = (starts[:, None] + jnp.arange(seg, dtype=jnp.int32)[None, :]).reshape(length)
    pos = jnp.concatenate([lax.dynamic_slice_in_dim(pos_embed, (me ^ d) * seg, seg, 0) for d in range(tm)], 0)
    slots = jnp.arange(mask_index.shape[1], dtype=jnp.int32)
    masks = []
    for g in range(groups):
        index_row = lax.dynamic_index_in_dim(mask_index, g * tm + me, 0, keepdims=False)
        count = lax.dynamic_index_in_dim(mask_count, g * tm + me, 0, keepdims=False)
        hit = (places[:, None] == index_row[None, :]) & (slots < count)[None, :]
        masks.append(jnp.any(hit, axis=1, keepdims=True).astype(F32))

    filled, normed_one, joints, attended, turned, logs = [], [], [], [], [], []
    for g in range(groups):
        f, n, j = project(arrived[g], masks[g], embed, pos, gain1, shift1, w_qkv, joint_bias)
        a, a_turned, log_sum = attend(j, width)
        if g < groups - 1:
            a, *arrived[g + 1] = tie(a, *arrived[g + 1])
        else:
            a, cot[1] = tie(a, cot[1])
        for kept, value in zip((filled, normed_one, joints, attended, turned, logs), (f, n, j, a, a_turned, log_sum)):
            kept.append(value)

    core = own_bit("clips", 1).astype(jnp.int32)
    kept_side = jnp.stack([core, me.astype(jnp.int32)])
    away_side = jnp.stack([1 - core, me.astype(jnp.int32)])
    shares = lax.axis_size("clips") // 2 * tm
    here = jnp.stack([(lax.axis_index("clips") // 2 * tm + me).astype(jnp.int32), core])
    hidden, normed_two, act, slope, *block_out = forward(
        filled, attended, w_out, out_bias, gain2, shift2, down_bias, w_up, up_bias, w_down, 1024, 256, tm
    )
    block_out[0], *cot = tie(block_out[0], *cot)
    cot = jnp.concatenate(cot, 1).reshape(groups * length, width)
    norm_acc, down, up, up_sums_away = back_first(away_side, normed_two, cot, act, slope, w_up, w_down, tile, chunk)
    down_got, up_got = hop(down, "clips", 1), hop(up, "clips", 1)
    down, up, up_sums, grad_hidden, mix, grad_out, sums_two = back_last(
        kept_side, turned, normed_two, cot, act, slope, w_up, w_down, w_out, gain2, hidden, norm_acc, ff // 2, chunk
    )
    one = Sum((2, 1))

    def after(values, *states):
        flat = [x for state in states for pair in state for x in pair]
        tied = list(tie(*values, *flat))
        values, flat = tied[: len(values)], tied[len(values) :]
        back = [[tuple(flat.pop(0) for _ in pair) for pair in state] for state in states]
        return (values, *back)

    state = [tuple(split_share(x) for x in pair) for pair in ((down, down_got), (up, up_got))]
    state = one.split(0, state)
    (mix, *block_out), state = after((mix, *block_out), state)
    state = one.send(0, state)
    block_out = send_clips(block_out)
    grads = attend_back(away_side, joints, mix, logs)
    qkv, bias_sums, acc = joint_first(away_side, normed_one, grads, w_qkv)
    qkv_got = hop(qkv, "clips", 1)
    sent_out = block_out
    (acc, sent_out[1], sent_out[2]), state = after((acc, sent_out[1], sent_out[2]), state)
    state = one.split(1, state)
    (mix, acc), state = after((mix, acc), state)
    state = one.send(1, state)
    grads = attend_back(kept_side, joints, mix, logs)
    (grads, *rest_out), state = after((grads, *sent_out[3:]), state)
    sent_out[3:] = rest_out
    third = (one.split_all, one.send_all)
    if len(one.orders[0]) > 2:
        third = (lambda s: one.split(2, s), lambda s: one.send(2, s))
    state = third[0](state)
    (grads,), state = after((grads,), state)
    state = third[1](state)
    qkv, rest_away, rest_kept, *input_grad = joint_last(
        kept_side, normed_one, grads, w_qkv, acc, grad_hidden, gain1, filled, masks, bias_sums, sums_two,
        up_sums_away, up_sums, grad_out.reshape(shares, width // shares, width), tm
    )
    (qkv, rest_away, rest_kept, *input_grad), state = after((qkv, rest_away, rest_kept, *input_grad), state)
    rest_away, rest_kept = rest_away.reshape(width, width), rest_kept.reshape(width, width)
    rest_got = hop(rest_away, "clips", 1)
    two = Sum((1, 1))
    pairs = [tuple(split_share(x) for x in pair) for pair in ((qkv, qkv_got), (rest_kept, rest_got))]
    cut_one, cut_two = ff // 2, -(-5 * width // 4 // LANES) * LANES
    share_rows = pairs[0][0].shape[-2]

    def scatter_steps(group, first):
        steps = [lambda s, i=i: group.split(i, s) for i in range(first, group.rounds)]
        return [(split, lambda s, i=i: group.send(i, s)) for i, split in zip(range(first, group.rounds), steps)]

    def gather_steps(group, cut):
        def prepare(i):
            if i == 0:
                return lambda s: [(group.share(s)[None],)]
            return lambda s: [(x,) for x in group.join(i - 1, s, cut)]

        return [
            (prepare(i), lambda s, i=i: group.gather(i, [x for (x,) in s], cut)) for i in range(group.rounds)
        ]

    def core_steps(group, cut):
        return [
            (
                lambda s: [(x,) for x in group.join(group.rounds - 1, s, cut)],
                lambda s: [(x, hop(x, "clips", 1)) for (x,) in s],
            )
        ]

    along = len(two.time_bits)
    steps_one = [None]
    if len(one.orders[0]) > 2:
        steps_one = scatter_steps(one, 3)[:-along] + [(one.split_all, one.send_all)]
    turn = len(steps_one) - 1
    back_one = gather_steps(one, cut_one)
    back_one[0] = (lambda s: [(one.share_all(s)[None],)], back_one[0][1])
    steps_one += back_one[1:] + [None] + core_steps(one, cut_one)
    steps_two = scatter_steps(two, 0)[:-along]
    steps_two.append((two.split_all, two.send_all))
    steps_two.append((lambda s: [(two.share_all(s),)], two.gather_all))
    back_two = gather_steps(two, cut_two)[along:]
    steps_two.append((lambda s: [(x,) for x in two.join_all(s, cut_two)], back_two[0][1]))
    steps_two += back_two[1:] + core_steps(two, cut_two)
    outputs = []
    for index in range(max(len(steps_one), len(steps_two))):
        if index == 2:
            block_out = all_clips(sent_out, patches.shape)
            (block_out,), state, pairs = after((block_out,), state, pairs)
        if index == len(steps_two) - 2:
            sent[1:3], state, pairs = after(sent[1:3], state, pairs)
        if index == len(steps_two) - 1:
            tied, pairs = after((*sent[3:], *outputs), pairs)
            sent[3:], outputs = tied[: len(sent) - 3], tied[len(sent) - 3 :]
        active = [steps[index] if index < len(steps) else None for steps in (steps_one, steps_two)]
        states = [step[0](x) if step else x for step, x in zip(active, (state, pairs))]
        live = [x for x, step in zip(states, active) if step]
        if index == 3:
            input_grad, *live = after(input_grad, *live)
            sent = send_clips(input_grad)
        elif index:
            _, *live = after((), *live)
        live = iter(live)
        state, pairs = (step[1](next(live)) if step else x for step, x in zip(active, states))
        if index == turn:
            state = back_one[0][1](back_one[0][0](state))
        if index == len(steps_one) - 1:
            one_all = [own for own, _ in state] + [other for _, other in state]
            if share_rows % 8 == 0:
                outputs = place(
                    place_one_kernel, here, one_all, one.gather_orders(), tm, ((2, ff // 2, width), (width, ff))
                )
    two_all = [own for own, _ in pairs] + [other for _, other in pairs]
    input_grad = all_clips(sent, patches.shape)

    orders_one, orders_two = one.gather_orders(), two.gather_orders(True)
    if share_rows % 8 == 0:
        down_sum, up_sum = outputs
        shapes = ((width, 3 * width), (width, width), (length, width), (width - length, width))
        qkv_sum, out_sum, pos_sum, small = place(place_two_kernel, here, two_all, orders_two, tm, shapes)
        down_sum = down_sum.reshape(ff, width)
    else:
        downs, ups = in_order(here, one_all, orders_one, tm)
        both = jnp.concatenate(in_order(here, two_all, orders_two, tm), -1)
        qkvs, rests = both[..., : 3 * width // 2], both[..., 3 * width // 2 :]
        down_sum = jnp.stack(jnp.split(downs, 2, -1), 2).reshape(ff, width)
        up_sum = jnp.concatenate(list(ups.reshape(2, width, ff // 2)), 1)
        qkv_sum = jnp.stack(list(qkvs.reshape(2, width, 3, width // 2)), 2).reshape(width, 3 * width)
        out_sum, rest = rests[0].reshape(width, width), rests[1]
        pos_sum = rest[:, : length // shares].reshape(length, width)
        small = rest[:, length // shares :].reshape(width - length, width)
    v = []
    at = 0
    for n in (1, 1, 1, ff // width, 1, 1, 1, 1, 1, 1):
        v.append(small[at : at + n].reshape(-1))
        at += n
    return (block_out, input_grad, qkv_sum, v[0], v[1], out_sum, v[2], up_sum, v[3], down_sum, v[4],
            v[5], v[6], v[7], v[8], v[9], pos_sum)


def solution(mesh):
    rows = P("clips", "tm", None)
    in_specs = (rows, P("clips", None), P("clips")) + (P(),) * 15 + (rows,)
    out_specs = (rows, rows) + (P(),) * 15
    return jax.shard_map(on_device, mesh=mesh, in_specs=in_specs, out_specs=out_specs, check_vma=False)
```
